32 devices in a mesh: band: 8 (over z, y), tm: 4 (over x, core).
Axes of the slice: x: 2, y: 2, z: 4, core: 2. Of those that a mesh axis runs over, the one named last changes fastest.
Arguments:
- fields: bfloat16 [512, 704, 1440], P('tm', 'band'), may hold values from -6 to 6
- wave_table: int32 [384], replicated, may hold values from 0 to 383, as said below
- day_of_year: int32 [512], P('tm'), may hold values from 0 to 364, as said below
- ar_coef: float32 [384, 384], P('band'), may hold values from -0.9 to 0.9
- log_var: float32 [384, 384], P('band'), may hold values from 0 to 2.5
Outputs:
- innovation: bfloat16 [512, 2, 384, 384], P('tm', None, 'band')
- grad_coef: float32 [384, 384], P('band', 'tm')
- grad_var: float32 [384, 384], P('band', 'tm')
The draws below stay inside these ranges and needn't reach their ends.
Inputs may be any that keep to these rules, and one draw needn't show every extreme that they name: `wave_table`: every wavenumber below 384 appears once; slots 2 k and 2 k + 1 hold some m and 383 - m. `day_of_year`: consecutive days follow one another in the year, 364 being followed by 0; both 364 and 0 occur.
All inputs are finite; a program needn't handle non-finite values.
Results may differ from the reference program's by a relative error of at most 0.008.
Values may be sent and summed in bfloat16 or wider, within the bound.
No kernel may reach another device: no remote copies, remote signals or barrier semaphores. Data moves between devices by JAX's collectives and lax.ppermute only.
A program may use at most 256 MiB of HBM per device.

```python
import math
import jax
import jax.numpy as jnp
from jax import lax

NLON = 1440
NLAT = 704
L = 384
MW = 384
DAYS = 512


def draw_wave_table(key, part):
    key = jax.random.fold_in(key, 11)
    lower_half = jax.random.permutation(key, MW // 2).astype(jnp.int32)
    paired = jnp.stack([lower_half, MW - 1 - lower_half], axis=1)
    return paired.reshape(MW).astype(jnp.int32)


def draw_day_of_year(key, part):
    key = jax.random.fold_in(key, 23)
    offset_hi = max(min(DAYS, 365) - 1, 1)
    offset = jax.random.randint(key, (), 0, offset_hi, dtype=jnp.int32)
    first_day = (364 - offset) % 365
    return ((first_day + jnp.arange(DAYS, dtype=jnp.int32)) % 365).astype(jnp.int32)


def shard_levels(own_key, shape, split, smallest, high):
    def one(position, shards_of):
        draws = jax.random.uniform(jax.random.fold_in(jax.random.fold_in(own_key, 6), position), (shards_of,), jnp.float32, smallest / len(split), high / len(split))
        return jnp.repeat(jnp.exp(draws), shape[position] // shards_of).reshape((-1,) + (1,) * (len(shape) - position - 1))

    loudness = one(*split[0])
    for cut in split[1:]:
        loudness = loudness * one(*cut)
    return loudness


def bell_draw(own_key, dims, scale, limit, cuts=(), kind=jnp.bfloat16):
    values = scale * jax.random.normal(own_key, dims, jnp.float32)
    if cuts:
        values = values * shard_levels(own_key, dims, cuts, -0.22, 0.18)
    return jnp.clip(values, -limit, limit).astype(kind)


def setup_inputs(seed: int = 0) -> dict:
    splits = jax.random.split(jax.random.key(seed), 6)
    fields = bell_draw(splits[0], (DAYS, NLAT, NLON), 1.0, 6.0, ((0, 4), (1, 8)))
    wave_table = draw_wave_table(jax.random.fold_in(splits[5], 71), 0)
    day_of_year = draw_day_of_year(jax.random.fold_in(splits[5], 71), 0)
    ar_coef = jnp.clip(jax.random.uniform(splits[3], (MW, L), jnp.float32, -0.9, 0.9) * shard_levels(splits[3], (MW, L), ((0, 8),), -0.4, 0.0), -0.9, 0.9)
    log_var = jnp.clip(2.5 * jax.random.uniform(splits[4], (MW, L), jnp.float32) ** shard_levels(splits[4], (MW, L), ((0, 8),), -0.2, 0.2), 0.0, 2.5)
    return dict(fields=fields, wave_table=wave_table, day_of_year=day_of_year, ar_coef=ar_coef, log_var=log_var)


def fourier_table(wave_list, lon_count):
    lon_index = jnp.arange(lon_count, dtype=jnp.int32)
    phase_index = lon_index[:, None] * wave_list[None, :].astype(jnp.int32) % lon_count
    angle_rad = phase_index.astype(jnp.float32) * (2.0 * math.pi / lon_count)
    return jnp.concatenate([jnp.cos(angle_rad), -jnp.sin(angle_rad)], axis=1).astype(jnp.bfloat16)

def legendre_setup(wave_list, lat_count):
    colatitude = (jnp.arange(lat_count, dtype=jnp.float32) + 0.5) * (math.pi / lat_count)
    cosines = jnp.cos(colatitude)
    sine_vals = jnp.sin(colatitude)
    wave_order = wave_list.astype(jnp.float32)[:, None]
    log_start = 0.5 * (jnp.log(wave_order + 0.5) + jax.scipy.special.gammaln(wave_order + 0.5) - jax.scipy.special.gammaln(wave_order + 1.0) - 0.5 * math.log(math.pi))
    log_start = log_start + wave_order * jnp.log(sine_vals)[None, :]
    weights = sine_vals * (math.pi / lat_count)
    return (wave_order, cosines, log_start, weights)

def legendre_step(degree_index, carry_state, wave_order, cosines, log_start):
    lagged, current, log_scale = carry_state
    degree_f = jnp.asarray(degree_index).astype(jnp.float32)
    above = degree_f - wave_order
    denominator = jnp.maximum(above * (degree_f + wave_order), 1.0)
    first_coef = jnp.sqrt(jnp.maximum((4.0 * degree_f * degree_f - 1.0) / denominator, 0.0))
    second_coef = jnp.sqrt(jnp.maximum(((degree_f - 1.0) ** 2 - wave_order * wave_order) * (2.0 * degree_f + 1.0) / ((2.0 * degree_f - 3.0) * denominator), 0.0))
    advanced = first_coef * cosines[None, :] * current - second_coef * lagged
    moving = above > 0.5
    at_start = jnp.abs(above) < 0.5
    new_lagged = jnp.where(moving, current, 0.0)
    new_current = jnp.where(moving, advanced, jnp.where(at_start, 1.0, 0.0))
    new_scale = jnp.where(at_start, log_start, log_scale)
    largest = jnp.maximum(jnp.abs(new_current), 1.0)
    new_lagged = new_lagged / largest
    new_current = new_current / largest
    new_scale = new_scale + jnp.log(largest)
    value = jnp.where(above > -0.5, new_current * jnp.exp(new_scale), 0.0)
    return ((new_lagged, new_current, new_scale), value)

def legendre_rows(wave_list, lat_count, degree_count):
    wave_order, cosines, log_start, weights = legendre_setup(wave_list, lat_count)
    zero_state = jnp.zeros((wave_list.shape[0], lat_count), jnp.float32)

    def advance(carry_state, degree_index):
        carry_state, value = legendre_step(degree_index, carry_state, wave_order, cosines, log_start)
        return (carry_state, (value * weights[None, :]).astype(jnp.bfloat16))
    final_state, legendre = lax.scan(advance, (zero_state, zero_state, zero_state), jnp.arange(degree_count, dtype=jnp.int32))
    return legendre

def reference(fields, wave_table, day_of_year, ar_coef, log_var):
    dft_table = fourier_table(wave_table, NLON)
    coeffs = jnp.dot(fields.reshape(DAYS * NLAT, NLON), dft_table, preferred_element_type=jnp.float32)
    coeffs = coeffs.astype(jnp.bfloat16).reshape(DAYS, NLAT, 2, MW)
    legendre = legendre_rows(wave_table, NLAT, L)
    spectral = jnp.einsum('djcs,lsj->dcsl', coeffs.astype(jnp.float32), legendre.astype(jnp.float32))
    previous = jnp.concatenate([jnp.zeros_like(spectral[:1]), spectral[:-1]], axis=0)
    degree_list = jnp.arange(L, dtype=jnp.int32)
    valid_mask = (degree_list[None, :] >= wave_table[:, None]).astype(jnp.float32)
    season = 1.0 + 0.5 * jnp.cos(day_of_year.astype(jnp.float32) * (2.0 * math.pi / 365.0))
    inverse_var = jnp.exp(-log_var)[None, :, :] / season[:, None, None]
    residual = spectral - ar_coef[None, None, :, :] * previous
    innovation = (residual * jnp.sqrt(inverse_var)[:, None] * valid_mask).astype(jnp.bfloat16)
    grad_coef = -valid_mask * lax.optimization_barrier(jnp.sum(residual * previous * inverse_var[:, None], axis=(0, 1))) / (2.0 * DAYS)
    grad_var = valid_mask * lax.optimization_barrier(jnp.sum(0.5 * (1.0 - residual * residual * inverse_var[:, None]), axis=(0, 1))) / (2.0 * DAYS)
    return (innovation, grad_coef, grad_var)
```

```python
import functools
import math

import jax
import jax.numpy as jnp
import numpy as np
from jax import lax
from jax.experimental import pallas as pl
from jax.experimental.pallas import tpu as pltpu
from jax.sharding import PartitionSpec as P

LANES = 128
TILE = 16
VMEM_LIMIT = 56 * 1024 * 1024


def round_up(value, unit):
    return -(-value // unit) * unit


def fourier_columns(waves, lon_count):
    fine_count = 32
    coarse_count = lon_count // fine_count
    scale = 2.0 * math.pi / lon_count

    def parts(lons):
        angle = (lons[:, None] * waves[None, :] % lon_count).astype(jnp.float32) * scale
        return jnp.cos(angle), jnp.sin(angle)

    coarse_cos, coarse_sin = parts(jnp.arange(coarse_count, dtype=jnp.int32) * fine_count)
    fine_cos, fine_sin = parts(jnp.arange(fine_count, dtype=jnp.int32))
    coarse_cos, coarse_sin = coarse_cos[:, None], coarse_sin[:, None]
    fine_cos, fine_sin = fine_cos[None], fine_sin[None]
    cosine = coarse_cos * fine_cos - coarse_sin * fine_sin
    minus_sine = -(coarse_sin * fine_cos + coarse_cos * fine_sin)
    shape = (lon_count, waves.shape[0])
    return cosine.reshape(shape), minus_sine.reshape(shape)


def table_kernel(steps, lane_tiles, top, low_ref, first_ref, second_ref, cos_ref, weight_ref, out_ref, rows_ref, scale_ref):
    tiles = range(lane_tiles)
    low = low_ref[...]
    high = top - low
    low_next = low + 1.0
    lat_count = out_ref.shape[2]

    def lanes(ref, tile):
        return ref[:, tile * LANES : (tile + 1) * LANES]

    cosines = [lanes(cos_ref, t) for t in tiles]
    weights = [lanes(weight_ref, t) for t in tiles]
    second = [lanes(second_ref, t) for t in tiles]
    for t in tiles:
        half = jnp.exp(0.5 * second[t])
        scale_ref[2, :, t * LANES : (t + 1) * LANES] = half * weights[t]
        scale_ref[3, :, t * LANES : (t + 1) * LANES] = half

    def block(index, carry):
        current, lagged, scale, last_inverse = carry
        for t in tiles:
            largest = jnp.maximum(jnp.maximum(jnp.abs(current[t]), jnp.abs(lagged[t])), 1.0)
            current[t] = current[t] / largest
            lagged[t] = lagged[t] / largest
            scale[t] = scale[t] + jnp.log(largest)
            half = jnp.exp(0.5 * scale[t])
            scale_ref[0, :, t * LANES : (t + 1) * LANES] = half * weights[t]
            scale_ref[1, :, t * LANES : (t + 1) * LANES] = half
        begin = (index * TILE).astype(jnp.float32)
        for step in range(TILE):
            row = begin + float(step)
            after = low < row
            above = row - jnp.where(after, low_next, 0.0)
            order = jnp.where(after, low, high)
            degree = above + order
            spread = above * (degree + order)
            square = 4.0 * degree * degree - 1.0
            root = lax.rsqrt(jnp.maximum(square * spread, 1.0))
            factor = square * root
            inverse = spread * root
            fresh = above == 0.0
            for t in tiles:
                advanced = factor * (cosines[t] * current[t] - last_inverse * lagged[t])
                lagged[t] = current[t]
                current[t] = jnp.where(fresh, 1.0, advanced)
                rows_ref[t, pl.ds(step, TILE, stride=TILE), :] = current[t]
            last_inverse = inverse
        renewed = (low_next >= begin) & (low_next < begin + float(TILE))
        for t in tiles:
            scale[t] = jnp.where(renewed, second[t], scale[t])
        row_index = lax.broadcasted_iota(jnp.int32, (TILE, LANES), 0).astype(jnp.float32) + begin
        for pair in range(TILE):
            mark = low[pair : pair + 1, :]
            before = (row_index <= mark) | (mark + 1.0 < begin)
            for t in tiles:
                span = slice(t * LANES, min((t + 1) * LANES, lat_count))
                width = span.stop - span.start
                here = slice(t * LANES, (t + 1) * LANES)
                values = rows_ref[t, pair * TILE : (pair + 1) * TILE, :]
                one = jnp.where(before, scale_ref[0, pair : pair + 1, here], scale_ref[2, pair : pair + 1, here])
                two = jnp.where(before, scale_ref[1, pair : pair + 1, here], scale_ref[3, pair : pair + 1, here])
                values = (values * one * two).astype(jnp.bfloat16)
                out_ref[pair, pl.ds(pl.multiple_of(index * TILE, TILE), TILE), span] = values[:, :width]
        return current, lagged, scale, last_inverse

    zeros = jnp.zeros((TILE, LANES), jnp.float32)
    start = (
        [zeros for _ in tiles],
        [zeros for _ in tiles],
        [lanes(first_ref, t) for t in tiles],
        zeros,
    )
    lax.fori_loop(0, steps // TILE, block, start)


def packed_table(low_waves, lat_begin, lat_half, lat_count, degree_count, steps):
    pair_count = low_waves.shape[0]
    lane_tiles = -(-lat_half // LANES)
    width = lane_tiles * LANES
    top = float(degree_count - 1)
    index = jnp.minimum(jnp.arange(width, dtype=jnp.int32), lat_half - 1) + lat_begin
    colatitude = (index.astype(jnp.float32) + 0.5) * (math.pi / lat_count)
    sines = jnp.sin(colatitude)
    log_sines = jnp.log(sines)
    low = low_waves.astype(jnp.float32)

    def log_start(order):
        base = 0.5 * (
            jnp.log(order + 0.5)
            + jax.scipy.special.gammaln(order + 0.5)
            - jax.scipy.special.gammaln(order + 1.0)
            - 0.5 * math.log(math.pi)
        )
        return base[:, None] + order[:, None] * log_sines[None, :]

    spread = lambda row: jnp.broadcast_to(row[None, :], (TILE, width))
    block = lambda *shape: pl.BlockSpec(shape, lambda i: (i,) + (0,) * (len(shape) - 1))
    whole = pl.BlockSpec((TILE, width), lambda i: (0, 0))
    return pl.pallas_call(
        functools.partial(table_kernel, steps, lane_tiles, top),
        grid=(pair_count // TILE,),
        in_specs=[block(TILE, LANES), block(TILE, width), block(TILE, width), whole, whole],
        out_specs=block(TILE, steps, lat_half),
        out_shape=jax.ShapeDtypeStruct((pair_count, steps, lat_half), jnp.bfloat16),
        scratch_shapes=[
            pltpu.VMEM((lane_tiles, TILE * TILE, LANES), jnp.float32),
            pltpu.VMEM((4, TILE, width), jnp.float32),
        ],
        compiler_params=pltpu.CompilerParams(vmem_limit_bytes=VMEM_LIMIT),
        cost_estimate=pl.CostEstimate(
            flops=pair_count * steps * width * 12, bytes_accessed=pair_count * steps * width * 2, transcendentals=0
        ),
    )(
        jnp.broadcast_to(low[:, None], (pair_count, LANES)),
        log_start(top - low),
        log_start(low),
        spread(jnp.cos(colatitude)),
        spread(sines * (math.pi / lat_count)),
    )


def gather_slots(in_ref, flat_ref, slot_ref):
    sources, lats, rows, days = in_ref.shape
    lat_half = sources * lats
    for part in range(2):
        for source in range(sources):
            values = in_ref[source, :, part * TILE : (part + 1) * TILE, :].astype(jnp.float32)
            flat_ref[pl.ds(source * lats * TILE, lats * TILE), :] = values.reshape(lats * TILE, days)
        for slot in range(TILE):
            column = flat_ref[pl.ds(slot, lat_half, stride=TILE), :]
            slot_ref[slot, :, part * days : (part + 1) * days] = column.astype(jnp.bfloat16)


def pair_sum(pair, low, table_ref, slot_ref):
    table = table_ref[pair]
    high_sum = jnp.dot(table, slot_ref[2 * pair], preferred_element_type=jnp.float32)
    low_sum = jnp.dot(table, slot_ref[2 * pair + 1], preferred_element_type=jnp.float32)
    row = lax.broadcasted_iota(jnp.int32, high_sum.shape, 0)
    return jnp.where(row <= low, high_sum, low_sum)


def partial_kernel(low_ref, in_ref, table_ref, out_ref, flat_ref, slot_ref):
    gather_slots(in_ref, flat_ref, slot_ref)

    def one(pair, carry):
        out_ref[pair] = pair_sum(pair, low_ref[pair], table_ref, slot_ref).astype(jnp.bfloat16)
        return carry

    lax.fori_loop(0, TILE // 2, one, 0)


def finish_kernel(
    low_ref, wave_ref, shift_ref, in_ref, table_ref, other_ref, ar_ref, half_ref, season_ref, *rest
):
    out_ref, misc_ref, flat_ref, slot_ref, turned_ref = rest[-5:]
    steps = table_ref.shape[1]
    days = out_ref.shape[0]
    degrees = out_ref.shape[3]
    lane_tiles = degrees // LANES
    gather_slots(in_ref, flat_ref, slot_ref)
    lane = lax.broadcasted_iota(jnp.int32, (steps, LANES), 1)
    turn = (
        lax.broadcasted_iota(jnp.int32, (days, days), 0) == lax.broadcasted_iota(jnp.int32, (days, days), 1)
    ).astype(jnp.bfloat16)
    pick_row = lax.broadcasted_iota(jnp.int32, (8, LANES), 0)
    pick_lane = lax.broadcasted_iota(jnp.int32, (8, LANES), 1)
    wanted = jnp.where(pick_row == 0, 0, jnp.where(pick_row == 1, 2, jnp.where(pick_row == 2, LANES - 1, pick_row - 0)))
    wanted = jnp.where(pick_row == 3, 1, jnp.where(pick_row == 4, 3, jnp.where(pick_row == 5, 4, wanted)))
    pick = ((pick_lane == wanted) & (pick_row < 6)).astype(jnp.bfloat16)
    transposed = (((1,), (1,)), ((), ()))

    def one(pair, carry):
        own = pair_sum(pair, low_ref[pair], table_ref, slot_ref)
        total = own + other_ref[pair].astype(jnp.float32)
        ar = ar_ref[pair]
        half = half_ref[pair]
        turned = []
        parts = []
        sum_coef = jnp.zeros((steps, LANES), jnp.float32)
        sum_var = jnp.zeros((steps, LANES), jnp.float32)
        for part in range(2):
            spectral = total[:, part * days : (part + 1) * days]
            parts.append(spectral)
            previous = jnp.where(lane == 0, 0.0, pltpu.roll(spectral, 1, 1))
            residual = spectral - ar * previous
            scaled = residual * season_ref[0:1, :]
            innovation = (scaled * half).astype(jnp.bfloat16)
            turned.append(
                lax.dot_general(turn, innovation, transposed, preferred_element_type=jnp.float32)
            )
            weighted = residual * season_ref[1:2, :]
            sum_coef = sum_coef + weighted * previous
            sum_var = sum_var + weighted * residual
        sum_coef = jnp.sum(sum_coef, axis=1, keepdims=True)
        sum_var = jnp.sum(sum_var, axis=1, keepdims=True)
        misc = jnp.where(
            (lane == 0) | (lane == LANES - 1),
            parts[0],
            jnp.where(lane < 3, pltpu.roll(parts[1], 2, 1), jnp.where(lane == 3, sum_coef, sum_var)),
        )
        misc_high = misc.astype(jnp.bfloat16)
        misc_low = (misc - misc_high.astype(jnp.float32)).astype(jnp.bfloat16)
        for piece in (misc_high, misc_low):
            turned.append(lax.dot_general(pick, piece, transposed, preferred_element_type=jnp.float32))
        stacked = jnp.concatenate(turned, axis=0).astype(jnp.bfloat16)
        row = lax.broadcasted_iota(jnp.int32, (steps, degrees), 0)
        degree = lax.broadcasted_iota(jnp.int32, (steps, degrees), 1)
        for position in range(2):
            slot = 2 * pair + position
            chosen = (row - degree == shift_ref[slot]) & (degree >= wave_ref[slot])
            placed = jnp.dot(stacked, chosen.astype(jnp.bfloat16), preferred_element_type=jnp.float32)
            for part in range(2):
                for t in range(lane_tiles):
                    turned_ref[part, t, pl.ds(slot, days, stride=TILE), :] = placed[
                        part * days : (part + 1) * days, t * LANES : (t + 1) * LANES
                    ]
            misc_ref[slot] = placed[2 * days : 2 * days + 8] + placed[2 * days + 8 : 2 * days + 16]
        return carry

    lax.fori_loop(0, TILE // 2, one, 0)

    def write(day, carry):
        for part in range(2):
            for t in range(lane_tiles):
                values = turned_ref[part, t, pl.ds(pl.multiple_of(day * TILE, TILE), TILE), :]
                out_ref[day, part, :, t * LANES : (t + 1) * LANES] = values.astype(jnp.bfloat16)
        return carry

    lax.fori_loop(0, days, write, 0)


def leading(shape, chunk):
    return pl.BlockSpec(shape, lambda i: (chunk,) + (0,) * (len(shape) - 1))


def partial_sums(chunk, low, block, table):
    sources, lats, rows, days = block.shape
    steps = table.shape[1]
    lat_half = sources * lats
    pairs = TILE // 2
    return pl.pallas_call(
        partial_kernel,
        grid=(1,),
        in_specs=[
            pl.BlockSpec(memory_space=pltpu.SMEM),
            leading(block.shape, 0),
            leading((pairs, steps, lat_half), chunk),
        ],
        out_specs=leading((pairs, steps, 2 * days), 0),
        out_shape=jax.ShapeDtypeStruct((pairs, steps, 2 * days), jnp.bfloat16),
        scratch_shapes=[
            pltpu.VMEM((lat_half * TILE, days), jnp.float32),
            pltpu.VMEM((TILE, lat_half, 2 * days), jnp.bfloat16),
        ],
        compiler_params=pltpu.CompilerParams(vmem_limit_bytes=VMEM_LIMIT),
        cost_estimate=pl.CostEstimate(
            flops=2 * TILE * steps * lat_half * 2 * days, bytes_accessed=8 * 1024 * 1024, transcendentals=0
        ),
    )(low, block, table)


def finish(chunk, first, low, waves, shifts, block, table, other, ar, half, season, held, slot_total):
    sources, lats, rows, days = block.shape
    steps = table.shape[1]
    lat_half = sources * lats
    pairs = TILE // 2
    smem = pl.BlockSpec(memory_space=pltpu.SMEM)
    operands = [low, waves, shifts, block, table, other, ar[chunk], half[chunk], season]
    in_specs = [
        smem,
        smem,
        smem,
        leading(block.shape, 0),
        leading((pairs, steps, lat_half), first + chunk),
        leading((pairs, steps, 2 * days), 0),
        leading((pairs, steps, LANES), 0),
        leading((pairs, steps, LANES), 0),
        leading((8, LANES), 0),
    ]
    aliases = {}
    if held is not None:
        operands.append(held)
        in_specs.append(pl.BlockSpec(memory_space=pl.ANY))
        aliases = {len(operands) - 1: 0}
    degree_count = slot_total[1]
    return pl.pallas_call(
        finish_kernel,
        grid=(1,),
        in_specs=in_specs,
        out_specs=[
            pl.BlockSpec((days, 2, TILE, degree_count), lambda i: (0, 0, chunk, 0)),
            leading((TILE, 8, degree_count), 0),
        ],
        out_shape=[
            jax.ShapeDtypeStruct((days, 2, slot_total[0], degree_count), jnp.bfloat16),
            jax.ShapeDtypeStruct((TILE, 8, degree_count), jnp.float32),
        ],
        input_output_aliases=aliases,
        scratch_shapes=[
            pltpu.VMEM((lat_half * TILE, days), jnp.float32),
            pltpu.VMEM((TILE, lat_half, 2 * days), jnp.bfloat16),
            pltpu.VMEM((2, degree_count // LANES, days * TILE, LANES), jnp.float32),
        ],
        compiler_params=pltpu.CompilerParams(vmem_limit_bytes=VMEM_LIMIT),
        cost_estimate=pl.CostEstimate(
            flops=4 * TILE * steps * lat_half * 2 * days, bytes_accessed=12 * 1024 * 1024, transcendentals=0
        ),
    )(*operands)


def pack_rows(values, low, steps):
    degrees = values.shape[2]
    row = jnp.arange(steps, dtype=jnp.int32)[None, :]
    first = row <= low[:, None]
    source = jnp.where(first, row + (degrees - 1) - low[:, None], degrees + row - 1)
    source = jnp.clip(source, 0, 2 * degrees - 1)
    return jnp.take_along_axis(values.reshape(values.shape[0], 2 * degrees), source, axis=1)


def per_device(fields, wave_table, day_of_year, ar_coef, log_var):
    band_count = lax.axis_size("band")
    time_count = lax.axis_size("tm")
    band = lax.axis_index("band")
    slot_count, degree_count = ar_coef.shape
    day_count, lat_local, lon_count = fields.shape
    lat_count = lat_local * band_count
    group = band_count // 2
    lat_half = lat_local * group
    steps = round_up(degree_count + 1, TILE)
    total_days = day_count * time_count
    slot_pad = round_up(slot_count, TILE)
    chunks = slot_pad // TILE
    pairs = slot_pad // 2
    half_index = band // group
    rank = band % group
    half_groups = [list(range(group)), list(range(group, band_count))]
    mirror = [(i, (i + group) % band_count) for i in range(band_count)]

    waves = wave_table.reshape(2, group, slot_count // 2, 2)
    high_low = jnp.stack([waves.max(-1), waves.min(-1)], axis=-1)
    high_low = jnp.pad(high_low, ((0, 0), (0, 0), (0, pairs - slot_count // 2), (0, 0)))
    present = jnp.arange(slot_pad) < slot_count
    ordered = high_low.reshape(2, group, chunks, TILE)
    own_order = lax.dynamic_index_in_dim(ordered, half_index, 0, keepdims=False)
    far_order = lax.dynamic_index_in_dim(ordered, 1 - half_index, 0, keepdims=False)

    def low_waves(order):
        return lax.dynamic_index_in_dim(order, rank, 0, keepdims=False).reshape(pairs, 2)[:, 1]

    own_low, far_low = low_waves(own_order), low_waves(far_order)
    lows = jnp.concatenate([far_low, own_low])
    lows = jnp.pad(lows, (0, round_up(2 * pairs, TILE) - 2 * pairs))

    def transform(order, first, count):
        picked = order[:, first : first + count].reshape(-1)
        cosine, minus_sine = fourier_columns(picked, lon_count)
        shape = (lon_count, group, count, 1, TILE)
        table = jnp.concatenate([cosine.reshape(shape), minus_sine.reshape(shape)], axis=3)
        if slot_pad != slot_count:
            mask = present.reshape(chunks, TILE)[first : first + count]
            table = table * mask[None, None, :, None, :]
        table = table.astype(jnp.bfloat16).reshape(lon_count, group * count * 2 * TILE)
        coeffs = jnp.einsum("djk,kq->jqd", fields, table, preferred_element_type=jnp.float32)
        coeffs = coeffs.astype(jnp.bfloat16).reshape(lat_local, group, count, 2 * TILE, day_count)
        return [coeffs[:, :, i].transpose(1, 0, 2, 3) for i in range(count)]

    def exchange(block):
        return lax.all_to_all(block, "band", 0, 0, axis_index_groups=half_groups, tiled=True)

    far_blocks = transform(far_order, 0, 1)
    if chunks > 1:
        far_blocks = far_blocks + transform(far_order, 1, chunks - 1)
    own_blocks = transform(own_order, 0, chunks)
    table = packed_table(lows, half_index * lat_half, lat_half, lat_count, degree_count, steps)

    others = []
    for chunk in range(chunks):
        block = exchange(far_blocks[chunk])
        low = far_low[chunk * TILE // 2 : (chunk + 1) * TILE // 2]
        sums = partial_sums(chunk, low, block, table)
        others.append(lax.ppermute(sums, "band", mirror))

    own_waves = lax.dynamic_slice_in_dim(wave_table, band * slot_count, slot_count)
    pad_slots = ((0, slot_pad - slot_count),)
    slot_waves = jnp.pad(own_waves, pad_slots)
    is_low = (slot_waves.reshape(pairs, 2) == own_low[:, None])
    first_low = is_low[:, 0]
    shifts = jnp.where(is_low, 1, -slot_waves.reshape(pairs, 2)).reshape(slot_pad)

    def by_pair(values):
        values = jnp.pad(values, pad_slots + ((0, 0),)).reshape(pairs, 2, degree_count)
        return jnp.where(first_low[:, None, None], values[:, ::-1], values)

    def spread_rows(values):
        packed = pack_rows(by_pair(values), own_low, steps)
        packed = jnp.broadcast_to(packed[:, :, None], (pairs, steps, LANES))
        return packed.reshape(chunks, TILE // 2, steps, LANES)

    ar_rows = spread_rows(ar_coef)
    half_rows = spread_rows(jnp.exp(-0.5 * log_var))
    season = 1.0 + 0.5 * jnp.cos(day_of_year.astype(jnp.float32) * (2.0 * math.pi / 365.0))
    later = (jnp.arange(day_count) > 0).astype(jnp.float32)
    season_rows = jnp.stack([lax.rsqrt(season), later / season])
    season_rows = jnp.pad(season_rows, ((0, 6), (0, 0)))

    innovation = None
    misc = []
    for chunk in range(chunks):
        block = exchange(own_blocks[chunk])
        low = own_low[chunk * TILE // 2 : (chunk + 1) * TILE // 2]
        span = slice(chunk * TILE, (chunk + 1) * TILE)
        innovation, rows = finish(
            chunk, chunks, low, slot_waves[span], shifts[span], block, table, others[chunk],
            ar_rows, half_rows, season_rows, innovation, (slot_pad, degree_count),
        )
        misc.append(rows)
    innovation = innovation[:, :, :slot_count]
    misc = jnp.concatenate(misc, axis=0)[:slot_count].transpose(1, 0, 2)
    first_day, last_day = misc[0:2], misc[2:4]
    route = [(i, i + 1) for i in range(time_count - 1)]
    carried = lax.ppermute(last_day.astype(jnp.bfloat16), "tm", route).astype(jnp.float32)

    degree_list = jnp.arange(degree_count, dtype=jnp.int32)
    valid_mask = (degree_list[None, :] >= own_waves[:, None]).astype(jnp.float32)
    variance = jnp.exp(-log_var)
    residual = first_day - ar_coef[None] * carried
    inverse = variance / season[0]
    opening = (residual * jnp.sqrt(inverse)[None] * valid_mask[None]).astype(jnp.bfloat16)
    innovation = lax.dynamic_update_slice_in_dim(innovation, opening[None], 0, 0)
    sum_coef = misc[4] * variance + jnp.sum(residual * carried, axis=0) * inverse
    sum_var = day_count - 0.5 * (misc[5] * variance + jnp.sum(residual * residual, axis=0) * inverse)
    sums = jnp.stack([sum_coef, sum_var]).astype(jnp.bfloat16)
    column_width = degree_count // time_count
    sums = sums.reshape(2, slot_count, time_count, column_width).transpose(2, 0, 1, 3)
    sums = lax.all_to_all(sums, "tm", 0, 0, tiled=True)
    sums = jnp.sum(sums.astype(jnp.float32), axis=0)
    local_mask = lax.dynamic_slice_in_dim(valid_mask, lax.axis_index("tm") * column_width, column_width, 1)
    grad_coef = -local_mask * sums[0] / (2.0 * total_days)
    grad_var = local_mask * sums[1] / (2.0 * total_days)
    return innovation, grad_coef, grad_var


def solution(mesh):
    in_specs = (P("tm", "band", None), P(), P("tm"), P("band", None), P("band", None))
    out_specs = (P("tm", None, "band", None), P("band", "tm"), P("band", "tm"))
    return jax.shard_map(
        per_device, mesh=mesh, in_specs=in_specs, out_specs=out_specs, check_vma=False
    )
```

```python
import functools
import math

import jax
import jax.numpy as jnp
from jax import lax
from jax.experimental import pallas as pl
from jax.experimental.pallas import tpu as pltpu
from jax.sharding import PartitionSpec as P

LANES = 128
TILE = 16
VMEM_LIMIT = 56 * 1024 * 1024


def round_up(value, unit):
    return -(-value // unit) * unit


def fourier_kernel(coarse_cos_ref, coarse_sin_ref, fine_cos_ref, fine_sin_ref, out_ref):
    lon_count = out_ref.shape[1]
    fine_cos, fine_sin = fine_cos_ref[...], fine_sin_ref[...]
    for index in range(-(-lon_count // LANES)):
        width = min(LANES, lon_count - index * LANES)
        coarse_cos = coarse_cos_ref[:, index : index + 1]
        coarse_sin = coarse_sin_ref[:, index : index + 1]
        values = (coarse_cos * fine_cos - coarse_sin * fine_sin).astype(jnp.bfloat16)
        out_ref[:, index * LANES : index * LANES + width] = values[:, :width]


def fourier_rows(waves, lon_count):
    blocks, slots = waves.shape
    rows = blocks * 2 * slots

    def parts(step):
        lons = jnp.arange(LANES, dtype=jnp.int32) * step
        phase = waves[:, :, None] * lons % lon_count
        angle = phase.astype(jnp.float32) * (2.0 * math.pi / lon_count)
        return jnp.cos(angle), jnp.sin(angle)

    def both(first, second):
        return jnp.stack([first, second], axis=1).reshape(rows, LANES)

    coarse_cos, coarse_sin = parts(LANES)
    fine_cos, fine_sin = parts(1)
    return pl.pallas_call(
        fourier_kernel,
        out_shape=jax.ShapeDtypeStruct((rows, lon_count), jnp.bfloat16),
        compiler_params=pltpu.CompilerParams(vmem_limit_bytes=VMEM_LIMIT),
        cost_estimate=pl.CostEstimate(
            flops=3 * rows * lon_count, bytes_accessed=2 * rows * lon_count, transcendentals=0
        ),
    )(
        both(coarse_cos, -coarse_sin),
        both(coarse_sin, coarse_cos),
        both(fine_cos, fine_cos),
        both(fine_sin, fine_sin),
    )


def table_kernel(steps, lane_tiles, top, low_ref, first_ref, second_ref, cos_ref, weight_ref, out_ref, rows_ref, scale_ref):
    tiles = range(lane_tiles)
    low = low_ref[...]
    high = top - low
    low_next = low + 1.0
    lat_count = out_ref.shape[2]
    pairs = out_ref.shape[0]

    def lanes(ref, tile):
        return ref[:, tile * LANES : (tile + 1) * LANES]

    cosines = [lanes(cos_ref, t) for t in tiles]
    weights = [lanes(weight_ref, t) for t in tiles]
    second = [lanes(second_ref, t) for t in tiles]
    for t in tiles:
        half = jnp.exp(0.5 * second[t])
        scale_ref[2, :, t * LANES : (t + 1) * LANES] = half * weights[t]
        scale_ref[3, :, t * LANES : (t + 1) * LANES] = half

    def block(index, carry):
        current, lagged, scale, last_inverse = carry
        for t in tiles:
            largest = jnp.maximum(jnp.maximum(jnp.abs(current[t]), jnp.abs(lagged[t])), 1.0)
            current[t] = current[t] / largest
            lagged[t] = lagged[t] / largest
            scale[t] = scale[t] + jnp.log(largest)
            half = jnp.exp(0.5 * scale[t])
            scale_ref[0, :, t * LANES : (t + 1) * LANES] = half * weights[t]
            scale_ref[1, :, t * LANES : (t + 1) * LANES] = half
        begin = (index * TILE).astype(jnp.float32)
        for step in range(TILE):
            row = begin + float(step)
            after = low < row
            above = row - jnp.where(after, low_next, 0.0)
            order = jnp.where(after, low, high)
            degree = above + order
            spread = above * (degree + order)
            square = 4.0 * degree * degree - 1.0
            root = lax.rsqrt(jnp.maximum(square * spread, 1.0))
            factor = square * root
            inverse = spread * root
            fresh = above == 0.0
            for t in tiles:
                advanced = factor * (cosines[t] * current[t] - last_inverse * lagged[t])
                lagged[t] = current[t]
                current[t] = jnp.where(fresh, 1.0, advanced)
                rows_ref[t, pl.ds(step, pairs, stride=TILE), :] = current[t]
            last_inverse = inverse
        renewed = (low_next >= begin) & (low_next < begin + float(TILE))
        for t in tiles:
            scale[t] = jnp.where(renewed, second[t], scale[t])
        row_index = lax.broadcasted_iota(jnp.int32, (TILE, LANES), 0).astype(jnp.float32) + begin
        for pair in range(pairs):
            mark = low[pair : pair + 1, :]
            before = (row_index <= mark) | (mark + 1.0 < begin)
            for t in tiles:
                span = slice(t * LANES, min((t + 1) * LANES, lat_count))
                width = span.stop - span.start
                here = slice(t * LANES, (t + 1) * LANES)
                values = rows_ref[t, pair * TILE : (pair + 1) * TILE, :]
                one = jnp.where(before, scale_ref[0, pair : pair + 1, here], scale_ref[2, pair : pair + 1, here])
                two = jnp.where(before, scale_ref[1, pair : pair + 1, here], scale_ref[3, pair : pair + 1, here])
                values = (values * one * two).astype(jnp.bfloat16)
                out_ref[pair, pl.ds(pl.multiple_of(index * TILE, TILE), TILE), span] = values[:, :width]
        return current, lagged, scale, last_inverse

    zeros = jnp.zeros((pairs, LANES), jnp.float32)
    start = (
        [zeros for _ in tiles],
        [zeros for _ in tiles],
        [lanes(first_ref, t) for t in tiles],
        zeros,
    )
    lax.fori_loop(0, steps // TILE, block, start)


def packed_table(low_waves, lats, lat_count, degree_count, steps):
    pair_count = low_waves.shape[0]
    lat_half = lats.shape[0]
    lane_tiles = -(-lat_half // LANES)
    width = lane_tiles * LANES
    top = float(degree_count - 1)
    index = jnp.pad(lats, (0, width - lat_half), mode="edge")
    colatitude = (index.astype(jnp.float32) + 0.5) * (math.pi / lat_count)
    sines = jnp.sin(colatitude)
    log_sines = jnp.log(sines)
    low = low_waves.astype(jnp.float32)

    def log_start(order):
        base = 0.5 * (
            jnp.log(order + 0.5)
            + jax.scipy.special.gammaln(order + 0.5)
            - jax.scipy.special.gammaln(order + 1.0)
            - 0.5 * math.log(math.pi)
        )
        return base[:, None] + order[:, None] * log_sines[None, :]

    def spread(row):
        return jnp.broadcast_to(row[None, :], (pair_count, width))

    return pl.pallas_call(
        functools.partial(table_kernel, steps, lane_tiles, top),
        out_shape=jax.ShapeDtypeStruct((pair_count, steps, lat_half), jnp.bfloat16),
        scratch_shapes=[
            pltpu.VMEM((lane_tiles, pair_count * TILE, LANES), jnp.float32),
            pltpu.VMEM((4, pair_count, width), jnp.float32),
        ],
        compiler_params=pltpu.CompilerParams(vmem_limit_bytes=VMEM_LIMIT),
        cost_estimate=pl.CostEstimate(
            flops=pair_count * steps * width * 60, bytes_accessed=pair_count * steps * width * 2, transcendentals=0
        ),
    )(
        jnp.broadcast_to(low[:, None], (pair_count, LANES)),
        log_start(top - low),
        log_start(low),
        spread(jnp.cos(colatitude)),
        spread(sines * (math.pi / lat_count)),
    )


def gather_slots(in_refs, flat_ref, slot_ref):
    lats, rows, days = in_refs[0].shape
    lat_half = len(in_refs) * lats
    for part in range(2):
        for source, in_ref in enumerate(in_refs):
            values = in_ref[:, part * TILE : (part + 1) * TILE, :].astype(jnp.float32)
            flat_ref[pl.ds(source * lats * TILE, lats * TILE), :] = values.reshape(lats * TILE, days)
        for slot in range(TILE):
            column = flat_ref[pl.ds(slot, lat_half, stride=TILE), :]
            slot_ref[slot, :, part * days : (part + 1) * days] = column.astype(jnp.bfloat16)


def pair_sum(pair, low, table_ref, slot_ref):
    table = table_ref[pair]
    high_sum = jnp.dot(table, slot_ref[2 * pair], preferred_element_type=jnp.float32)
    low_sum = jnp.dot(table, slot_ref[2 * pair + 1], preferred_element_type=jnp.float32)
    row = lax.broadcasted_iota(jnp.int32, high_sum.shape, 0)
    return jnp.where(row <= low, high_sum, low_sum)


def partial_kernel(low_ref, table_ref, *rest):
    out_ref, flat_ref, slot_ref = rest[-3:]
    gather_slots(rest[:-3], flat_ref, slot_ref)

    def one(pair, carry):
        out_ref[pair] = pair_sum(pair, low_ref[pair], table_ref, slot_ref).astype(jnp.bfloat16)
        return carry

    lax.fori_loop(0, TILE // 2, one, 0)


def finish_kernel(sources, low_ref, wave_ref, shift_ref, table_ref, other_ref, own_ref, season_ref, *rest):
    out_ref, misc_ref, flat_ref, slot_ref, turned_ref = rest[-5:]
    steps = table_ref.shape[1]
    days = out_ref.shape[0]
    degrees = out_ref.shape[3]
    lane_tiles = degrees // LANES
    gather_slots(rest[:sources], flat_ref, slot_ref)
    lane = lax.broadcasted_iota(jnp.int32, (steps, LANES), 1)
    turn = (
        lax.broadcasted_iota(jnp.int32, (days, days), 0) == lax.broadcasted_iota(jnp.int32, (days, days), 1)
    ).astype(jnp.bfloat16)
    pick_row = lax.broadcasted_iota(jnp.int32, (8, LANES), 0)
    pick_lane = lax.broadcasted_iota(jnp.int32, (8, LANES), 1)
    wanted = jnp.where(pick_row == 1, 2, jnp.where(pick_row == 2, LANES - 1, 0))
    wanted = jnp.where(pick_row > 2, jnp.where(pick_row == 3, 1, pick_row - 1), wanted)
    pick = ((pick_lane == wanted) & (pick_row < 6)).astype(jnp.bfloat16)
    row = lax.broadcasted_iota(jnp.int32, (steps, degrees), 0)
    degree = lax.broadcasted_iota(jnp.int32, (steps, degrees), 1)
    transposed = (((1,), (1,)), ((), ()))

    def one(pair, carry):
        own = pair_sum(pair, low_ref[pair], table_ref, slot_ref)
        total = own + other_ref[pair].astype(jnp.float32)
        places = []
        own_rows = jnp.zeros((steps, 8), jnp.float32)
        for position in range(2):
            slot = 2 * pair + position
            chosen = (row - degree == shift_ref[slot]) & (degree >= wave_ref[slot])
            places.append(chosen.astype(jnp.bfloat16))
            own_rows = own_rows + lax.dot_general(
                places[position], own_ref[slot], transposed, preferred_element_type=jnp.float32
            )
        ar = own_rows[:, 0:1] + own_rows[:, 1:2]
        half = own_rows[:, 2:3] + own_rows[:, 3:4]
        turned = []
        parts = []
        sum_coef = jnp.zeros((steps, LANES), jnp.float32)
        sum_var = jnp.zeros((steps, LANES), jnp.float32)
        for part in range(2):
            spectral = total[:, part * days : (part + 1) * days]
            parts.append(spectral)
            previous = jnp.where(lane == 0, 0.0, pltpu.roll(spectral, 1, 1))
            residual = spectral - ar * previous
            scaled = residual * season_ref[0:1, :]
            innovation = (scaled * half).astype(jnp.bfloat16)
            turned.append(
                lax.dot_general(turn, innovation, transposed, preferred_element_type=jnp.float32)
            )
            weighted = residual * season_ref[1:2, :]
            sum_coef = sum_coef + weighted * previous
            sum_var = sum_var + weighted * residual
        sum_coef = jnp.sum(sum_coef, axis=1, keepdims=True)
        sum_var = jnp.sum(sum_var, axis=1, keepdims=True)
        misc = jnp.where(
            (lane == 0) | (lane == LANES - 1),
            parts[0],
            jnp.where(lane < 3, pltpu.roll(parts[1], 2, 1), jnp.where(lane == 3, sum_coef, sum_var)),
        )
        misc_high = misc.astype(jnp.bfloat16)
        misc_low = (misc - misc_high.astype(jnp.float32)).astype(jnp.bfloat16)
        for piece in (misc_high, misc_low):
            turned.append(lax.dot_general(pick, piece, transposed, preferred_element_type=jnp.float32))
        stacked = jnp.concatenate(turned, axis=0).astype(jnp.bfloat16)
        for position in range(2):
            slot = 2 * pair + position
            placed = jnp.dot(stacked, places[position], preferred_element_type=jnp.float32)
            for part in range(2):
                for t in range(lane_tiles):
                    turned_ref[part, t, pl.ds(slot, days, stride=TILE), :] = placed[
                        part * days : (part + 1) * days, t * LANES : (t + 1) * LANES
                    ]
            misc_ref[slot] = placed[2 * days : 2 * days + 8] + placed[2 * days + 8 : 2 * days + 16]
        return carry

    lax.fori_loop(0, TILE // 2, one, 0)

    def write(day, carry):
        for part in range(2):
            for t in range(lane_tiles):
                values = turned_ref[part, t, pl.ds(pl.multiple_of(day * TILE, TILE), TILE), :]
                out_ref[day, part, :, t * LANES : (t + 1) * LANES] = values.astype(jnp.bfloat16)
        return carry

    lax.fori_loop(0, days, write, 0)


def leading(shape, chunk):
    return pl.BlockSpec(shape, lambda i: (chunk,) + (0,) * (len(shape) - 1))


def partial_sums(chunk, low, blocks, table):
    lats, rows, days = blocks[0].shape
    steps, lat_half = table.shape[1:]
    pairs = TILE // 2
    return pl.pallas_call(
        partial_kernel,
        grid=(1,),
        in_specs=[
            pl.BlockSpec(memory_space=pltpu.SMEM),
            leading((pairs, steps, lat_half), chunk),
        ]
        + [leading(block.shape, 0) for block in blocks],
        out_specs=leading((pairs, steps, 2 * days), 0),
        out_shape=jax.ShapeDtypeStruct((pairs, steps, 2 * days), jnp.bfloat16),
        scratch_shapes=[
            pltpu.VMEM((lat_half * TILE, days), jnp.float32),
            pltpu.VMEM((TILE, lat_half, 2 * days), jnp.bfloat16),
        ],
        compiler_params=pltpu.CompilerParams(vmem_limit_bytes=VMEM_LIMIT),
        cost_estimate=pl.CostEstimate(
            flops=6 * TILE * steps * lat_half * 2 * days, bytes_accessed=8 * 1024 * 1024, transcendentals=0
        ),
    )(low, table, *blocks)


def finish(chunk, low, waves, shifts, blocks, table, other, own, season, held, slot_total):
    lats, rows, days = blocks[0].shape
    steps, lat_half = table.shape[1:]
    pairs = TILE // 2
    degrees = own.shape[2]
    smem = pl.BlockSpec(memory_space=pltpu.SMEM)
    operands = [low, waves, shifts, table, other, own, season, *blocks]
    in_specs = [
        smem,
        smem,
        smem,
        leading((pairs, steps, lat_half), chunk),
        leading((pairs, steps, 2 * days), 0),
        leading((TILE, 8, degrees), chunk),
        leading((8, LANES), 0),
    ] + [leading(block.shape, 0) for block in blocks]
    aliases = {}
    if held is not None:
        operands.append(held)
        in_specs.append(pl.BlockSpec(memory_space=pl.ANY))
        aliases = {len(operands) - 1: 0}
    return pl.pallas_call(
        functools.partial(finish_kernel, len(blocks)),
        grid=(1,),
        in_specs=in_specs,
        out_specs=[
            pl.BlockSpec((days, 2, TILE, degrees), lambda i: (0, 0, chunk, 0)),
            leading((TILE, 8, degrees), 0),
        ],
        out_shape=[
            jax.ShapeDtypeStruct((days, 2, slot_total, degrees), jnp.bfloat16),
            jax.ShapeDtypeStruct((TILE, 8, degrees), jnp.float32),
        ],
        input_output_aliases=aliases,
        scratch_shapes=[
            pltpu.VMEM((lat_half * TILE, days), jnp.float32),
            pltpu.VMEM((TILE, lat_half, 2 * days), jnp.bfloat16),
            pltpu.VMEM((2, degrees // LANES, days * TILE, LANES), jnp.float32),
        ],
        compiler_params=pltpu.CompilerParams(vmem_limit_bytes=VMEM_LIMIT),
        cost_estimate=pl.CostEstimate(
            flops=12 * TILE * steps * lat_half * 2 * days, bytes_accessed=12 * 1024 * 1024, transcendentals=0
        ),
    )(*operands)


def split_rows(values):
    high = lax.reduce_precision(values, 8, 7)
    return high.astype(jnp.bfloat16), (values - high).astype(jnp.bfloat16)


def after(values, waited):
    return lax.optimization_barrier((values, waited))[0]


def per_device(fields, wave_table, day_of_year, ar_coef, log_var):
    band_count = lax.axis_size("band")
    time_count = lax.axis_size("tm")
    band = lax.axis_index("band")
    slot_count, degree_count = ar_coef.shape
    day_count, lat_local, lon_count = fields.shape
    lat_count = lat_local * band_count
    group = band_count // 2
    steps = round_up(degree_count + 1, TILE)
    total_days = day_count * time_count
    slot_pad = round_up(slot_count, TILE)
    chunks = slot_pad // TILE
    pairs = slot_pad // 2
    half_index = band // group
    rank = band % group
    mirror = [(i, (i + group) % band_count) for i in range(band_count)]
    peers = [rank ^ k for k in range(group)]

    waves = wave_table.reshape(2, group, slot_count // 2, 2)
    high_low = jnp.stack([waves.max(-1), waves.min(-1)], axis=-1)
    high_low = jnp.pad(high_low, ((0, 0), (0, 0), (0, pairs - slot_count // 2), (0, 0)))
    ordered = high_low.reshape(2, group, slot_pad)
    present = jnp.arange(slot_pad) < slot_count

    def by_peer(side):
        table = lax.dynamic_index_in_dim(ordered, side, 0, keepdims=False)
        return jnp.stack([lax.dynamic_index_in_dim(table, peer, 0, keepdims=False) for peer in peers])

    own_waves, far_waves = by_peer(half_index), by_peer(1 - half_index)
    own_low, far_low = own_waves[0, 1::2], far_waves[0, 1::2]
    lats = jnp.concatenate(
        [(half_index * group + peer) * lat_local + jnp.arange(lat_local, dtype=jnp.int32) for peer in peers]
    )

    def transform(source, waves_of, first, count):
        picked = waves_of[:, first * TILE : (first + count) * TILE].reshape(group * count, TILE)
        table = fourier_rows(picked, lon_count)
        if slot_pad != slot_count:
            mask = present[first * TILE : (first + count) * TILE].reshape(count, 1, TILE)
            mask = jnp.broadcast_to(mask, (group, count, 2, TILE)).reshape(-1, 1)
            table = table * mask.astype(jnp.bfloat16)
        coeffs = jnp.einsum("djk,qk->jqd", source, table, preferred_element_type=jnp.float32)
        coeffs = coeffs.astype(jnp.bfloat16).reshape(lat_local, group, count, 2 * TILE, day_count)
        return [[coeffs[:, peer, i] for peer in range(group)] for i in range(count)]

    def exchange(blocks):
        moved = [
            lax.ppermute(blocks[k], "band", [(i, i ^ k) for i in range(band_count)]) for k in range(1, group)
        ]
        return [blocks[0]] + moved

    far_blocks = transform(fields, far_waves, 0, 1)
    arrived = [exchange(far_blocks[0])]
    if chunks > 1:
        far_blocks = far_blocks + transform(after(fields, far_blocks[0][0]), far_waves, 1, chunks - 1)
    far_table = packed_table(after(far_low, far_blocks[-1][0]), lats, lat_count, degree_count, steps)

    def queue(blocks):
        if len(arrived) > 1:
            blocks = after(blocks, arrived[-2][1])
        arrived.append(exchange(blocks))

    for chunk in range(1, chunks):
        queue(far_blocks[chunk])

    others = []

    def send_sums(chunk):
        low = far_low[chunk * TILE // 2 : (chunk + 1) * TILE // 2]
        sums = partial_sums(chunk, low, arrived[chunk], far_table)
        others.append(lax.ppermute(sums, "band", mirror))
        return sums

    first_sums = send_sums(0)
    own_blocks = transform(after(fields, first_sums), own_waves, 0, chunks)
    own_table = packed_table(after(own_low, own_blocks[0][0]), lats, lat_count, degree_count, steps)
    for chunk in range(chunks):
        queue(own_blocks[chunk])
        if chunk + 1 < chunks:
            send_sums(chunk + 1)

    slot_waves = lax.dynamic_slice_in_dim(wave_table, band * slot_count, slot_count)
    pad_slots = (0, slot_pad - slot_count)
    kernel_waves = jnp.pad(slot_waves, pad_slots)
    is_low = kernel_waves == jnp.repeat(own_low, 2)
    shifts = jnp.where(is_low, 1, -kernel_waves)
    own_rows = jnp.stack([*split_rows(ar_coef), *split_rows(jnp.exp(-0.5 * log_var))], axis=1)
    own_rows = jnp.pad(own_rows, (pad_slots, (0, 4), (0, 0)))
    season = 1.0 + 0.5 * jnp.cos(day_of_year.astype(jnp.float32) * (2.0 * math.pi / 365.0))
    later = (jnp.arange(day_count) > 0).astype(jnp.float32)
    season_rows = jnp.pad(jnp.stack([lax.rsqrt(season), later / season]), ((0, 6), (0, 0)))

    innovation = None
    misc = []
    for chunk in range(chunks):
        low = own_low[chunk * TILE // 2 : (chunk + 1) * TILE // 2]
        span = slice(chunk * TILE, (chunk + 1) * TILE)
        innovation, rows = finish(
            chunk, low, kernel_waves[span], shifts[span], arrived[chunks + chunk], own_table, others[chunk],
            own_rows, season_rows, innovation, slot_pad,
        )
        misc.append(rows)
    innovation = innovation[:, :, :slot_count]
    misc = jnp.concatenate(misc, axis=0)[:slot_count, :6]

    degree_list = jnp.arange(degree_count, dtype=jnp.int32)
    valid_mask = (degree_list[None, :] >= slot_waves[:, None]).astype(jnp.float32)
    edges = misc.transpose(1, 0, 2)
    route = [(i, i + 1) for i in range(time_count - 1)]
    carried = lax.ppermute(edges[2:4].astype(jnp.bfloat16), "tm", route).astype(jnp.float32)
    scale = jnp.exp(-0.5 * log_var) * lax.rsqrt(season[0]) * valid_mask
    opening = ((edges[0:2] - ar_coef[None] * carried) * scale[None]).astype(jnp.bfloat16)
    innovation = lax.dynamic_update_slice_in_dim(innovation, opening[None], 0, 0)

    column_width = degree_count // time_count
    place = lax.axis_index("tm")
    columns = [misc[:, :, i * column_width : (i + 1) * column_width] for i in range(time_count)]
    moved = lax.all_to_all(jnp.stack(columns).astype(jnp.bfloat16), "tm", 0, 0, tiled=True).astype(jnp.float32)

    def own_columns(values):
        return lax.dynamic_slice_in_dim(values, place * column_width, column_width, 1)

    local_ar, local_var = own_columns(ar_coef), jnp.exp(-own_columns(log_var))
    first_days = day_of_year[0] + (jnp.arange(time_count, dtype=jnp.int32) - place) * day_count
    first_days = (first_days % 365).astype(jnp.float32)
    openness = 1.0 / (1.0 + 0.5 * jnp.cos(first_days * (2.0 * math.pi / 365.0)))
    first = moved[:, :, 0:2]
    before = jnp.concatenate([jnp.zeros_like(moved[:1, :, 2:4]), moved[:-1, :, 2:4]], axis=0)
    residual = first - local_ar[None, :, None] * before
    weighted = residual * openness[:, None, None, None]
    sum_coef = jnp.sum(moved[:, :, 4], axis=0) + jnp.sum(weighted * before, axis=(0, 2))
    sum_var = jnp.sum(moved[:, :, 5], axis=0) + jnp.sum(weighted * residual, axis=(0, 2))
    local_mask = own_columns(valid_mask)
    grad_coef = -local_mask * local_var * sum_coef / (2.0 * total_days)
    grad_var = local_mask * (total_days - 0.5 * local_var * sum_var) / (2.0 * total_days)
    return innovation, grad_coef, grad_var


def solution(mesh):
    in_specs = (P("tm", "band", None), P(), P("tm"), P("band", None), P("band", None))
    out_specs = (P("tm", None, "band", None), P("band", "tm"), P("band", "tm"))
    return jax.shard_map(
        per_device, mesh=mesh, in_specs=in_specs, out_specs=out_specs, check_vma=False
    )
```

```python
import functools
import math

import jax
import jax.numpy as jnp
from jax import lax
from jax.experimental import pallas as pl
from jax.experimental.pallas import tpu as pltpu
from jax.sharding import PartitionSpec as P

LANES = 128
TILE = 16
HALF = TILE // 4
VMEM_LIMIT = 56 * 1024 * 1024


def round_up(value, unit):
    return -(-value // unit) * unit


def fourier_kernel(coarse_cos_ref, coarse_sin_ref, fine_cos_ref, fine_sin_ref, out_ref):
    lon_count = out_ref.shape[1]
    fine_cos, fine_sin = fine_cos_ref[...], fine_sin_ref[...]
    for index in range(-(-lon_count // LANES)):
        width = min(LANES, lon_count - index * LANES)
        coarse_cos = coarse_cos_ref[:, index : index + 1]
        coarse_sin = coarse_sin_ref[:, index : index + 1]
        values = (coarse_cos * fine_cos - coarse_sin * fine_sin).astype(jnp.bfloat16)
        out_ref[:, index * LANES : index * LANES + width] = values[:, :width]


def fourier_rows(waves, lon_count):
    blocks, slots = waves.shape
    rows = blocks * 2 * slots

    def parts(step):
        lons = jnp.arange(LANES, dtype=jnp.int32) * step
        phase = waves[:, :, None] * lons % lon_count
        angle = phase.astype(jnp.float32) * (2.0 * math.pi / lon_count)
        return jnp.cos(angle), jnp.sin(angle)

    def both(first, second):
        return jnp.stack([first, second], axis=1).reshape(rows, LANES)

    coarse_cos, coarse_sin = parts(LANES)
    fine_cos, fine_sin = parts(1)
    return pl.pallas_call(
        fourier_kernel,
        out_shape=jax.ShapeDtypeStruct((rows, lon_count), jnp.bfloat16),
        compiler_params=pltpu.CompilerParams(vmem_limit_bytes=VMEM_LIMIT),
    )(
        both(coarse_cos, -coarse_sin),
        both(coarse_sin, coarse_cos),
        both(fine_cos, fine_cos),
        both(fine_sin, fine_sin),
    )


def transform_kernel(in_ref, table_ref, *out_refs):
    lats, _, days = in_ref.shape
    for lat in range(0, lats, 2):
        both = jnp.concatenate([in_ref[lat], in_ref[lat + 1]], axis=1)
        sums = jnp.dot(table_ref[...], both, preferred_element_type=jnp.float32).astype(jnp.bfloat16)
        begin = 0
        for out_ref in out_refs:
            piece = sums[begin : begin + out_ref.shape[1]]
            begin += out_ref.shape[1]
            out_ref[lat] = piece[:, :days]
            out_ref[lat + 1] = piece[:, days:]


def longitude_sums(fields, table, block_rows):
    lats, lon_count, days = fields.shape
    group = 8 if lats % 8 == 0 else 2
    rows = table.shape[0]
    blocks = rows // block_rows
    return pl.pallas_call(
        transform_kernel,
        grid=(lats // group,),
        in_specs=[
            pl.BlockSpec((group, lon_count, days), lambda i: (i, 0, 0)),
            pl.BlockSpec((rows, lon_count), lambda i: (0, 0)),
        ],
        out_specs=[pl.BlockSpec((group, block_rows, days), lambda i: (i, 0, 0))] * blocks,
        out_shape=[jax.ShapeDtypeStruct((lats, block_rows, days), jnp.bfloat16)] * blocks,
        compiler_params=pltpu.CompilerParams(vmem_limit_bytes=VMEM_LIMIT),
    )(fields, table)


def table_kernel(steps, lane_tiles, top, low_ref, first_ref, second_ref, cos_ref, weight_ref, out_ref, rows_ref, scale_ref):
    tiles = range(lane_tiles)
    low = low_ref[...]
    high = top - low
    low_next = low + 1.0
    lat_count = out_ref.shape[2]
    pairs = out_ref.shape[0]

    def lanes(ref, tile):
        return ref[:, tile * LANES : (tile + 1) * LANES]

    cosines = [lanes(cos_ref, t) for t in tiles]
    weights = [lanes(weight_ref, t) for t in tiles]
    second = [lanes(second_ref, t) for t in tiles]
    for t in tiles:
        half = jnp.exp(0.5 * second[t])
        scale_ref[2, :, t * LANES : (t + 1) * LANES] = half * weights[t]
        scale_ref[3, :, t * LANES : (t + 1) * LANES] = half

    def block(index, carry):
        current, lagged, scale, last_inverse = carry
        for t in tiles:
            largest = jnp.maximum(jnp.maximum(jnp.abs(current[t]), jnp.abs(lagged[t])), 1.0)
            current[t] = current[t] / largest
            lagged[t] = lagged[t] / largest
            scale[t] = scale[t] + jnp.log(largest)
            half = jnp.exp(0.5 * scale[t])
            scale_ref[0, :, t * LANES : (t + 1) * LANES] = half * weights[t]
            scale_ref[1, :, t * LANES : (t + 1) * LANES] = half
        begin = (index * TILE).astype(jnp.float32)
        for step in range(TILE):
            row = begin + float(step)
            after = low < row
            above = row - jnp.where(after, low_next, 0.0)
            order = jnp.where(after, low, high)
            degree = above + order
            spread = above * (degree + order)
            square = 4.0 * degree * degree - 1.0
            root = lax.rsqrt(jnp.maximum(square * spread, 1.0))
            factor = square * root
            inverse = spread * root
            fresh = above == 0.0
            for t in tiles:
                advanced = factor * (cosines[t] * current[t] - last_inverse * lagged[t])
                lagged[t] = current[t]
                current[t] = jnp.where(fresh, 1.0, advanced)
                rows_ref[t, pl.ds(step, pairs, stride=TILE), :] = current[t]
            last_inverse = inverse
        renewed = (low_next >= begin) & (low_next < begin + float(TILE))
        for t in tiles:
            scale[t] = jnp.where(renewed, second[t], scale[t])
        row_index = lax.broadcasted_iota(jnp.int32, (TILE, LANES), 0).astype(jnp.float32) + begin
        for pair in range(pairs):
            mark = low[pair : pair + 1, :]
            before = (row_index <= mark) | (mark + 1.0 < begin)
            for t in tiles:
                span = slice(t * LANES, min((t + 1) * LANES, lat_count))
                width = span.stop - span.start
                here = slice(t * LANES, (t + 1) * LANES)
                values = rows_ref[t, pair * TILE : (pair + 1) * TILE, :]
                one = jnp.where(before, scale_ref[0, pair : pair + 1, here], scale_ref[2, pair : pair + 1, here])
                two = jnp.where(before, scale_ref[1, pair : pair + 1, here], scale_ref[3, pair : pair + 1, here])
                values = (values * one * two).astype(jnp.bfloat16)
                out_ref[pair, pl.ds(pl.multiple_of(index * TILE, TILE), TILE), span] = values[:, :width]
        return current, lagged, scale, last_inverse

    zeros = jnp.zeros((pairs, LANES), jnp.float32)
    start = (
        [zeros for _ in tiles],
        [zeros for _ in tiles],
        [lanes(first_ref, t) for t in tiles],
        zeros,
    )
    lax.fori_loop(0, steps // TILE, block, start)


def packed_table(low_waves, lats, lat_count, degree_count, steps):
    pair_count = low_waves.shape[0]
    lat_half = lats.shape[0]
    lane_tiles = -(-lat_half // LANES)
    width = lane_tiles * LANES
    top = float(degree_count - 1)
    index = jnp.pad(lats, (0, width - lat_half), mode="edge")
    colatitude = (index.astype(jnp.float32) + 0.5) * (math.pi / lat_count)
    sines = jnp.sin(colatitude)
    log_sines = jnp.log(sines)
    low = low_waves.astype(jnp.float32)

    def log_start(order):
        base = 0.5 * (
            jnp.log(order + 0.5)
            + jax.scipy.special.gammaln(order + 0.5)
            - jax.scipy.special.gammaln(order + 1.0)
            - 0.5 * math.log(math.pi)
        )
        return base[:, None] + order[:, None] * log_sines[None, :]

    def spread(row):
        return jnp.broadcast_to(row[None, :], (pair_count, width))

    return pl.pallas_call(
        functools.partial(table_kernel, steps, lane_tiles, top),
        out_shape=jax.ShapeDtypeStruct((pair_count, steps, lat_half), jnp.bfloat16),
        scratch_shapes=[
            pltpu.VMEM((lane_tiles, pair_count * TILE, LANES), jnp.float32),
            pltpu.VMEM((4, pair_count, width), jnp.float32),
        ],
        compiler_params=pltpu.CompilerParams(vmem_limit_bytes=VMEM_LIMIT),
    )(
        jnp.broadcast_to(low[:, None], (pair_count, LANES)),
        log_start(top - low),
        log_start(low),
        spread(jnp.cos(colatitude)),
        spread(sines * (math.pi / lat_count)),
    )


def gather_slots(in_refs, flat_ref, slot_ref):
    lats, rows, days = in_refs[0].shape
    lat_half = len(in_refs) * lats
    for part in range(2):
        for source, in_ref in enumerate(in_refs):
            values = in_ref[:, part * TILE : (part + 1) * TILE, :].astype(jnp.float32)
            flat_ref[pl.ds(source * lats * TILE, lats * TILE), :] = values.reshape(lats * TILE, days)
        for slot in range(TILE):
            column = flat_ref[pl.ds(slot, lat_half, stride=TILE), :]
            slot_ref[slot, :, part * days : (part + 1) * days] = column.astype(jnp.bfloat16)


def pair_sum(pair, low, table_ref, slot_ref):
    table = table_ref[pair]
    high_sum = jnp.dot(table, slot_ref[2 * pair], preferred_element_type=jnp.float32)
    low_sum = jnp.dot(table, slot_ref[2 * pair + 1], preferred_element_type=jnp.float32)
    row = lax.broadcasted_iota(jnp.int32, high_sum.shape, 0)
    return jnp.where(row <= low, high_sum, low_sum)


def by_halves(one):
    def two(step, carry):
        one(0, step)
        one(1, step)
        return carry

    lax.fori_loop(0, HALF, two, 0)


def partial_kernel(low_ref, table_ref, *rest):
    *in_refs, first_ref, second_ref, flat_ref, slot_ref = rest
    out_refs = (first_ref, second_ref)
    gather_slots(in_refs, flat_ref, slot_ref)

    def one(half, step):
        pair = half * HALF + step
        out_refs[half][step] = pair_sum(pair, low_ref[pair], table_ref, slot_ref).astype(jnp.bfloat16)

    by_halves(one)


def finish_kernel(sources, low_ref, wave_ref, shift_ref, table_ref, first_ref, second_ref, own_ref, season_ref, *rest):
    out_ref, misc_ref, flat_ref, slot_ref, turned_ref = rest[-5:]
    steps = table_ref.shape[1]
    days = out_ref.shape[0]
    degrees = out_ref.shape[3]
    lane_tiles = degrees // LANES
    gather_slots(rest[:sources], flat_ref, slot_ref)
    lane = lax.broadcasted_iota(jnp.int32, (steps, LANES), 1)
    turn = (
        lax.broadcasted_iota(jnp.int32, (days, days), 0) == lax.broadcasted_iota(jnp.int32, (days, days), 1)
    ).astype(jnp.bfloat16)
    pick_row = lax.broadcasted_iota(jnp.int32, (8, LANES), 0)
    pick_lane = lax.broadcasted_iota(jnp.int32, (8, LANES), 1)
    wanted = jnp.where(pick_row == 1, 2, jnp.where(pick_row == 2, LANES - 1, 0))
    wanted = jnp.where(pick_row > 2, jnp.where(pick_row == 3, 1, pick_row - 1), wanted)
    pick = ((pick_lane == wanted) & (pick_row < 6)).astype(jnp.bfloat16)
    row = lax.broadcasted_iota(jnp.int32, (steps, degrees), 0)
    degree = lax.broadcasted_iota(jnp.int32, (steps, degrees), 1)
    transposed = (((1,), (1,)), ((), ()))

    other_refs = (first_ref, second_ref)

    def one(part_of, step):
        pair = part_of * HALF + step
        own = pair_sum(pair, low_ref[pair], table_ref, slot_ref)
        total = own + other_refs[part_of][step].astype(jnp.float32)
        places = []
        own_rows = jnp.zeros((steps, 8), jnp.float32)
        for position in range(2):
            slot = 2 * pair + position
            chosen = (row - degree == shift_ref[slot]) & (degree >= wave_ref[slot])
            places.append(chosen.astype(jnp.bfloat16))
            own_rows = own_rows + lax.dot_general(
                places[position], own_ref[slot], transposed, preferred_element_type=jnp.float32
            )
        ar = own_rows[:, 0:1] + own_rows[:, 1:2]
        half = own_rows[:, 2:3] + own_rows[:, 3:4]
        turned = []
        parts = []
        sum_coef = jnp.zeros((steps, LANES), jnp.float32)
        sum_var = jnp.zeros((steps, LANES), jnp.float32)
        for part in range(2):
            spectral = total[:, part * days : (part + 1) * days]
            parts.append(spectral)
            previous = jnp.where(lane == 0, 0.0, pltpu.roll(spectral, 1, 1))
            residual = spectral - ar * previous
            scaled = residual * season_ref[0:1, :]
            innovation = (scaled * half).astype(jnp.bfloat16)
            turned.append(
                lax.dot_general(turn, innovation, transposed, preferred_element_type=jnp.float32)
            )
            weighted = residual * season_ref[1:2, :]
            sum_coef = sum_coef + weighted * previous
            sum_var = sum_var + weighted * residual
        sum_coef = jnp.sum(sum_coef, axis=1, keepdims=True)
        sum_var = jnp.sum(sum_var, axis=1, keepdims=True)
        misc = jnp.where(
            (lane == 0) | (lane == LANES - 1),
            parts[0],
            jnp.where(lane < 3, pltpu.roll(parts[1], 2, 1), jnp.where(lane == 3, sum_coef, sum_var)),
        )
        misc_high = misc.astype(jnp.bfloat16)
        misc_low = (misc - misc_high.astype(jnp.float32)).astype(jnp.bfloat16)
        for piece in (misc_high, misc_low):
            turned.append(lax.dot_general(pick, piece, transposed, preferred_element_type=jnp.float32))
        stacked = jnp.concatenate(turned, axis=0).astype(jnp.bfloat16)
        for position in range(2):
            slot = 2 * pair + position
            placed = jnp.dot(stacked, places[position], preferred_element_type=jnp.float32)
            for part in range(2):
                for t in range(lane_tiles):
                    turned_ref[part, t, pl.ds(slot, days, stride=TILE), :] = placed[
                        part * days : (part + 1) * days, t * LANES : (t + 1) * LANES
                    ]
            misc_ref[slot] = placed[2 * days : 2 * days + 8] + placed[2 * days + 8 : 2 * days + 16]

    by_halves(one)

    def write(day, carry):
        for part in range(2):
            for t in range(lane_tiles):
                values = turned_ref[part, t, pl.ds(pl.multiple_of(day * TILE, TILE), TILE), :]
                out_ref[day, part, :, t * LANES : (t + 1) * LANES] = values.astype(jnp.bfloat16)
        return carry

    lax.fori_loop(0, days, write, 0)


def leading(shape, chunk):
    return pl.BlockSpec(shape, lambda i: (chunk,) + (0,) * (len(shape) - 1))


def partial_sums(chunk, place, low, blocks, table):
    lats, rows, days = blocks[0].shape
    steps, lat_half = table.shape[1:]
    pairs = TILE // 2
    return pl.pallas_call(
        partial_kernel,
        grid=(1,),
        in_specs=[
            pl.BlockSpec(memory_space=pltpu.SMEM),
            leading((pairs, steps, lat_half), chunk),
        ]
        + [pl.BlockSpec((lats, 2 * TILE, days), lambda i: (0, place, 0)) for _ in blocks],
        out_specs=[leading((HALF, steps, 2 * days), 0)] * 2,
        out_shape=[jax.ShapeDtypeStruct((HALF, steps, 2 * days), jnp.bfloat16)] * 2,
        scratch_shapes=[
            pltpu.VMEM((lat_half * TILE, days), jnp.float32),
            pltpu.VMEM((TILE, lat_half, 2 * days), jnp.bfloat16),
        ],
        compiler_params=pltpu.CompilerParams(vmem_limit_bytes=VMEM_LIMIT),
    )(low, table, *blocks)


def finish(chunk, low, waves, shifts, blocks, table, other, own, season, held, slot_total):
    lats, rows, days = blocks[0].shape
    steps, lat_half = table.shape[1:]
    pairs = TILE // 2
    degrees = own.shape[2]
    smem = pl.BlockSpec(memory_space=pltpu.SMEM)
    operands = [low, waves, shifts, table, *other, own, season, *blocks]
    in_specs = [
        smem,
        smem,
        smem,
        leading((pairs, steps, lat_half), chunk),
        leading((HALF, steps, 2 * days), 0),
        leading((HALF, steps, 2 * days), 0),
        leading((TILE, 8, degrees), chunk),
        leading((8, LANES), 0),
    ] + [leading(block.shape, 0) for block in blocks]
    aliases = {}
    if held is not None:
        operands.append(held)
        in_specs.append(pl.BlockSpec(memory_space=pl.ANY))
        aliases = {len(operands) - 1: 0}
    return pl.pallas_call(
        functools.partial(finish_kernel, len(blocks)),
        grid=(1,),
        in_specs=in_specs,
        out_specs=[
            pl.BlockSpec((days, 2, TILE, degrees), lambda i: (0, 0, chunk, 0)),
            leading((TILE, 8, degrees), 0),
        ],
        out_shape=[
            jax.ShapeDtypeStruct((days, 2, slot_total, degrees), jnp.bfloat16),
            jax.ShapeDtypeStruct((TILE, 8, degrees), jnp.float32),
        ],
        input_output_aliases=aliases,
        scratch_shapes=[
            pltpu.VMEM((lat_half * TILE, days), jnp.float32),
            pltpu.VMEM((TILE, lat_half, 2 * days), jnp.bfloat16),
            pltpu.VMEM((2, degrees // LANES, days * TILE, LANES), jnp.float32),
        ],
        compiler_params=pltpu.CompilerParams(vmem_limit_bytes=VMEM_LIMIT),
    )(*operands)


def split_rows(values):
    high = lax.reduce_precision(values, 8, 7)
    return high.astype(jnp.bfloat16), (values - high).astype(jnp.bfloat16)


def after(values, waited):
    return lax.optimization_barrier((values, waited))[0]


def per_device(fields, wave_table, day_of_year, ar_coef, log_var):
    band_count = lax.axis_size("band")
    time_count = lax.axis_size("tm")
    band = lax.axis_index("band")
    slot_count, degree_count = ar_coef.shape
    day_count, lat_local, lon_count = fields.shape
    lat_count = lat_local * band_count
    group = band_count // 2
    steps = round_up(degree_count + 1, TILE)
    total_days = day_count * time_count
    slot_pad = round_up(slot_count, TILE)
    chunks = slot_pad // TILE
    pairs = slot_pad // 2
    half_index = band // group
    rank = band % group
    mirror = [(i, (i + group) % band_count) for i in range(band_count)]
    peers = [rank ^ k for k in range(group)]

    fields = fields.transpose(1, 2, 0)

    waves = wave_table.reshape(2, group, slot_count // 2, 2)
    high_low = jnp.stack([waves.max(-1), waves.min(-1)], axis=-1)
    high_low = jnp.pad(high_low, ((0, 0), (0, 0), (0, pairs - slot_count // 2), (0, 0)))
    ordered = high_low.reshape(2, group, slot_pad)
    present = jnp.arange(slot_pad) < slot_count

    def by_peer(side):
        table = lax.dynamic_index_in_dim(ordered, side, 0, keepdims=False)
        return jnp.stack([lax.dynamic_index_in_dim(table, peer, 0, keepdims=False) for peer in peers])

    own_waves, far_waves = by_peer(half_index), by_peer(1 - half_index)
    own_low, far_low = own_waves[0, 1::2], far_waves[0, 1::2]
    lats = jnp.concatenate(
        [(half_index * group + peer) * lat_local + jnp.arange(lat_local, dtype=jnp.int32) for peer in peers]
    )

    def transform(source, waves_of, first, count, block_chunks):
        picked = waves_of[:, first * TILE : (first + count) * TILE].reshape(group * count, TILE)
        table = fourier_rows(picked, lon_count)
        if slot_pad != slot_count:
            mask = present[first * TILE : (first + count) * TILE].reshape(count, 1, TILE)
            mask = jnp.broadcast_to(mask, (group, count, 2, TILE)).reshape(-1, 1)
            table = table * mask.astype(jnp.bfloat16)
        return longitude_sums(source, table, block_chunks * 2 * TILE)

    def exchange(blocks):
        moved = [blocks[0]] + [None] * (group - 1)
        for k in [*range(group // 2, group), *range(1, group // 2)]:
            moved[k] = lax.ppermute(blocks[k], "band", [(i, i ^ k) for i in range(band_count)])
        return moved

    blocks = transform(fields, far_waves, 0, 1, 1)
    far = [exchange(blocks)]
    if chunks > 1:
        blocks = transform(after(fields, blocks[0]), far_waves, 1, chunks - 1, chunks - 1)
        far.append(exchange(blocks))
    far_table = packed_table(after(far_low, blocks[0]), lats, lat_count, degree_count, steps)

    others = []

    def send_sums(chunk, waited):
        low = far_low[chunk * TILE // 2 : (chunk + 1) * TILE // 2]
        sums = partial_sums(chunk, max(chunk - 1, 0), after(low, waited), far[min(chunk, 1)], far_table)
        sums = after(sums, others[-1]) if others else sums
        others.append([lax.ppermute(part, "band", mirror) for part in sums])
        return sums

    sums = send_sums(0, blocks[0])

    fields, own_waves, own_low, ar_coef, log_var = after((fields, own_waves, own_low, ar_coef, log_var), sums)
    blocks = transform(fields, own_waves, 0, chunks, 1)
    own_table = packed_table(after(own_low, blocks[0]), lats, lat_count, degree_count, steps)
    for chunk in range(1, chunks):
        send_sums(chunk, own_table)

    slot_waves = lax.dynamic_slice_in_dim(wave_table, band * slot_count, slot_count)
    pad_slots = (0, slot_pad - slot_count)
    kernel_waves = jnp.pad(slot_waves, pad_slots)
    is_low = kernel_waves == jnp.repeat(own_low, 2)
    shifts = jnp.where(is_low, 1, -kernel_waves)
    own_rows = jnp.stack([*split_rows(ar_coef), *split_rows(jnp.exp(-0.5 * log_var))], axis=1)
    own_rows = jnp.pad(own_rows, (pad_slots, (0, 4), (0, 0)))
    season = 1.0 + 0.5 * jnp.cos(day_of_year.astype(jnp.float32) * (2.0 * math.pi / 365.0))
    later = (jnp.arange(day_count) > 0).astype(jnp.float32)
    season_rows = jnp.pad(jnp.stack([lax.rsqrt(season), later / season]), ((0, 6), (0, 0)))

    own = [exchange(after(blocks[::chunks], (far[-1], others[0], own_table)))]
    innovation = None
    misc = []
    for chunk in range(chunks):
        if chunk + 1 < chunks:
            own.append(exchange(after(blocks[chunk + 1 :: chunks], (own[-1], misc[:chunk]))))
        low = own_low[chunk * TILE // 2 : (chunk + 1) * TILE // 2]
        span = slice(chunk * TILE, (chunk + 1) * TILE)
        innovation, rows = finish(
            chunk, low, kernel_waves[span], shifts[span], own[chunk], own_table, others[chunk],
            own_rows, season_rows, innovation, slot_pad,
        )
        misc.append(rows)
    innovation = innovation[:, :, :slot_count]
    misc = jnp.concatenate(misc, axis=0)[:slot_count, :6]

    degree_list = jnp.arange(degree_count, dtype=jnp.int32)
    valid_mask = (degree_list[None, :] >= slot_waves[:, None]).astype(jnp.float32)
    edges = misc.transpose(1, 0, 2)
    route = [(i, i + 1) for i in range(time_count - 1)]
    carried = lax.ppermute(edges[2:4].astype(jnp.bfloat16), "tm", route).astype(jnp.float32)
    scale = jnp.exp(-0.5 * log_var) * lax.rsqrt(season[0]) * valid_mask
    opening = ((edges[0:2] - ar_coef[None] * carried) * scale[None]).astype(jnp.bfloat16)
    innovation = lax.dynamic_update_slice_in_dim(innovation, opening[None], 0, 0)

    column_width = degree_count // time_count
    place = lax.axis_index("tm")
    columns = [misc[:, :, i * column_width : (i + 1) * column_width] for i in range(time_count)]
    moved = lax.all_to_all(jnp.stack(columns).astype(jnp.bfloat16), "tm", 0, 0, tiled=True).astype(jnp.float32)

    def own_columns(values):
        return lax.dynamic_slice_in_dim(values, place * column_width, column_width, 1)

    local_ar, local_var = own_columns(ar_coef), jnp.exp(-own_columns(log_var))
    first_days = day_of_year[0] + (jnp.arange(time_count, dtype=jnp.int32) - place) * day_count
    first_days = (first_days % 365).astype(jnp.float32)
    openness = 1.0 / (1.0 + 0.5 * jnp.cos(first_days * (2.0 * math.pi / 365.0)))
    first = moved[:, :, 0:2]
    before = jnp.concatenate([jnp.zeros_like(moved[:1, :, 2:4]), moved[:-1, :, 2:4]], axis=0)
    residual = first - local_ar[None, :, None] * before
    weighted = residual * openness[:, None, None, None]
    sum_coef = jnp.sum(moved[:, :, 4], axis=0) + jnp.sum(weighted * before, axis=(0, 2))
    sum_var = jnp.sum(moved[:, :, 5], axis=0) + jnp.sum(weighted * residual, axis=(0, 2))
    local_mask = own_columns(valid_mask)
    grad_coef = -local_mask * local_var * sum_coef / (2.0 * total_days)
    grad_var = local_mask * (total_days - 0.5 * local_var * sum_var) / (2.0 * total_days)
    return innovation, grad_coef, grad_var


def solution(mesh):
    in_specs = (P("tm", "band", None), P(), P("tm"), P("band", None), P("band", None))
    out_specs = (P("tm", None, "band", None), P("band", "tm"), P("band", "tm"))
    return jax.shard_map(
        per_device, mesh=mesh, in_specs=in_specs, out_specs=out_specs, check_vma=False
    )
```

```python
import functools
import math

import jax
import jax.numpy as jnp
from jax import lax
from jax.experimental import pallas as pl
from jax.experimental.pallas import tpu as pltpu
from jax.sharding import PartitionSpec as P

LANES = 128
TILE = 16
HALF = TILE // 4
VMEM_LIMIT = 56 * 1024 * 1024


def round_up(value, unit):
    return -(-value // unit) * unit


def fourier_kernel(coarse_cos_ref, coarse_sin_ref, fine_cos_ref, fine_sin_ref, out_ref):
    lon_count = out_ref.shape[1]
    fine_cos, fine_sin = fine_cos_ref[...], fine_sin_ref[...]
    for index in range(-(-lon_count // LANES)):
        width = min(LANES, lon_count - index * LANES)
        coarse_cos = coarse_cos_ref[:, index : index + 1]
        coarse_sin = coarse_sin_ref[:, index : index + 1]
        values = (coarse_cos * fine_cos - coarse_sin * fine_sin).astype(jnp.bfloat16)
        out_ref[:, index * LANES : index * LANES + width] = values[:, :width]


def fourier_rows(waves, lon_count):
    blocks, slots = waves.shape
    rows = blocks * 2 * slots

    def parts(step):
        lons = jnp.arange(LANES, dtype=jnp.int32) * step
        phase = waves[:, :, None] * lons % lon_count
        angle = phase.astype(jnp.float32) * (2.0 * math.pi / lon_count)
        return jnp.cos(angle), jnp.sin(angle)

    def both(first, second):
        return jnp.stack([first, second], axis=1).reshape(rows, LANES)

    coarse_cos, coarse_sin = parts(LANES)
    fine_cos, fine_sin = parts(1)
    return pl.pallas_call(
        fourier_kernel,
        out_shape=jax.ShapeDtypeStruct((rows, lon_count), jnp.bfloat16),
        compiler_params=pltpu.CompilerParams(vmem_limit_bytes=VMEM_LIMIT),
    )(
        both(coarse_cos, -coarse_sin),
        both(coarse_sin, coarse_cos),
        both(fine_cos, fine_cos),
        both(fine_sin, fine_sin),
    )


def transform_kernel(in_ref, table_ref, *out_refs):
    lats, _, days = in_ref.shape
    for lat in range(0, lats, 2):
        both = jnp.concatenate([in_ref[lat], in_ref[lat + 1]], axis=1)
        sums = jnp.dot(table_ref[...], both, preferred_element_type=jnp.float32).astype(jnp.bfloat16)
        begin = 0
        for out_ref in out_refs:
            piece = sums[begin : begin + out_ref.shape[1]]
            begin += out_ref.shape[1]
            out_ref[lat] = piece[:, :days]
            out_ref[lat + 1] = piece[:, days:]


def longitude_sums(fields, table, block_rows):
    lats, lon_count, days = fields.shape
    group = 8 if lats % 8 == 0 else 2
    rows = table.shape[0]
    blocks = rows // block_rows
    return pl.pallas_call(
        transform_kernel,
        grid=(lats // group,),
        in_specs=[
            pl.BlockSpec((group, lon_count, days), lambda i: (i, 0, 0)),
            pl.BlockSpec((rows, lon_count), lambda i: (0, 0)),
        ],
        out_specs=[pl.BlockSpec((group, block_rows, days), lambda i: (i, 0, 0))] * blocks,
        out_shape=[jax.ShapeDtypeStruct((lats, block_rows, days), jnp.bfloat16)] * blocks,
        compiler_params=pltpu.CompilerParams(vmem_limit_bytes=VMEM_LIMIT),
    )(fields, table)


def table_kernel(steps, lane_tiles, top, low_ref, first_ref, second_ref, cos_ref, weight_ref, out_ref, rows_ref, scale_ref):
    tiles = range(lane_tiles)
    low = low_ref[...]
    high = top - low
    low_next = low + 1.0
    lat_count = out_ref.shape[2]
    pairs = out_ref.shape[0]

    def lanes(ref, tile):
        return ref[:, tile * LANES : (tile + 1) * LANES]

    cosines = [lanes(cos_ref, t) for t in tiles]
    weights = [lanes(weight_ref, t) for t in tiles]
    second = [lanes(second_ref, t) for t in tiles]
    for t in tiles:
        half = jnp.exp(0.5 * second[t])
        scale_ref[2, :, t * LANES : (t + 1) * LANES] = half * weights[t]
        scale_ref[3, :, t * LANES : (t + 1) * LANES] = half

    def block(index, carry):
        current, lagged, scale, last_inverse = carry
        for t in tiles:
            largest = jnp.maximum(jnp.maximum(jnp.abs(current[t]), jnp.abs(lagged[t])), 1.0)
            current[t] = current[t] / largest
            lagged[t] = lagged[t] / largest
            scale[t] = scale[t] + jnp.log(largest)
            half = jnp.exp(0.5 * scale[t])
            scale_ref[0, :, t * LANES : (t + 1) * LANES] = half * weights[t]
            scale_ref[1, :, t * LANES : (t + 1) * LANES] = half
        begin = (index * TILE).astype(jnp.float32)
        for step in range(TILE):
            row = begin + float(step)
            after = low < row
            above = row - jnp.where(after, low_next, 0.0)
            order = jnp.where(after, low, high)
            degree = above + order
            spread = above * (degree + order)
            square = 4.0 * degree * degree - 1.0
            root = lax.rsqrt(jnp.maximum(square * spread, 1.0))
            factor = square * root
            inverse = spread * root
            fresh = above == 0.0
            for t in tiles:
                advanced = factor * (cosines[t] * current[t] - last_inverse * lagged[t])
                lagged[t] = current[t]
                current[t] = jnp.where(fresh, 1.0, advanced)
                rows_ref[t, pl.ds(step, pairs, stride=TILE), :] = current[t]
            last_inverse = inverse
        renewed = (low_next >= begin) & (low_next < begin + float(TILE))
        for t in tiles:
            scale[t] = jnp.where(renewed, second[t], scale[t])
        row_index = lax.broadcasted_iota(jnp.int32, (TILE, LANES), 0).astype(jnp.float32) + begin
        for pair in range(pairs):
            mark = low[pair : pair + 1, :]
            before = (row_index <= mark) | (mark + 1.0 < begin)
            for t in tiles:
                span = slice(t * LANES, min((t + 1) * LANES, lat_count))
                width = span.stop - span.start
                here = slice(t * LANES, (t + 1) * LANES)
                values = rows_ref[t, pair * TILE : (pair + 1) * TILE, :]
                one = jnp.where(before, scale_ref[0, pair : pair + 1, here], scale_ref[2, pair : pair + 1, here])
                two = jnp.where(before, scale_ref[1, pair : pair + 1, here], scale_ref[3, pair : pair + 1, here])
                values = (values * one * two).astype(jnp.bfloat16)
                out_ref[pair, pl.ds(pl.multiple_of(index * TILE, TILE), TILE), span] = values[:, :width]
        return current, lagged, scale, last_inverse

    zeros = jnp.zeros((pairs, LANES), jnp.float32)
    start = (
        [zeros for _ in tiles],
        [zeros for _ in tiles],
        [lanes(first_ref, t) for t in tiles],
        zeros,
    )
    lax.fori_loop(0, steps // TILE, block, start)


def packed_table(low_waves, lats, lat_count, degree_count, steps):
    pair_count = low_waves.shape[0]
    lat_half = lats.shape[0]
    lane_tiles = -(-lat_half // LANES)
    width = lane_tiles * LANES
    top = float(degree_count - 1)
    index = jnp.pad(lats, (0, width - lat_half), mode="edge")
    colatitude = (index.astype(jnp.float32) + 0.5) * (math.pi / lat_count)
    sines = jnp.sin(colatitude)
    log_sines = jnp.log(sines)
    low = low_waves.astype(jnp.float32)

    def log_start(order):
        base = 0.5 * (
            jnp.log(order + 0.5)
            + jax.scipy.special.gammaln(order + 0.5)
            - jax.scipy.special.gammaln(order + 1.0)
            - 0.5 * math.log(math.pi)
        )
        return base[:, None] + order[:, None] * log_sines[None, :]

    def spread(row):
        return jnp.broadcast_to(row[None, :], (pair_count, width))

    return pl.pallas_call(
        functools.partial(table_kernel, steps, lane_tiles, top),
        out_shape=jax.ShapeDtypeStruct((pair_count, steps, lat_half), jnp.bfloat16),
        scratch_shapes=[
            pltpu.VMEM((lane_tiles, pair_count * TILE, LANES), jnp.float32),
            pltpu.VMEM((4, pair_count, width), jnp.float32),
        ],
        compiler_params=pltpu.CompilerParams(vmem_limit_bytes=VMEM_LIMIT),
    )(
        jnp.broadcast_to(low[:, None], (pair_count, LANES)),
        log_start(top - low),
        log_start(low),
        spread(jnp.cos(colatitude)),
        spread(sines * (math.pi / lat_count)),
    )


def gather_slots(in_refs, flat_ref, slot_ref):
    lats, rows, days = in_refs[0].shape
    lat_half = len(in_refs) * lats
    for part in range(2):
        for source, in_ref in enumerate(in_refs):
            values = in_ref[:, part * TILE : (part + 1) * TILE, :].astype(jnp.float32)
            flat_ref[pl.ds(source * lats * TILE, lats * TILE), :] = values.reshape(lats * TILE, days)
        for slot in range(TILE):
            column = flat_ref[pl.ds(slot, lat_half, stride=TILE), :]
            slot_ref[slot, :, part * days : (part + 1) * days] = column.astype(jnp.bfloat16)


def pair_sum(pair, low, table_ref, slot_ref):
    table = table_ref[pair]
    high_sum = jnp.dot(table, slot_ref[2 * pair], preferred_element_type=jnp.float32)
    low_sum = jnp.dot(table, slot_ref[2 * pair + 1], preferred_element_type=jnp.float32)
    row = lax.broadcasted_iota(jnp.int32, high_sum.shape, 0)
    return jnp.where(row <= low, high_sum, low_sum)


def by_halves(one):
    def two(step, carry):
        one(0, step)
        one(1, step)
        return carry

    lax.fori_loop(0, HALF, two, 0)


def partial_kernel(degrees, low_ref, table_ref, *rest):
    *in_refs, first_ref, second_ref, flat_ref, slot_ref, last_ref = rest
    out_refs = (first_ref, second_ref)
    gather_slots(in_refs, flat_ref, slot_ref)
    last_ref[...] = jnp.zeros_like(last_ref)
    last_row = lax.broadcasted_iota(jnp.int32, last_ref.shape[1:], 0)

    def one(half, step):
        pair = half * HALF + step
        sums = pair_sum(pair, low_ref[pair], table_ref, slot_ref)
        begin = pl.multiple_of(step * degrees, TILE)
        out_refs[half][pl.ds(begin, degrees), :] = sums[:degrees].astype(jnp.bfloat16)
        last_ref[half] = jnp.where(last_row == step, sums[degrees : degrees + 1], last_ref[half])

    by_halves(one)
    for half in range(2):
        out_refs[half][HALF * degrees :, :] = last_ref[half].astype(jnp.bfloat16)


def pack_kernel(low_ref, in_ref, ar_ref, half_ref):
    pairs, _, width = in_ref.shape
    steps = ar_ref.shape[1]
    lane = lax.broadcasted_iota(jnp.int32, (1, width), 1)
    degrees = round_up(steps, LANES) - LANES

    def one(pair, carry):
        low = low_ref[pair]
        rows = in_ref[pair]
        high_rows = pltpu.roll(rows, width - (degrees - 1 - low), 1)
        low_rows = pltpu.roll(rows, 1, 1)
        for index, out_ref in enumerate((ar_ref, half_ref)):
            packed = jnp.where(
                lane <= low, high_rows[2 * index : 2 * index + 1], low_rows[2 * index + 1 : 2 * index + 2]
            )
            out_ref[pair] = jnp.broadcast_to(packed, (LANES, width)).T[:steps]
        return carry

    lax.fori_loop(0, pairs, one, 0)


def packed_columns(low, values, steps):
    pairs = values.shape[0]
    return pl.pallas_call(
        pack_kernel,
        in_specs=[pl.BlockSpec(memory_space=pltpu.SMEM), pl.BlockSpec(memory_space=pltpu.VMEM)],
        out_shape=[jax.ShapeDtypeStruct((pairs, steps, LANES), jnp.float32)] * 2,
        compiler_params=pltpu.CompilerParams(vmem_limit_bytes=VMEM_LIMIT),
    )(low, values)


def finish_kernel(sources, low_ref, swap_ref, table_ref, first_ref, second_ref, ar_ref, half_ref, season_ref, *rest):
    out_ref, misc_ref, flat_ref, slot_ref, turned_ref = rest[-5:]
    steps = table_ref.shape[1]
    days = out_ref.shape[0]
    degrees = out_ref.shape[3]
    lane_tiles = degrees // LANES
    width = degrees + LANES
    gather_slots(rest[:sources], flat_ref, slot_ref)
    lane = lax.broadcasted_iota(jnp.int32, (steps, LANES), 1)
    degree = lax.broadcasted_iota(jnp.int32, (2 * days + TILE, degrees), 1)
    last_row = lax.broadcasted_iota(jnp.int32, (TILE, 2 * days), 0)
    turn = (
        lax.broadcasted_iota(jnp.int32, (days, days), 0) == lax.broadcasted_iota(jnp.int32, (days, days), 1)
    ).astype(jnp.bfloat16)
    pick_row = lax.broadcasted_iota(jnp.int32, (TILE, LANES), 0)
    pick_lane = lax.broadcasted_iota(jnp.int32, (TILE, LANES), 1)
    pick = (pick_lane == jnp.where(pick_row < 8, pick_row, pick_row + (LANES // 2 - 8))).astype(jnp.bfloat16)
    transposed = (((1,), (1,)), ((), ()))
    other_refs = (first_ref, second_ref)

    def one(part_of, step):
        pair = part_of * HALF + step
        low = low_ref[pair]
        other_ref = other_refs[part_of]
        main = other_ref[pl.ds(pl.multiple_of(step * degrees, TILE), degrees), :].astype(jnp.float32)
        last = jnp.where(last_row == step, other_ref[HALF * degrees :, :].astype(jnp.float32), 0.0)
        last = jnp.where(last_row == 0, jnp.sum(last, axis=0, keepdims=True), 0.0)
        total = pair_sum(pair, low, table_ref, slot_ref) + jnp.concatenate([main, last], axis=0)
        ar = ar_ref[pair]
        half = half_ref[pair]
        turned = []
        shifted_parts = []
        sum_coef = jnp.zeros((steps, LANES), jnp.float32)
        sum_var = jnp.zeros((steps, LANES), jnp.float32)
        for part in range(2):
            spectral = total[:, part * days : (part + 1) * days]
            shifted = pltpu.roll(spectral, 1, 1)
            shifted_parts.append(shifted)
            previous = jnp.where(lane == 0, 0.0, shifted)
            residual = spectral - ar * previous
            innovation = (residual * season_ref[0:1, :] * half).astype(jnp.bfloat16)
            turned.append(
                lax.dot_general(turn, innovation, transposed, preferred_element_type=jnp.float32)
            )
            weighted = residual * season_ref[1:2, :]
            sum_coef = sum_coef + weighted * previous
            sum_var = sum_var + weighted * residual
        sum_coef = jnp.sum(sum_coef, axis=1, keepdims=True)
        sum_var = jnp.sum(sum_var, axis=1, keepdims=True)
        misc = jnp.where(
            lane < 2,
            shifted_parts[0],
            jnp.where(lane < 4, pltpu.roll(shifted_parts[1], 2, 1), jnp.where(lane == 4, sum_coef, sum_var)),
        )
        misc_high = misc.astype(jnp.bfloat16).astype(jnp.float32)
        misc_low = pltpu.roll(misc - misc_high, LANES // 2, 1)
        misc = jnp.where(lane < LANES // 2, misc_high, misc_low).astype(jnp.bfloat16)
        turned.append(lax.dot_general(pick, misc, transposed, preferred_element_type=jnp.float32))
        stacked = jnp.concatenate(turned, axis=0)
        stacked = jnp.concatenate(
            [stacked, jnp.zeros((stacked.shape[0], width - steps), jnp.float32)], axis=1
        )
        high = degrees - 1 - low
        swap = swap_ref[pair]
        for shift, first, slot in ((high, high, 2 * pair + swap), (width - 1, low, 2 * pair + 1 - swap)):
            placed = jnp.where(degree >= first, pltpu.roll(stacked, shift, 1)[:, :degrees], 0.0)
            for part in range(2):
                for t in range(lane_tiles):
                    turned_ref[part, t, pl.ds(slot, days, stride=TILE), :] = placed[
                        part * days : (part + 1) * days, t * LANES : (t + 1) * LANES
                    ]
            misc_ref[slot] = placed[2 * days : 2 * days + 8] + placed[2 * days + 8 :]

    by_halves(one)

    def write(day, carry):
        for part in range(2):
            for t in range(lane_tiles):
                values = turned_ref[part, t, pl.ds(pl.multiple_of(day * TILE, TILE), TILE), :]
                out_ref[day, part, :, t * LANES : (t + 1) * LANES] = values.astype(jnp.bfloat16)
        return carry

    lax.fori_loop(0, days, write, 0)


def leading(shape, chunk):
    return pl.BlockSpec(shape, lambda i: (chunk,) + (0,) * (len(shape) - 1))


def partial_sums(chunk, place, low, blocks, table, degrees):
    lats, rows, days = blocks[0].shape
    steps, lat_half = table.shape[1:]
    out_rows = HALF * degrees + TILE
    pairs = TILE // 2
    return pl.pallas_call(
        functools.partial(partial_kernel, degrees),
        grid=(1,),
        in_specs=[
            pl.BlockSpec(memory_space=pltpu.SMEM),
            leading((pairs, steps, lat_half), chunk),
        ]
        + [pl.BlockSpec((lats, 2 * TILE, days), lambda i: (0, place, 0)) for _ in blocks],
        out_specs=[leading((out_rows, 2 * days), 0)] * 2,
        out_shape=[jax.ShapeDtypeStruct((out_rows, 2 * days), jnp.bfloat16)] * 2,
        scratch_shapes=[
            pltpu.VMEM((lat_half * TILE, days), jnp.float32),
            pltpu.VMEM((TILE, lat_half, 2 * days), jnp.bfloat16),
            pltpu.VMEM((2, TILE, 2 * days), jnp.float32),
        ],
        compiler_params=pltpu.CompilerParams(vmem_limit_bytes=VMEM_LIMIT),
    )(low, table, *blocks)


def finish(chunk, low, swap, blocks, table, other, columns, season, held, slot_total, degrees):
    lats, rows, days = blocks[0].shape
    steps, lat_half = table.shape[1:]
    pairs = TILE // 2
    smem = pl.BlockSpec(memory_space=pltpu.SMEM)
    operands = [low, swap, table, *other, *columns, season, *blocks]
    in_specs = [
        smem,
        smem,
        leading((pairs, steps, lat_half), chunk),
        leading(other[0].shape, 0),
        leading(other[1].shape, 0),
        leading((pairs, steps, LANES), chunk),
        leading((pairs, steps, LANES), chunk),
        leading((8, LANES), 0),
    ] + [leading(block.shape, 0) for block in blocks]
    aliases = {}
    if held is not None:
        operands.append(held)
        in_specs.append(pl.BlockSpec(memory_space=pl.ANY))
        aliases = {len(operands) - 1: 0}
    return pl.pallas_call(
        functools.partial(finish_kernel, len(blocks)),
        grid=(1,),
        in_specs=in_specs,
        out_specs=[
            pl.BlockSpec((days, 2, TILE, degrees), lambda i: (0, 0, chunk, 0)),
            leading((TILE, 8, degrees), 0),
        ],
        out_shape=[
            jax.ShapeDtypeStruct((days, 2, slot_total, degrees), jnp.bfloat16),
            jax.ShapeDtypeStruct((TILE, 8, degrees), jnp.float32),
        ],
        input_output_aliases=aliases,
        scratch_shapes=[
            pltpu.VMEM((lat_half * TILE, days), jnp.float32),
            pltpu.VMEM((TILE, lat_half, 2 * days), jnp.bfloat16),
            pltpu.VMEM((2, degrees // LANES, days * TILE, LANES), jnp.float32),
        ],
        compiler_params=pltpu.CompilerParams(vmem_limit_bytes=VMEM_LIMIT),
    )(*operands)


def after(values, waited):
    return lax.optimization_barrier((values, waited))[0]


def per_device(fields, wave_table, day_of_year, ar_coef, log_var):
    band_count = lax.axis_size("band")
    time_count = lax.axis_size("tm")
    band = lax.axis_index("band")
    slot_count, degree_count = ar_coef.shape
    day_count, lat_local, lon_count = fields.shape
    lat_count = lat_local * band_count
    group = band_count // 2
    steps = round_up(degree_count + 1, TILE)
    total_days = day_count * time_count
    slot_pad = round_up(slot_count, TILE)
    chunks = slot_pad // TILE
    pairs = slot_pad // 2
    half_index = band // group
    rank = band % group
    mirror = [(i, (i + group) % band_count) for i in range(band_count)]
    peers = [rank ^ k for k in range(group)]

    fields = fields.transpose(1, 2, 0)

    waves = wave_table.reshape(2, group, slot_count // 2, 2)
    high_low = jnp.stack([waves.max(-1), waves.min(-1)], axis=-1)
    high_low = jnp.pad(high_low, ((0, 0), (0, 0), (0, pairs - slot_count // 2), (0, 0)))
    ordered = high_low.reshape(2, group, slot_pad)
    present = jnp.arange(slot_pad) < slot_count

    def by_peer(side):
        table = lax.dynamic_index_in_dim(ordered, side, 0, keepdims=False)
        return jnp.stack([lax.dynamic_index_in_dim(table, peer, 0, keepdims=False) for peer in peers])

    own_waves, far_waves = by_peer(half_index), by_peer(1 - half_index)
    own_low, far_low = own_waves[0, 1::2], far_waves[0, 1::2]
    lats = jnp.concatenate(
        [(half_index * group + peer) * lat_local + jnp.arange(lat_local, dtype=jnp.int32) for peer in peers]
    )

    def transform(source, waves_of, first, count, block_chunks):
        picked = waves_of[:, first * TILE : (first + count) * TILE].reshape(group * count, TILE)
        table = fourier_rows(picked, lon_count)
        if slot_pad != slot_count:
            mask = present[first * TILE : (first + count) * TILE].reshape(count, 1, TILE)
            mask = jnp.broadcast_to(mask, (group, count, 2, TILE)).reshape(-1, 1)
            table = table * mask.astype(jnp.bfloat16)
        return longitude_sums(source, table, block_chunks * 2 * TILE)

    across, along = list(range(group // 2, group)), list(range(1, group // 2))

    def exchange(blocks, order):
        moved = [blocks[0]] + [None] * (group - 1)
        for k in order:
            moved[k] = lax.ppermute(blocks[k], "band", [(i, i ^ k) for i in range(band_count)])
        return moved

    blocks = transform(fields, far_waves, 0, 1, 1)
    far = [exchange(blocks, across + along)]
    if chunks > 1:
        blocks = transform(after(fields, blocks[0]), far_waves, 1, chunks - 1, chunks - 1)
        far.append(exchange(blocks, across[:1] + along + across[1:]))
    far_table = packed_table(after(far_low, blocks[0]), lats, lat_count, degree_count, steps)

    others = []

    def send_sums(chunk, waited):
        low = far_low[chunk * TILE // 2 : (chunk + 1) * TILE // 2]
        sums = partial_sums(chunk, max(chunk - 1, 0), after(low, waited), far[min(chunk, 1)], far_table, degree_count)
        sums = after(sums, others[-1]) if others else sums
        others.append([lax.ppermute(part, "band", mirror) for part in sums])
        return sums

    sums = send_sums(0, blocks[0])

    fields, own_waves, own_low, ar_coef, log_var = after((fields, own_waves, own_low, ar_coef, log_var), sums)
    blocks = transform(fields, own_waves, 0, chunks, 1)
    own_table = packed_table(after(own_low, blocks[0]), lats, lat_count, degree_count, steps)
    for chunk in range(1, chunks):
        send_sums(chunk, own_table)

    slot_waves = lax.dynamic_slice_in_dim(wave_table, band * slot_count, slot_count)
    pad_slots = (0, slot_pad - slot_count)
    swap = (jnp.pad(slot_waves, pad_slots)[::2] == own_low).astype(jnp.int32)

    def by_pair(values):
        values = jnp.pad(values, (pad_slots, (0, LANES))).reshape(pairs, 2, degree_count + LANES)
        return jnp.where(swap[:, None, None] == 1, values[:, ::-1], values)

    values = jnp.concatenate([by_pair(ar_coef), by_pair(jnp.exp(-0.5 * log_var))], axis=1)
    columns = packed_columns(own_low, jnp.pad(values, ((0, 0), (0, 4), (0, 0))), steps)
    season = 1.0 + 0.5 * jnp.cos(day_of_year.astype(jnp.float32) * (2.0 * math.pi / 365.0))
    later = (jnp.arange(day_count) > 0).astype(jnp.float32)
    season_rows = jnp.pad(jnp.stack([lax.rsqrt(season), later / season]), ((0, 6), (0, 0)))

    own = [exchange(after(blocks[::chunks], (far[-1], own_table)), across + along)]
    innovation = None
    misc = []
    for chunk in range(chunks):
        if chunk + 1 < chunks:
            own.append(exchange(after(blocks[chunk + 1 :: chunks], (own[-1], misc[:chunk])), across + along))
        span = slice(chunk * TILE // 2, (chunk + 1) * TILE // 2)
        innovation, rows = finish(
            chunk, own_low[span], swap[span], own[chunk], own_table, others[chunk], columns, season_rows,
            innovation, slot_pad, degree_count,
        )
        misc.append(rows)
    innovation = innovation[:, :, :slot_count]
    misc = jnp.concatenate(misc, axis=0)[:slot_count, :6]

    degree_list = jnp.arange(degree_count, dtype=jnp.int32)
    valid_mask = (degree_list[None, :] >= slot_waves[:, None]).astype(jnp.float32)
    edges = misc.transpose(1, 0, 2)
    route = [(i, i + 1) for i in range(time_count - 1)]
    carried = lax.ppermute(edges[0:4:2].astype(jnp.bfloat16), "tm", route).astype(jnp.float32)
    scale = jnp.exp(-0.5 * log_var) * lax.rsqrt(season[0]) * valid_mask
    opening = ((edges[1:4:2] - ar_coef[None] * carried) * scale[None]).astype(jnp.bfloat16)
    innovation = lax.dynamic_update_slice_in_dim(innovation, opening[None], 0, 0)

    column_width = degree_count // time_count
    place = lax.axis_index("tm")
    columns = [misc[:, :, i * column_width : (i + 1) * column_width] for i in range(time_count)]
    moved = lax.all_to_all(jnp.stack(columns).astype(jnp.bfloat16), "tm", 0, 0, tiled=True).astype(jnp.float32)

    def own_columns(values):
        return lax.dynamic_slice_in_dim(values, place * column_width, column_width, 1)

    local_ar, local_var = own_columns(ar_coef), jnp.exp(-own_columns(log_var))
    first_days = day_of_year[0] + (jnp.arange(time_count, dtype=jnp.int32) - place) * day_count
    first_days = (first_days % 365).astype(jnp.float32)
    openness = 1.0 / (1.0 + 0.5 * jnp.cos(first_days * (2.0 * math.pi / 365.0)))
    first = moved[:, :, 1:4:2]
    before = jnp.concatenate([jnp.zeros_like(moved[:1, :, 0:4:2]), moved[:-1, :, 0:4:2]], axis=0)
    residual = first - local_ar[None, :, None] * before
    weighted = residual * openness[:, None, None, None]
    sum_coef = jnp.sum(moved[:, :, 4], axis=0) + jnp.sum(weighted * before, axis=(0, 2))
    sum_var = jnp.sum(moved[:, :, 5], axis=0) + jnp.sum(weighted * residual, axis=(0, 2))
    local_mask = own_columns(valid_mask)
    grad_coef = -local_mask * local_var * sum_coef / (2.0 * total_days)
    grad_var = local_mask * (total_days - 0.5 * local_var * sum_var) / (2.0 * total_days)
    return innovation, grad_coef, grad_var


def solution(mesh):
    in_specs = (P("tm", "band", None), P(), P("tm"), P("band", None), P("band", None))
    out_specs = (P("tm", None, "band", None), P("band", "tm"), P("band", "tm"))
    return jax.shard_map(
        per_device, mesh=mesh, in_specs=in_specs, out_specs=out_specs, check_vma=False
    )
```

```python
import functools
import math

import jax
import jax.numpy as jnp
from jax import lax
from jax.experimental import pallas as pl
from jax.experimental.pallas import tpu as pltpu
from jax.sharding import PartitionSpec as P

LANES = 128
TILE = 16
HALF = TILE // 4
ROWS = 80
DAY_ROWS = 32
VMEM_LIMIT = 56 * 1024 * 1024


def round_up(value, unit):
    return -(-value // unit) * unit


def fourier_kernel(coarse_cos_ref, coarse_sin_ref, fine_cos_ref, fine_sin_ref, out_ref):
    lon_count = out_ref.shape[1]
    fine_cos, fine_sin = fine_cos_ref[...], fine_sin_ref[...]
    for index in range(-(-lon_count // LANES)):
        width = min(LANES, lon_count - index * LANES)
        coarse_cos = coarse_cos_ref[:, index : index + 1]
        coarse_sin = coarse_sin_ref[:, index : index + 1]
        values = (coarse_cos * fine_cos - coarse_sin * fine_sin).astype(jnp.bfloat16)
        out_ref[:, index * LANES : index * LANES + width] = values[:, :width]


def fourier_rows(waves, lon_count):
    blocks, slots = waves.shape
    rows = blocks * 2 * slots

    def parts(step):
        lons = jnp.arange(LANES, dtype=jnp.int32) * step
        phase = waves[:, :, None] * lons % lon_count
        angle = phase.astype(jnp.float32) * (2.0 * math.pi / lon_count)
        return jnp.cos(angle), jnp.sin(angle)

    def both(first, second):
        return jnp.stack([first, second], axis=1).reshape(rows, LANES)

    coarse_cos, coarse_sin = parts(LANES)
    fine_cos, fine_sin = parts(1)
    return pl.pallas_call(
        fourier_kernel,
        out_shape=jax.ShapeDtypeStruct((rows, lon_count), jnp.bfloat16),
        compiler_params=pltpu.CompilerParams(vmem_limit_bytes=VMEM_LIMIT),
    )(
        both(coarse_cos, -coarse_sin),
        both(coarse_sin, coarse_cos),
        both(fine_cos, fine_cos),
        both(fine_sin, fine_sin),
    )


def transform_kernel(in_ref, table_ref, *out_refs):
    lats, _, days = in_ref.shape
    for lat in range(0, lats, 2):
        both = in_ref[lat]
        if lat + 1 < lats:
            both = jnp.concatenate([both, in_ref[lat + 1]], axis=1)
        sums = jnp.dot(table_ref[...], both, preferred_element_type=jnp.float32).astype(jnp.bfloat16)
        begin = 0
        for out_ref in out_refs:
            piece = sums[begin : begin + out_ref.shape[1]]
            begin += out_ref.shape[1]
            out_ref[lat] = piece[:, :days]
            if lat + 1 < lats:
                out_ref[lat + 1] = piece[:, days:]


def longitude_sums(fields, table, block_rows, share=(0, 1)):
    lats, lon_count, days = fields.shape
    lats = lats // share[1]
    group = 8 if lats % 8 == 0 else 4 if lats % 4 == 0 else 1
    skip = share[0] * lats // group
    rows = table.shape[0]
    blocks = rows // block_rows
    return pl.pallas_call(
        transform_kernel,
        grid=(lats // group,),
        in_specs=[
            pl.BlockSpec((group, lon_count, days), lambda i: (skip + i, 0, 0)),
            pl.BlockSpec((rows, lon_count), lambda i: (0, 0)),
        ],
        out_specs=[pl.BlockSpec((group, block_rows, days), lambda i: (i, 0, 0))] * blocks,
        out_shape=[jax.ShapeDtypeStruct((lats, block_rows, days), jnp.bfloat16)] * blocks,
        compiler_params=pltpu.CompilerParams(vmem_limit_bytes=VMEM_LIMIT),
    )(fields, table)


def table_kernel(steps, lane_tiles, top, low_ref, first_ref, second_ref, cos_ref, weight_ref, out_ref, rows_ref, scale_ref):
    tiles = range(lane_tiles)
    low = low_ref[...]
    high = top - low
    low_next = low + 1.0
    lat_count = out_ref.shape[2]
    pairs = out_ref.shape[0]

    def lanes(ref, tile):
        return ref[:, tile * LANES : (tile + 1) * LANES]

    cosines = [lanes(cos_ref, t) for t in tiles]
    weights = [lanes(weight_ref, t) for t in tiles]
    second = [lanes(second_ref, t) for t in tiles]
    for t in tiles:
        half = jnp.exp(0.5 * second[t])
        scale_ref[2, :, t * LANES : (t + 1) * LANES] = half * weights[t]
        scale_ref[3, :, t * LANES : (t + 1) * LANES] = half

    def block(index, carry):
        current, lagged, scale, last_inverse = carry
        for t in tiles:
            largest = jnp.maximum(jnp.maximum(jnp.abs(current[t]), jnp.abs(lagged[t])), 1.0)
            current[t] = current[t] / largest
            lagged[t] = lagged[t] / largest
            scale[t] = scale[t] + jnp.log(largest)
            half = jnp.exp(0.5 * scale[t])
            scale_ref[0, :, t * LANES : (t + 1) * LANES] = half * weights[t]
            scale_ref[1, :, t * LANES : (t + 1) * LANES] = half
        begin = (index * TILE).astype(jnp.float32)
        for step in range(TILE):
            row = begin + float(step)
            after = low < row
            above = row - jnp.where(after, low_next, 0.0)
            order = jnp.where(after, low, high)
            degree = above + order
            spread = above * (degree + order)
            square = 4.0 * degree * degree - 1.0
            root = lax.rsqrt(jnp.maximum(square * spread, 1.0))
            factor = square * root
            inverse = spread * root
            fresh = above == 0.0
            for t in tiles:
                advanced = factor * (cosines[t] * current[t] - last_inverse * lagged[t])
                lagged[t] = current[t]
                current[t] = jnp.where(fresh, 1.0, advanced)
                rows_ref[t, pl.ds(step, pairs, stride=TILE), :] = current[t]
            last_inverse = inverse
        renewed = (low_next >= begin) & (low_next < begin + float(TILE))
        for t in tiles:
            scale[t] = jnp.where(renewed, second[t], scale[t])
        row_index = lax.broadcasted_iota(jnp.int32, (TILE, LANES), 0).astype(jnp.float32) + begin
        for pair in range(pairs):
            mark = low[pair : pair + 1, :]
            before = (row_index <= mark) | (mark + 1.0 < begin)
            for t in tiles:
                span = slice(t * LANES, min((t + 1) * LANES, lat_count))
                width = span.stop - span.start
                here = slice(t * LANES, (t + 1) * LANES)
                values = rows_ref[t, pair * TILE : (pair + 1) * TILE, :]
                one = jnp.where(before, scale_ref[0, pair : pair + 1, here], scale_ref[2, pair : pair + 1, here])
                two = jnp.where(before, scale_ref[1, pair : pair + 1, here], scale_ref[3, pair : pair + 1, here])
                values = (values * one * two).astype(jnp.bfloat16)
                out_ref[pair, pl.ds(pl.multiple_of(index * TILE, TILE), TILE), span] = values[:, :width]
        return current, lagged, scale, last_inverse

    zeros = jnp.zeros((pairs, LANES), jnp.float32)
    start = (
        [zeros for _ in tiles],
        [zeros for _ in tiles],
        [lanes(first_ref, t) for t in tiles],
        zeros,
    )
    lax.fori_loop(0, steps // TILE, block, start)


def packed_table(low_waves, lats, lat_count, degree_count, steps):
    pair_count = low_waves.shape[0]
    lat_half = lats.shape[0]
    lane_tiles = -(-lat_half // LANES)
    width = lane_tiles * LANES
    top = float(degree_count - 1)
    index = jnp.pad(lats, (0, width - lat_half), mode="edge")
    colatitude = (index.astype(jnp.float32) + 0.5) * (math.pi / lat_count)
    sines = jnp.sin(colatitude)
    log_sines = jnp.log(sines)
    low = low_waves.astype(jnp.float32)

    def log_start(order):
        base = 0.5 * (
            jnp.log(order + 0.5)
            + jax.scipy.special.gammaln(order + 0.5)
            - jax.scipy.special.gammaln(order + 1.0)
            - 0.5 * math.log(math.pi)
        )
        return base[:, None] + order[:, None] * log_sines[None, :]

    def spread(row):
        return jnp.broadcast_to(row[None, :], (pair_count, width))

    return pl.pallas_call(
        functools.partial(table_kernel, steps, lane_tiles, top),
        out_shape=jax.ShapeDtypeStruct((pair_count, steps, lat_half), jnp.bfloat16),
        scratch_shapes=[
            pltpu.VMEM((lane_tiles, pair_count * TILE, LANES), jnp.float32),
            pltpu.VMEM((4, pair_count, width), jnp.float32),
        ],
        compiler_params=pltpu.CompilerParams(vmem_limit_bytes=VMEM_LIMIT),
    )(
        jnp.broadcast_to(low[:, None], (pair_count, LANES)),
        log_start(top - low),
        log_start(low),
        spread(jnp.cos(colatitude)),
        spread(sines * (math.pi / lat_count)),
    )


def gather_slots(in_refs, flat_ref, slot_ref):
    lats, rows, days = in_refs[0].shape
    lat_half = len(in_refs) * lats
    for part in range(2):
        for source, in_ref in enumerate(in_refs):
            values = in_ref[:, part * TILE : (part + 1) * TILE, :].astype(jnp.float32)
            flat_ref[pl.ds(source * lats * TILE, lats * TILE), :] = values.reshape(lats * TILE, days)
        for slot in range(TILE):
            column = flat_ref[pl.ds(slot, lat_half, stride=TILE), :]
            slot_ref[slot, :, part * days : (part + 1) * days] = column.astype(jnp.bfloat16)


def pair_sum(pair, low, table_ref, slot_ref):
    table = table_ref[pair]
    high_sum = jnp.dot(table, slot_ref[2 * pair], preferred_element_type=jnp.float32)
    low_sum = jnp.dot(table, slot_ref[2 * pair + 1], preferred_element_type=jnp.float32)
    row = lax.broadcasted_iota(jnp.int32, high_sum.shape, 0)
    return jnp.where(row <= low, high_sum, low_sum)


def by_halves(one):
    def two(step, carry):
        one(0, step)
        one(1, step)
        return carry

    lax.fori_loop(0, HALF, two, 0)


def partial_kernel(degrees, low_ref, table_ref, *rest):
    *in_refs, first_ref, second_ref, flat_ref, slot_ref, last_ref = rest
    out_refs = (first_ref, second_ref)
    gather_slots(in_refs, flat_ref, slot_ref)
    last_ref[...] = jnp.zeros_like(last_ref)
    last_row = lax.broadcasted_iota(jnp.int32, last_ref.shape[1:], 0)

    def one(half, step):
        pair = half * HALF + step
        sums = pair_sum(pair, low_ref[pair], table_ref, slot_ref)
        begin = pl.multiple_of(step * degrees, TILE)
        out_refs[half][pl.ds(begin, degrees), :] = sums[:degrees].astype(jnp.bfloat16)
        last_ref[half] = jnp.where(last_row == step, sums[degrees : degrees + 1], last_ref[half])

    by_halves(one)
    for half in range(2):
        out_refs[half][HALF * degrees :, :] = last_ref[half].astype(jnp.bfloat16)


def pack_kernel(low_ref, in_ref, ar_ref, half_ref):
    pairs, _, width = in_ref.shape
    steps = ar_ref.shape[1]
    lane = lax.broadcasted_iota(jnp.int32, (1, width), 1)
    degrees = round_up(steps, LANES) - LANES

    def one(pair, carry):
        low = low_ref[pair]
        rows = in_ref[pair]
        high_rows = pltpu.roll(rows, width - (degrees - 1 - low), 1)
        low_rows = pltpu.roll(rows, 1, 1)
        for index, out_ref in enumerate((ar_ref, half_ref)):
            packed = jnp.where(
                lane <= low, high_rows[2 * index : 2 * index + 1], low_rows[2 * index + 1 : 2 * index + 2]
            )
            out_ref[pair] = jnp.broadcast_to(packed, (LANES, width)).T[:steps]
        return carry

    lax.fori_loop(0, pairs, one, 0)


def packed_columns(low, values, steps):
    pairs = values.shape[0]
    return pl.pallas_call(
        pack_kernel,
        in_specs=[pl.BlockSpec(memory_space=pltpu.SMEM), pl.BlockSpec(memory_space=pltpu.VMEM)],
        out_shape=[jax.ShapeDtypeStruct((pairs, steps, LANES), jnp.float32)] * 2,
        compiler_params=pltpu.CompilerParams(vmem_limit_bytes=VMEM_LIMIT),
    )(low, values)


def finish_kernel(sources, low_ref, swap_ref, table_ref, first_ref, second_ref, ar_ref, half_ref, season_ref, *rest):
    out_ref, misc_ref, flat_ref, slot_ref, turned_ref, innovation_ref, stacked_ref = rest[-7:]
    steps = table_ref.shape[1]
    days = out_ref.shape[0]
    degrees = out_ref.shape[3]
    lane_tiles = degrees // LANES
    width = degrees + LANES
    gather_slots(rest[:sources], flat_ref, slot_ref)
    lane = lax.broadcasted_iota(jnp.int32, (ROWS, LANES), 1)
    degree = lax.broadcasted_iota(jnp.int32, (DAY_ROWS, degrees), 1)
    last_row = lax.broadcasted_iota(jnp.int32, (TILE, 2 * days), 0)
    turn = (
        lax.broadcasted_iota(jnp.int32, (days, days), 0) == lax.broadcasted_iota(jnp.int32, (days, days), 1)
    ).astype(jnp.bfloat16)
    pick_row = lax.broadcasted_iota(jnp.int32, (TILE, LANES), 0)
    pick_lane = lax.broadcasted_iota(jnp.int32, (TILE, LANES), 1)
    pick = (pick_lane == jnp.where(pick_row < 8, pick_row, pick_row + (LANES // 2 - 8))).astype(jnp.bfloat16)
    transposed = (((1,), (1,)), ((), ()))
    other_refs = (first_ref, second_ref)

    for half in range(2):
        stacked_ref[half, :, steps:] = jnp.zeros((2 * days + TILE, width - steps), jnp.float32)

    def one(part_of, step):
        pair = part_of * HALF + step
        low = low_ref[pair]
        other_ref = other_refs[part_of]
        begin = pl.multiple_of(step * degrees, TILE)
        last = jnp.where(last_row == step, other_ref[HALF * degrees :, :].astype(jnp.float32), 0.0)
        last = jnp.where(last_row == 0, jnp.sum(last, axis=0, keepdims=True), 0.0)
        table = table_ref[pair]
        high_sum = jnp.dot(table, slot_ref[2 * pair], preferred_element_type=jnp.float32)
        low_sum = jnp.dot(table, slot_ref[2 * pair + 1], preferred_element_type=jnp.float32)
        for first in range(0, steps, ROWS):
            here = slice(first, first + ROWS)
            row = lax.broadcasted_iota(jnp.int32, (ROWS, 2 * days), 0) + first
            own = jnp.where(row <= low, high_sum[here], low_sum[here])
            count = min(ROWS, degrees - first)
            other = other_ref[pl.ds(begin + first, count), :].astype(jnp.float32)
            if count < ROWS:
                other = jnp.concatenate([other, last], axis=0)
            total = own + other
            ar = ar_ref[pair, here]
            half = half_ref[pair, here]
            shifted_parts = []
            sum_coef = sum_var = 0.0
            for part in range(2):
                spectral = total[:, part * days : (part + 1) * days]
                shifted = pltpu.roll(spectral, 1, 1)
                shifted_parts.append(shifted)
                previous = jnp.where(lane == 0, 0.0, shifted)
                residual = spectral - ar * previous
                innovation_ref[part_of, part, here] = (residual * season_ref[0:1, :] * half).astype(jnp.bfloat16)
                weighted = residual * season_ref[1:2, :]
                sum_coef = sum_coef + weighted * previous
                sum_var = sum_var + weighted * residual
            sum_coef = jnp.sum(sum_coef, axis=1, keepdims=True)
            sum_var = jnp.sum(sum_var, axis=1, keepdims=True)
            misc = jnp.where(
                lane < 2,
                shifted_parts[0],
                jnp.where(lane < 4, pltpu.roll(shifted_parts[1], 2, 1), jnp.where(lane == 4, sum_coef, sum_var)),
            )
            misc_high = misc.astype(jnp.bfloat16).astype(jnp.float32)
            misc_low = pltpu.roll(misc - misc_high, LANES // 2, 1)
            misc = jnp.where(lane < LANES // 2, misc_high, misc_low)
            innovation_ref[part_of, 2, here] = misc.astype(jnp.bfloat16)
        for part in range(3):
            placer = turn if part < 2 else pick
            stacked_ref[part_of, part * days : part * days + placer.shape[0], :steps] = lax.dot_general(
                placer, innovation_ref[part_of, part], transposed, preferred_element_type=jnp.float32
            )
        high = degrees - 1 - low
        swap = swap_ref[pair]
        for shift, start, slot in ((high, high, 2 * pair + swap), (width - 1, low, 2 * pair + 1 - swap)):
            for first in range(0, 2 * days, DAY_ROWS):
                stacked = stacked_ref[part_of, first : first + DAY_ROWS, :]
                placed = jnp.where(degree >= start, pltpu.roll(stacked, shift, 1)[:, :degrees], 0.0)
                part, day = divmod(first, days)
                for t in range(lane_tiles):
                    turned_ref[part, t, pl.ds(day * TILE + slot, DAY_ROWS, stride=TILE), :] = placed[
                        :, t * LANES : (t + 1) * LANES
                    ]
            stacked = stacked_ref[part_of, 2 * days :, :]
            placed = jnp.where(degree[:TILE] >= start, pltpu.roll(stacked, shift, 1)[:, :degrees], 0.0)
            misc_ref[slot] = placed[:8] + placed[8:]

    by_halves(one)

    def write(day, carry):
        for part in range(2):
            for t in range(lane_tiles):
                values = turned_ref[part, t, pl.ds(pl.multiple_of(day * TILE, TILE), TILE), :]
                out_ref[day, part, :, t * LANES : (t + 1) * LANES] = values.astype(jnp.bfloat16)
        return carry

    lax.fori_loop(0, days, write, 0)


def leading(shape, chunk):
    return pl.BlockSpec(shape, lambda i: (chunk,) + (0,) * (len(shape) - 1))


def partial_sums(chunk, place, low, blocks, table, degrees):
    lats, rows, days = blocks[0].shape
    steps, lat_half = table.shape[1:]
    out_rows = HALF * degrees + TILE
    pairs = TILE // 2
    return pl.pallas_call(
        functools.partial(partial_kernel, degrees),
        grid=(1,),
        in_specs=[
            pl.BlockSpec(memory_space=pltpu.SMEM),
            leading((pairs, steps, lat_half), chunk),
        ]
        + [pl.BlockSpec((lats, 2 * TILE, days), lambda i: (0, place, 0)) for _ in blocks],
        out_specs=[leading((out_rows, 2 * days), 0)] * 2,
        out_shape=[jax.ShapeDtypeStruct((out_rows, 2 * days), jnp.bfloat16)] * 2,
        scratch_shapes=[
            pltpu.VMEM((lat_half * TILE, days), jnp.float32),
            pltpu.VMEM((TILE, lat_half, 2 * days), jnp.bfloat16),
            pltpu.VMEM((2, TILE, 2 * days), jnp.float32),
        ],
        compiler_params=pltpu.CompilerParams(vmem_limit_bytes=VMEM_LIMIT),
    )(low, table, *blocks)


def finish(chunk, low, swap, blocks, table, other, columns, season, held, slot_total, degrees):
    lats, rows, days = blocks[0].shape
    steps, lat_half = table.shape[1:]
    pairs = TILE // 2
    smem = pl.BlockSpec(memory_space=pltpu.SMEM)
    operands = [low, swap, table, *other, *columns, season, *blocks]
    in_specs = [
        smem,
        smem,
        leading((pairs, steps, lat_half), chunk),
        leading(other[0].shape, 0),
        leading(other[1].shape, 0),
        leading((pairs, steps, LANES), chunk),
        leading((pairs, steps, LANES), chunk),
        leading((8, LANES), 0),
    ] + [leading(block.shape, 0) for block in blocks]
    aliases = {}
    if held is not None:
        operands.append(held)
        in_specs.append(pl.BlockSpec(memory_space=pl.ANY))
        aliases = {len(operands) - 1: 0}
    return pl.pallas_call(
        functools.partial(finish_kernel, len(blocks)),
        grid=(1,),
        in_specs=in_specs,
        out_specs=[
            pl.BlockSpec((days, 2, TILE, degrees), lambda i: (0, 0, chunk, 0)),
            leading((TILE, 8, degrees), 0),
        ],
        out_shape=[
            jax.ShapeDtypeStruct((days, 2, slot_total, degrees), jnp.bfloat16),
            jax.ShapeDtypeStruct((TILE, 8, degrees), jnp.float32),
        ],
        input_output_aliases=aliases,
        scratch_shapes=[
            pltpu.VMEM((lat_half * TILE, days), jnp.float32),
            pltpu.VMEM((TILE, lat_half, 2 * days), jnp.bfloat16),
            pltpu.VMEM((2, degrees // LANES, days * TILE, LANES), jnp.float32),
            pltpu.VMEM((2, 3, steps, LANES), jnp.bfloat16),
            pltpu.VMEM((2, 2 * days + TILE, degrees + LANES), jnp.float32),
        ],
        compiler_params=pltpu.CompilerParams(vmem_limit_bytes=VMEM_LIMIT),
    )(*operands)


def after(values, waited):
    return lax.optimization_barrier((values, waited))[0]


def per_device(fields, wave_table, day_of_year, ar_coef, log_var):
    band_count = lax.axis_size("band")
    time_count = lax.axis_size("tm")
    band = lax.axis_index("band")
    slot_count, degree_count = ar_coef.shape
    day_count, lat_local, lon_count = fields.shape
    lat_count = lat_local * band_count
    group = band_count // 2
    steps = round_up(degree_count + 1, TILE)
    total_days = day_count * time_count
    slot_pad = round_up(slot_count, TILE)
    chunks = slot_pad // TILE
    pairs = slot_pad // 2
    half_index = band // group
    rank = band % group
    mirror = [(i, (i + group) % band_count) for i in range(band_count)]
    peers = [rank ^ k for k in range(group)]

    fields = fields.transpose(1, 2, 0)

    waves = wave_table.reshape(2, group, slot_count // 2, 2)
    high_low = jnp.stack([waves.max(-1), waves.min(-1)], axis=-1)
    high_low = jnp.pad(high_low, ((0, 0), (0, 0), (0, pairs - slot_count // 2), (0, 0)))
    ordered = high_low.reshape(2, group, slot_pad)
    present = jnp.arange(slot_pad) < slot_count

    def by_peer(side):
        table = lax.dynamic_index_in_dim(ordered, side, 0, keepdims=False)
        return jnp.stack([lax.dynamic_index_in_dim(table, peer, 0, keepdims=False) for peer in peers])

    own_waves, far_waves = by_peer(half_index), by_peer(1 - half_index)
    own_low, far_low = own_waves[0, 1::2], far_waves[0, 1::2]
    lats = jnp.concatenate(
        [(half_index * group + peer) * lat_local + jnp.arange(lat_local, dtype=jnp.int32) for peer in peers]
    )

    def table_of(waves_of, first, count):
        picked = waves_of[:, first * TILE : (first + count) * TILE].reshape(group * count, TILE)
        table = fourier_rows(picked, lon_count)
        if slot_pad != slot_count:
            mask = present[first * TILE : (first + count) * TILE].reshape(count, 1, TILE)
            mask = jnp.broadcast_to(mask, (group, count, 2, TILE)).reshape(-1, 1)
            table = table * mask.astype(jnp.bfloat16)
        return table

    across, along = list(range(group // 2, group)), list(range(1, group // 2))

    def exchange(blocks, order):
        moved = [blocks[0]] + [None] * (group - 1)
        for k in order:
            moved[k] = lax.ppermute(blocks[k], "band", [(i, i ^ k) for i in range(band_count)])
        return moved

    shares = 2 if lat_local % 2 == 0 else 1
    fourier = table_of(far_waves, 0, 1)
    first_blocks = []
    waited = fields
    for share in range(shares):
        first_blocks.append(longitude_sums(waited, fourier, 2 * TILE, (share, shares)))
        waited = after(fields, first_blocks[-1][0])
    moved = [exchange(blocks, across) for blocks in first_blocks]
    for share in range(shares):
        for k in along:
            moved[share][k] = exchange(first_blocks[share], [k])[k]
    far = [[moved[share][k] for k in range(group) for share in range(shares)]]
    blocks = first_blocks[-1]
    if chunks > 1:
        blocks = longitude_sums(waited, table_of(far_waves, 1, chunks - 1), (chunks - 1) * 2 * TILE)
        far.append(exchange(blocks, across[:1] + along + across[1:]))
    far_table = packed_table(after(far_low, blocks[0]), lats, lat_count, degree_count, steps)

    others = []

    def send_sums(chunk, waited):
        low = far_low[chunk * TILE // 2 : (chunk + 1) * TILE // 2]
        sums = partial_sums(chunk, max(chunk - 1, 0), after(low, waited), far[min(chunk, 1)], far_table, degree_count)
        sums = after(sums, others[-1]) if others else sums
        others.append([lax.ppermute(part, "band", mirror) for part in sums])
        return sums

    sums = send_sums(0, blocks[0])

    fields, own_waves, own_low, ar_coef, log_var = after((fields, own_waves, own_low, ar_coef, log_var), sums)
    blocks = longitude_sums(fields, table_of(own_waves, 0, chunks), 2 * TILE)
    own_table = packed_table(after(own_low, blocks[0]), lats, lat_count, degree_count, steps)
    for chunk in range(1, chunks):
        send_sums(chunk, own_table)

    slot_waves = lax.dynamic_slice_in_dim(wave_table, band * slot_count, slot_count)
    pad_slots = (0, slot_pad - slot_count)
    swap = (jnp.pad(slot_waves, pad_slots)[::2] == own_low).astype(jnp.int32)

    def by_pair(values):
        values = jnp.pad(values, (pad_slots, (0, LANES))).reshape(pairs, 2, degree_count + LANES)
        return jnp.where(swap[:, None, None] == 1, values[:, ::-1], values)

    values = jnp.concatenate([by_pair(ar_coef), by_pair(jnp.exp(-0.5 * log_var))], axis=1)
    columns = packed_columns(own_low, jnp.pad(values, ((0, 0), (0, 4), (0, 0))), steps)
    season = 1.0 + 0.5 * jnp.cos(day_of_year.astype(jnp.float32) * (2.0 * math.pi / 365.0))
    later = (jnp.arange(day_count) > 0).astype(jnp.float32)
    season_rows = jnp.pad(jnp.stack([lax.rsqrt(season), later / season]), ((0, 6), (0, 0)))

    own = [exchange(after(blocks[::chunks], (far[-1], own_table)), across + along)]
    innovation = None
    misc = []
    for chunk in range(chunks):
        if chunk + 1 < chunks:
            own.append(exchange(after(blocks[chunk + 1 :: chunks], (own[-1], misc[:chunk])), across + along))
        span = slice(chunk * TILE // 2, (chunk + 1) * TILE // 2)
        innovation, rows = finish(
            chunk, own_low[span], swap[span], own[chunk], own_table, others[chunk], columns, season_rows,
            innovation, slot_pad, degree_count,
        )
        misc.append(rows)
    innovation = innovation[:, :, :slot_count]
    misc = jnp.concatenate(misc, axis=0)[:slot_count, :6]

    degree_list = jnp.arange(degree_count, dtype=jnp.int32)
    valid_mask = (degree_list[None, :] >= slot_waves[:, None]).astype(jnp.float32)
    edges = misc.transpose(1, 0, 2)
    route = [(i, i + 1) for i in range(time_count - 1)]
    carried = lax.ppermute(edges[0:4:2].astype(jnp.bfloat16), "tm", route).astype(jnp.float32)
    scale = jnp.exp(-0.5 * log_var) * lax.rsqrt(season[0]) * valid_mask
    opening = ((edges[1:4:2] - ar_coef[None] * carried) * scale[None]).astype(jnp.bfloat16)
    innovation = lax.dynamic_update_slice_in_dim(innovation, opening[None], 0, 0)

    column_width = degree_count // time_count
    place = lax.axis_index("tm")
    columns = [misc[:, :, i * column_width : (i + 1) * column_width] for i in range(time_count)]
    moved = lax.all_to_all(jnp.stack(columns).astype(jnp.bfloat16), "tm", 0, 0, tiled=True).astype(jnp.float32)

    def own_columns(values):
        return lax.dynamic_slice_in_dim(values, place * column_width, column_width, 1)

    local_ar, local_var = own_columns(ar_coef), jnp.exp(-own_columns(log_var))
    first_days = day_of_year[0] + (jnp.arange(time_count, dtype=jnp.int32) - place) * day_count
    first_days = (first_days % 365).astype(jnp.float32)
    openness = 1.0 / (1.0 + 0.5 * jnp.cos(first_days * (2.0 * math.pi / 365.0)))
    first = moved[:, :, 1:4:2]
    before = jnp.concatenate([jnp.zeros_like(moved[:1, :, 0:4:2]), moved[:-1, :, 0:4:2]], axis=0)
    residual = first - local_ar[None, :, None] * before
    weighted = residual * openness[:, None, None, None]
    sum_coef = jnp.sum(moved[:, :, 4], axis=0) + jnp.sum(weighted * before, axis=(0, 2))
    sum_var = jnp.sum(moved[:, :, 5], axis=0) + jnp.sum(weighted * residual, axis=(0, 2))
    local_mask = own_columns(valid_mask)
    grad_coef = -local_mask * local_var * sum_coef / (2.0 * total_days)
    grad_var = local_mask * (total_days - 0.5 * local_var * sum_var) / (2.0 * total_days)
    return innovation, grad_coef, grad_var


def solution(mesh):
    in_specs = (P("tm", "band", None), P(), P("tm"), P("band", None), P("band", None))
    out_specs = (P("tm", None, "band", None), P("band", "tm"), P("band", "tm"))
    return jax.shard_map(
        per_device, mesh=mesh, in_specs=in_specs, out_specs=out_specs, check_vma=False
    )
```

```python
import functools
import math

import jax
import jax.numpy as jnp
from jax import lax
from jax.experimental import pallas as pl
from jax.experimental.pallas import tpu as pltpu
from jax.sharding import PartitionSpec as P

LANES = 128
TILE = 16
PITCH = TILE + 1
HALF = TILE // 4
ROWS = 80
DAY_ROWS = 32
VMEM_LIMIT = 56 * 1024 * 1024


def round_up(value, unit):
    return -(-value // unit) * unit


def fourier_kernel(coarse_cos_ref, coarse_sin_ref, fine_cos_ref, fine_sin_ref, out_ref):
    lon_count = out_ref.shape[1]
    fine_cos, fine_sin = fine_cos_ref[...], fine_sin_ref[...]
    for index in range(-(-lon_count // LANES)):
        width = min(LANES, lon_count - index * LANES)
        coarse_cos = coarse_cos_ref[:, index : index + 1]
        coarse_sin = coarse_sin_ref[:, index : index + 1]
        values = (coarse_cos * fine_cos - coarse_sin * fine_sin).astype(jnp.bfloat16)
        out_ref[:, index * LANES : index * LANES + width] = values[:, :width]


def fourier_rows(waves, lon_count):
    blocks, slots = waves.shape
    rows = blocks * 2 * slots

    def parts(step):
        lons = jnp.arange(LANES, dtype=jnp.int32) * step
        phase = waves[:, :, None] * lons % lon_count
        angle = phase.astype(jnp.float32) * (2.0 * math.pi / lon_count)
        return jnp.cos(angle), jnp.sin(angle)

    def both(first, second):
        return jnp.stack([first, second], axis=1).reshape(rows, LANES)

    coarse_cos, coarse_sin = parts(LANES)
    fine_cos, fine_sin = parts(1)
    return pl.pallas_call(
        fourier_kernel,
        out_shape=jax.ShapeDtypeStruct((rows, lon_count), jnp.bfloat16),
        compiler_params=pltpu.CompilerParams(vmem_limit_bytes=VMEM_LIMIT),
    )(
        both(coarse_cos, -coarse_sin),
        both(coarse_sin, coarse_cos),
        both(fine_cos, fine_cos),
        both(fine_sin, fine_sin),
    )


def transform_kernel(in_ref, table_ref, *out_refs):
    lats, _, days = in_ref.shape
    for lat in range(0, lats, 2):
        both = jnp.concatenate([in_ref[lat], in_ref[lat + 1]], axis=1)
        sums = jnp.dot(table_ref[...], both, preferred_element_type=jnp.float32).astype(jnp.bfloat16)
        begin = 0
        for out_ref in out_refs:
            piece = sums[begin : begin + out_ref.shape[1]]
            begin += out_ref.shape[1]
            out_ref[lat] = piece[:, :days]
            out_ref[lat + 1] = piece[:, days:]


def longitude_sums(fields, table, block_rows):
    lats, lon_count, days = fields.shape
    group = 8 if lats % 8 == 0 else 2
    rows = table.shape[0]
    blocks = rows // block_rows
    return pl.pallas_call(
        transform_kernel,
        grid=(lats // group,),
        in_specs=[
            pl.BlockSpec((group, lon_count, days), lambda i: (i, 0, 0)),
            pl.BlockSpec((rows, lon_count), lambda i: (0, 0)),
        ],
        out_specs=[pl.BlockSpec((group, block_rows, days), lambda i: (i, 0, 0))] * blocks,
        out_shape=[jax.ShapeDtypeStruct((lats, block_rows, days), jnp.bfloat16)] * blocks,
        compiler_params=pltpu.CompilerParams(vmem_limit_bytes=VMEM_LIMIT),
    )(fields, table)


def table_kernel(steps, lane_tiles, top, low_ref, first_ref, second_ref, cos_ref, weight_ref, out_ref, rows_ref, scale_ref):
    tiles = range(lane_tiles)
    low = low_ref[...]
    high = top - low
    low_next = low + 1.0
    lat_count = out_ref.shape[2]
    pairs = out_ref.shape[0]

    def lanes(ref, tile):
        return ref[:, tile * LANES : (tile + 1) * LANES]

    cosines = [lanes(cos_ref, t) for t in tiles]
    weights = [lanes(weight_ref, t) for t in tiles]
    second = [lanes(second_ref, t) for t in tiles]
    for t in tiles:
        half = jnp.exp(0.5 * second[t])
        scale_ref[2, :, t * LANES : (t + 1) * LANES] = half * weights[t]
        scale_ref[3, :, t * LANES : (t + 1) * LANES] = half

    def block(index, carry):
        current, lagged, scale, last_inverse = carry
        for t in tiles:
            largest = jnp.maximum(jnp.maximum(jnp.abs(current[t]), jnp.abs(lagged[t])), 1.0)
            current[t] = current[t] / largest
            lagged[t] = lagged[t] / largest
            scale[t] = scale[t] + jnp.log(largest)
            half = jnp.exp(0.5 * scale[t])
            scale_ref[0, :, t * LANES : (t + 1) * LANES] = half * weights[t]
            scale_ref[1, :, t * LANES : (t + 1) * LANES] = half
        begin = (index * TILE).astype(jnp.float32)
        for step in range(TILE):
            row = begin + float(step)
            after = low < row
            above = row - jnp.where(after, low_next, 0.0)
            order = jnp.where(after, low, high)
            degree = above + order
            spread = above * (degree + order)
            square = 4.0 * degree * degree - 1.0
            root = lax.rsqrt(jnp.maximum(square * spread, 1.0))
            factor = square * root
            inverse = spread * root
            fresh = above == 0.0
            for t in tiles:
                advanced = factor * (cosines[t] * current[t] - last_inverse * lagged[t])
                lagged[t] = current[t]
                current[t] = jnp.where(fresh, 1.0, advanced)
                rows_ref[t, pl.ds(step, pairs, stride=TILE), :] = current[t]
            last_inverse = inverse
        renewed = (low_next >= begin) & (low_next < begin + float(TILE))
        for t in tiles:
            scale[t] = jnp.where(renewed, second[t], scale[t])
        row_index = lax.broadcasted_iota(jnp.int32, (TILE, LANES), 0).astype(jnp.float32) + begin
        for pair in range(pairs):
            mark = low[pair : pair + 1, :]
            before = (row_index <= mark) | (mark + 1.0 < begin)
            for t in tiles:
                span = slice(t * LANES, min((t + 1) * LANES, lat_count))
                width = span.stop - span.start
                here = slice(t * LANES, (t + 1) * LANES)
                values = rows_ref[t, pair * TILE : (pair + 1) * TILE, :]
                one = jnp.where(before, scale_ref[0, pair : pair + 1, here], scale_ref[2, pair : pair + 1, here])
                two = jnp.where(before, scale_ref[1, pair : pair + 1, here], scale_ref[3, pair : pair + 1, here])
                values = (values * one * two).astype(jnp.bfloat16)
                out_ref[pair, pl.ds(pl.multiple_of(index * TILE, TILE), TILE), span] = values[:, :width]
        return current, lagged, scale, last_inverse

    zeros = jnp.zeros((pairs, LANES), jnp.float32)
    start = (
        [zeros for _ in tiles],
        [zeros for _ in tiles],
        [lanes(first_ref, t) for t in tiles],
        zeros,
    )
    lax.fori_loop(0, steps // TILE, block, start)


def packed_table(low_waves, lats, lat_count, degree_count, steps):
    pair_count = low_waves.shape[0]
    lat_half = lats.shape[0]
    lane_tiles = -(-lat_half // LANES)
    width = lane_tiles * LANES
    top = float(degree_count - 1)
    index = jnp.pad(lats, (0, width - lat_half), mode="edge")
    colatitude = (index.astype(jnp.float32) + 0.5) * (math.pi / lat_count)
    sines = jnp.sin(colatitude)
    log_sines = jnp.log(sines)
    low = low_waves.astype(jnp.float32)

    def log_start(order):
        base = 0.5 * (
            jnp.log(order + 0.5)
            + jax.scipy.special.gammaln(order + 0.5)
            - jax.scipy.special.gammaln(order + 1.0)
            - 0.5 * math.log(math.pi)
        )
        return base[:, None] + order[:, None] * log_sines[None, :]

    def spread(row):
        return jnp.broadcast_to(row[None, :], (pair_count, width))

    return pl.pallas_call(
        functools.partial(table_kernel, steps, lane_tiles, top),
        out_shape=jax.ShapeDtypeStruct((pair_count, steps, lat_half), jnp.bfloat16),
        scratch_shapes=[
            pltpu.VMEM((lane_tiles, pair_count * TILE, LANES), jnp.float32),
            pltpu.VMEM((4, pair_count, width), jnp.float32),
        ],
        compiler_params=pltpu.CompilerParams(vmem_limit_bytes=VMEM_LIMIT),
    )(
        jnp.broadcast_to(low[:, None], (pair_count, LANES)),
        log_start(top - low),
        log_start(low),
        spread(jnp.cos(colatitude)),
        spread(sines * (math.pi / lat_count)),
    )


def gather_slots(in_refs, flat_ref, slot_ref):
    lats, rows, days = in_refs[0].shape
    lat_half = len(in_refs) * lats
    step = 8 if lats % 8 == 0 else lats

    for part in range(2):
        for source, in_ref in enumerate(in_refs):

            def spread(index, carry, source=source, in_ref=in_ref, part=part):
                first = index * step
                values = in_ref[pl.ds(first, step), part * TILE : (part + 1) * TILE, :].astype(jnp.float32)
                begin = source * lats + first
                if step == 8:
                    window = flat_ref.at[pl.ds(pl.multiple_of(begin * PITCH, 8), 8 * PITCH)]
                else:
                    window = flat_ref.at[begin * PITCH : (begin + step) * PITCH]
                for lat in range(step):
                    window[lat * PITCH : lat * PITCH + TILE, :] = values[lat]
                return carry

            if step == 8:
                lax.fori_loop(0, lats // step, spread, 0)
            else:
                spread(0, 0)
        for slot in range(TILE):
            column = flat_ref[pl.ds(slot, lat_half, stride=PITCH), :]
            slot_ref[slot, :, part * days : (part + 1) * days] = column.astype(jnp.bfloat16)


def pair_sum(pair, low, table_ref, slot_ref):
    table = table_ref[pair]
    high_sum = jnp.dot(table, slot_ref[2 * pair], preferred_element_type=jnp.float32)
    low_sum = jnp.dot(table, slot_ref[2 * pair + 1], preferred_element_type=jnp.float32)
    row = lax.broadcasted_iota(jnp.int32, high_sum.shape, 0)
    return jnp.where(row <= low, high_sum, low_sum)


def by_halves(one):
    def two(step, carry):
        one(0, step)
        one(1, step)
        return carry

    lax.fori_loop(0, HALF, two, 0)


def partial_kernel(degrees, low_ref, table_ref, *rest):
    *in_refs, first_ref, second_ref, flat_ref, slot_ref, last_ref = rest
    out_refs = (first_ref, second_ref)
    gather_slots(in_refs, flat_ref, slot_ref)
    last_ref[...] = jnp.zeros_like(last_ref)
    last_row = lax.broadcasted_iota(jnp.int32, last_ref.shape[1:], 0)

    def one(half, step):
        pair = half * HALF + step
        sums = pair_sum(pair, low_ref[pair], table_ref, slot_ref)
        begin = pl.multiple_of(step * degrees, TILE)
        out_refs[half][pl.ds(begin, degrees), :] = sums[:degrees].astype(jnp.bfloat16)
        last_ref[half] = jnp.where(last_row == step, sums[degrees : degrees + 1], last_ref[half])

    by_halves(one)
    for half in range(2):
        out_refs[half][HALF * degrees :, :] = last_ref[half].astype(jnp.bfloat16)


def pack_kernel(low_ref, in_ref, ar_ref, half_ref):
    pairs, _, width = in_ref.shape
    steps = ar_ref.shape[1]
    lane = lax.broadcasted_iota(jnp.int32, (1, width), 1)
    degrees = round_up(steps, LANES) - LANES

    def one(pair, carry):
        low = low_ref[pair]
        rows = in_ref[pair]
        high_rows = pltpu.roll(rows, width - (degrees - 1 - low), 1)
        low_rows = pltpu.roll(rows, 1, 1)
        for index, out_ref in enumerate((ar_ref, half_ref)):
            packed = jnp.where(
                lane <= low, high_rows[2 * index : 2 * index + 1], low_rows[2 * index + 1 : 2 * index + 2]
            )
            out_ref[pair] = jnp.broadcast_to(packed, (LANES, width)).T[:steps]
        return carry

    lax.fori_loop(0, pairs, one, 0)


def packed_columns(low, values, steps):
    pairs = values.shape[0]
    return pl.pallas_call(
        pack_kernel,
        in_specs=[pl.BlockSpec(memory_space=pltpu.SMEM), pl.BlockSpec(memory_space=pltpu.VMEM)],
        out_shape=[jax.ShapeDtypeStruct((pairs, steps, LANES), jnp.float32)] * 2,
        compiler_params=pltpu.CompilerParams(vmem_limit_bytes=VMEM_LIMIT),
    )(low, values)


def finish_kernel(sources, low_ref, swap_ref, table_ref, first_ref, second_ref, ar_ref, half_ref, season_ref, *rest):
    out_ref, misc_ref, flat_ref, slot_ref, turned_ref, innovation_ref, stacked_ref = rest[-7:]
    steps = table_ref.shape[1]
    days = out_ref.shape[0]
    degrees = out_ref.shape[3]
    lane_tiles = degrees // LANES
    width = degrees + LANES
    gather_slots(rest[:sources], flat_ref, slot_ref)
    lane = lax.broadcasted_iota(jnp.int32, (ROWS, LANES), 1)
    degree = lax.broadcasted_iota(jnp.int32, (DAY_ROWS, degrees), 1)
    last_row = lax.broadcasted_iota(jnp.int32, (TILE, 2 * days), 0)
    turn = (
        lax.broadcasted_iota(jnp.int32, (days, days), 0) == lax.broadcasted_iota(jnp.int32, (days, days), 1)
    ).astype(jnp.bfloat16)
    pick_row = lax.broadcasted_iota(jnp.int32, (TILE, LANES), 0)
    pick_lane = lax.broadcasted_iota(jnp.int32, (TILE, LANES), 1)
    pick = (pick_lane == jnp.where(pick_row < 8, pick_row, pick_row + (LANES // 2 - 8))).astype(jnp.bfloat16)
    transposed = (((1,), (1,)), ((), ()))
    other_refs = (first_ref, second_ref)

    for half in range(2):
        stacked_ref[half, :, steps:] = jnp.zeros((2 * days + TILE, width - steps), jnp.float32)

    def one(part_of, step):
        pair = part_of * HALF + step
        low = low_ref[pair]
        other_ref = other_refs[part_of]
        begin = pl.multiple_of(step * degrees, TILE)
        last = jnp.where(last_row == step, other_ref[HALF * degrees :, :].astype(jnp.float32), 0.0)
        last = jnp.where(last_row == 0, jnp.sum(last, axis=0, keepdims=True), 0.0)
        table = table_ref[pair]
        high_sum = jnp.dot(table, slot_ref[2 * pair], preferred_element_type=jnp.float32)
        low_sum = jnp.dot(table, slot_ref[2 * pair + 1], preferred_element_type=jnp.float32)
        for first in range(0, steps, ROWS):
            here = slice(first, first + ROWS)
            row = lax.broadcasted_iota(jnp.int32, (ROWS, 2 * days), 0) + first
            own = jnp.where(row <= low, high_sum[here], low_sum[here])
            count = min(ROWS, degrees - first)
            other = other_ref[pl.ds(begin + first, count), :].astype(jnp.float32)
            if count < ROWS:
                other = jnp.concatenate([other, last], axis=0)
            total = own + other
            ar = ar_ref[pair, here]
            half = half_ref[pair, here]
            shifted_parts = []
            sum_coef = sum_var = 0.0
            for part in range(2):
                spectral = total[:, part * days : (part + 1) * days]
                shifted = pltpu.roll(spectral, 1, 1)
                shifted_parts.append(shifted)
                previous = jnp.where(lane == 0, 0.0, shifted)
                residual = spectral - ar * previous
                innovation_ref[part_of, part, here] = (residual * season_ref[0:1, :] * half).astype(jnp.bfloat16)
                weighted = residual * season_ref[1:2, :]
                sum_coef = sum_coef + weighted * previous
                sum_var = sum_var + weighted * residual
            sum_coef = jnp.sum(sum_coef, axis=1, keepdims=True)
            sum_var = jnp.sum(sum_var, axis=1, keepdims=True)
            misc = jnp.where(
                lane < 2,
                shifted_parts[0],
                jnp.where(lane < 4, pltpu.roll(shifted_parts[1], 2, 1), jnp.where(lane == 4, sum_coef, sum_var)),
            )
            misc_high = misc.astype(jnp.bfloat16).astype(jnp.float32)
            misc_low = pltpu.roll(misc - misc_high, LANES // 2, 1)
            misc = jnp.where(lane < LANES // 2, misc_high, misc_low)
            innovation_ref[part_of, 2, here] = misc.astype(jnp.bfloat16)
        for part in range(3):
            placer = turn if part < 2 else pick
            stacked_ref[part_of, part * days : part * days + placer.shape[0], :steps] = lax.dot_general(
                placer, innovation_ref[part_of, part], transposed, preferred_element_type=jnp.float32
            )
        high = degrees - 1 - low
        swap = swap_ref[pair]
        for shift, start, slot in ((high, high, 2 * pair + swap), (width - 1, low, 2 * pair + 1 - swap)):
            for first in range(0, 2 * days, DAY_ROWS):
                stacked = stacked_ref[part_of, first : first + DAY_ROWS, :]
                placed = jnp.where(degree >= start, pltpu.roll(stacked, shift, 1)[:, :degrees], 0.0)
                part, day = divmod(first, days)
                for t in range(lane_tiles):
                    turned_ref[part, t, pl.ds(day * PITCH + slot, DAY_ROWS, stride=PITCH), :] = placed[
                        :, t * LANES : (t + 1) * LANES
                    ]
            stacked = stacked_ref[part_of, 2 * days :, :]
            placed = jnp.where(degree[:TILE] >= start, pltpu.roll(stacked, shift, 1)[:, :degrees], 0.0)
            misc_ref[slot] = placed[:8] + placed[8:]

    by_halves(one)

    def write(step, carry):
        begin = pl.multiple_of(step * 8 * PITCH, 8)
        for part in range(2):
            for t in range(lane_tiles):
                window = turned_ref.at[part, t, pl.ds(begin, 8 * PITCH)]
                for day in range(8):
                    values = window[day * PITCH : day * PITCH + TILE, :]
                    out_ref[step * 8 + day, part, :, t * LANES : (t + 1) * LANES] = values.astype(jnp.bfloat16)
        return carry

    lax.fori_loop(0, days // 8, write, 0)


def leading(shape, chunk):
    return pl.BlockSpec(shape, lambda i: (chunk,) + (0,) * (len(shape) - 1))


def partial_sums(chunk, place, low, blocks, table, degrees):
    lats, rows, days = blocks[0].shape
    steps, lat_half = table.shape[1:]
    out_rows = HALF * degrees + TILE
    pairs = TILE // 2
    return pl.pallas_call(
        functools.partial(partial_kernel, degrees),
        grid=(1,),
        in_specs=[
            pl.BlockSpec(memory_space=pltpu.SMEM),
            leading((pairs, steps, lat_half), chunk),
        ]
        + [pl.BlockSpec((lats, 2 * TILE, days), lambda i: (0, place, 0)) for _ in blocks],
        out_specs=[leading((out_rows, 2 * days), 0)] * 2,
        out_shape=[jax.ShapeDtypeStruct((out_rows, 2 * days), jnp.bfloat16)] * 2,
        scratch_shapes=[
            pltpu.VMEM((lat_half * PITCH, days), jnp.float32),
            pltpu.VMEM((TILE, lat_half, 2 * days), jnp.bfloat16),
            pltpu.VMEM((2, TILE, 2 * days), jnp.float32),
        ],
        compiler_params=pltpu.CompilerParams(vmem_limit_bytes=VMEM_LIMIT),
    )(low, table, *blocks)


def finish(chunk, low, swap, blocks, table, other, columns, season, held, slot_total, degrees):
    lats, rows, days = blocks[0].shape
    steps, lat_half = table.shape[1:]
    pairs = TILE // 2
    smem = pl.BlockSpec(memory_space=pltpu.SMEM)
    operands = [low, swap, table, *other, *columns, season, *blocks]
    in_specs = [
        smem,
        smem,
        leading((pairs, steps, lat_half), chunk),
        leading(other[0].shape, 0),
        leading(other[1].shape, 0),
        leading((pairs, steps, LANES), chunk),
        leading((pairs, steps, LANES), chunk),
        leading((8, LANES), 0),
    ] + [leading(block.shape, 0) for block in blocks]
    aliases = {}
    if held is not None:
        operands.append(held)
        in_specs.append(pl.BlockSpec(memory_space=pl.ANY))
        aliases = {len(operands) - 1: 0}
    return pl.pallas_call(
        functools.partial(finish_kernel, len(blocks)),
        grid=(1,),
        in_specs=in_specs,
        out_specs=[
            pl.BlockSpec((days, 2, TILE, degrees), lambda i: (0, 0, chunk, 0)),
            leading((TILE, 8, degrees), 0),
        ],
        out_shape=[
            jax.ShapeDtypeStruct((days, 2, slot_total, degrees), jnp.bfloat16),
            jax.ShapeDtypeStruct((TILE, 8, degrees), jnp.float32),
        ],
        input_output_aliases=aliases,
        scratch_shapes=[
            pltpu.VMEM((lat_half * PITCH, days), jnp.float32),
            pltpu.VMEM((TILE, lat_half, 2 * days), jnp.bfloat16),
            pltpu.VMEM((2, degrees // LANES, days * PITCH, LANES), jnp.float32),
            pltpu.VMEM((2, 3, steps, LANES), jnp.bfloat16),
            pltpu.VMEM((2, 2 * days + TILE, degrees + LANES), jnp.float32),
        ],
        compiler_params=pltpu.CompilerParams(vmem_limit_bytes=VMEM_LIMIT),
    )(*operands)


def after(values, waited):
    return lax.optimization_barrier((values, waited))[0]


def per_device(fields, wave_table, day_of_year, ar_coef, log_var):
    band_count = lax.axis_size("band")
    time_count = lax.axis_size("tm")
    band = lax.axis_index("band")
    slot_count, degree_count = ar_coef.shape
    day_count, lat_local, lon_count = fields.shape
    lat_count = lat_local * band_count
    group = band_count // 2
    steps = round_up(degree_count + 1, TILE)
    total_days = day_count * time_count
    slot_pad = round_up(slot_count, TILE)
    chunks = slot_pad // TILE
    pairs = slot_pad // 2
    half_index = band // group
    rank = band % group
    mirror = [(i, (i + group) % band_count) for i in range(band_count)]
    peers = [rank ^ k for k in range(group)]

    fields = fields.transpose(1, 2, 0)

    waves = wave_table.reshape(2, group, slot_count // 2, 2)
    high_low = jnp.stack([waves.max(-1), waves.min(-1)], axis=-1)
    high_low = jnp.pad(high_low, ((0, 0), (0, 0), (0, pairs - slot_count // 2), (0, 0)))
    ordered = high_low.reshape(2, group, slot_pad)
    present = jnp.arange(slot_pad) < slot_count

    def by_peer(side):
        table = lax.dynamic_index_in_dim(ordered, side, 0, keepdims=False)
        return jnp.stack([lax.dynamic_index_in_dim(table, peer, 0, keepdims=False) for peer in peers])

    own_waves, far_waves = by_peer(half_index), by_peer(1 - half_index)
    own_low, far_low = own_waves[0, 1::2], far_waves[0, 1::2]
    lats = jnp.concatenate(
        [(half_index * group + peer) * lat_local + jnp.arange(lat_local, dtype=jnp.int32) for peer in peers]
    )

    def table_of(waves_of, first, count):
        picked = waves_of[:, first * TILE : (first + count) * TILE].reshape(group * count, TILE)
        table = fourier_rows(picked, lon_count)
        if slot_pad != slot_count:
            mask = present[first * TILE : (first + count) * TILE].reshape(count, 1, TILE)
            mask = jnp.broadcast_to(mask, (group, count, 2, TILE)).reshape(-1, 1)
            table = table * mask.astype(jnp.bfloat16)
        return table

    across, along = list(range(group // 2, group)), list(range(1, group // 2))

    def exchange(blocks, order):
        moved = [blocks[0]] + [None] * (group - 1)
        for k in order:
            moved[k] = lax.ppermute(blocks[k], "band", [(i, i ^ k) for i in range(band_count)])
        return moved

    blocks = longitude_sums(fields, table_of(far_waves, 0, 1), 2 * TILE)
    far = [exchange(blocks, across + along)]
    if chunks > 1:
        later = after(fields, blocks[0])
        blocks = longitude_sums(later, table_of(far_waves, 1, chunks - 1), (chunks - 1) * 2 * TILE)
        far.append(exchange(blocks, across[:1] + along + across[1:]))
    far_table = packed_table(after(far_low, blocks[0]), lats, lat_count, degree_count, steps)

    others = []

    def send_sums(chunk, waited):
        low = far_low[chunk * TILE // 2 : (chunk + 1) * TILE // 2]
        sums = partial_sums(chunk, max(chunk - 1, 0), after(low, waited), far[min(chunk, 1)], far_table, degree_count)
        sums = after(sums, others[-1]) if others else sums
        others.append([lax.ppermute(part, "band", mirror) for part in sums])
        return sums

    sums = send_sums(0, blocks[0])

    fields, own_waves, own_low, ar_coef, log_var = after((fields, own_waves, own_low, ar_coef, log_var), sums)
    blocks = longitude_sums(fields, table_of(own_waves, 0, chunks), 2 * TILE)
    own_table = packed_table(after(own_low, blocks[0]), lats, lat_count, degree_count, steps)
    slot_waves = lax.dynamic_slice_in_dim(wave_table, band * slot_count, slot_count)
    pad_slots = (0, slot_pad - slot_count)
    swap = (jnp.pad(slot_waves, pad_slots)[::2] == own_low).astype(jnp.int32)

    def by_pair(values):
        values = jnp.pad(values, (pad_slots, (0, LANES))).reshape(pairs, 2, degree_count + LANES)
        return jnp.where(swap[:, None, None] == 1, values[:, ::-1], values)

    values = jnp.concatenate([by_pair(ar_coef), by_pair(jnp.exp(-0.5 * log_var))], axis=1)
    columns = packed_columns(own_low, jnp.pad(values, ((0, 0), (0, 4), (0, 0))), steps)
    for chunk in range(1, chunks):
        send_sums(chunk, own_table if chunk == 1 else columns[0])

    season = 1.0 + 0.5 * jnp.cos(day_of_year.astype(jnp.float32) * (2.0 * math.pi / 365.0))
    later = (jnp.arange(day_count) > 0).astype(jnp.float32)
    season_rows = jnp.pad(jnp.stack([lax.rsqrt(season), later / season]), ((0, 6), (0, 0)))

    own = [exchange(after(blocks[::chunks], (far[-1], own_table)), across + along)]
    innovation = None
    misc = []
    for chunk in range(chunks):
        if chunk + 1 < chunks:
            own.append(exchange(after(blocks[chunk + 1 :: chunks], (own[-1], misc[:chunk])), across + along))
        span = slice(chunk * TILE // 2, (chunk + 1) * TILE // 2)
        innovation, rows = finish(
            chunk, own_low[span], swap[span], own[chunk], own_table, others[chunk], columns, season_rows,
            innovation, slot_pad, degree_count,
        )
        misc.append(rows)
    innovation = innovation[:, :, :slot_count]
    misc = jnp.concatenate(misc, axis=0)[:slot_count, :6]

    degree_list = jnp.arange(degree_count, dtype=jnp.int32)
    valid_mask = (degree_list[None, :] >= slot_waves[:, None]).astype(jnp.float32)
    edges = misc.transpose(1, 0, 2)
    route = [(i, i + 1) for i in range(time_count - 1)]
    carried = lax.ppermute(edges[0:4:2].astype(jnp.bfloat16), "tm", route).astype(jnp.float32)
    scale = jnp.exp(-0.5 * log_var) * lax.rsqrt(season[0]) * valid_mask
    opening = ((edges[1:4:2] - ar_coef[None] * carried) * scale[None]).astype(jnp.bfloat16)
    innovation = lax.dynamic_update_slice_in_dim(innovation, opening[None], 0, 0)

    column_width = degree_count // time_count
    place = lax.axis_index("tm")
    columns = [misc[:, :, i * column_width : (i + 1) * column_width] for i in range(time_count)]
    moved = lax.all_to_all(jnp.stack(columns).astype(jnp.bfloat16), "tm", 0, 0, tiled=True).astype(jnp.float32)

    def own_columns(values):
        return lax.dynamic_slice_in_dim(values, place * column_width, column_width, 1)

    local_ar, local_var = own_columns(ar_coef), jnp.exp(-own_columns(log_var))
    first_days = day_of_year[0] + (jnp.arange(time_count, dtype=jnp.int32) - place) * day_count
    first_days = (first_days % 365).astype(jnp.float32)
    openness = 1.0 / (1.0 + 0.5 * jnp.cos(first_days * (2.0 * math.pi / 365.0)))
    first = moved[:, :, 1:4:2]
    before = jnp.concatenate([jnp.zeros_like(moved[:1, :, 0:4:2]), moved[:-1, :, 0:4:2]], axis=0)
    residual = first - local_ar[None, :, None] * before
    weighted = residual * openness[:, None, None, None]
    sum_coef = jnp.sum(moved[:, :, 4], axis=0) + jnp.sum(weighted * before, axis=(0, 2))
    sum_var = jnp.sum(moved[:, :, 5], axis=0) + jnp.sum(weighted * residual, axis=(0, 2))
    local_mask = own_columns(valid_mask)
    grad_coef = -local_mask * local_var * sum_coef / (2.0 * total_days)
    grad_var = local_mask * (total_days - 0.5 * local_var * sum_var) / (2.0 * total_days)
    return innovation, grad_coef, grad_var


def solution(mesh):
    in_specs = (P("tm", "band", None), P(), P("tm"), P("band", None), P("band", None))
    out_specs = (P("tm", None, "band", None), P("band", "tm"), P("band", "tm"))
    return jax.shard_map(
        per_device, mesh=mesh, in_specs=in_specs, out_specs=out_specs, check_vma=False
    )
```

```python
import functools
import math

import jax
import jax.numpy as jnp
from jax import lax
from jax.experimental import pallas as pl
from jax.experimental.pallas import tpu as pltpu
from jax.sharding import PartitionSpec as P

LANES = 128
TILE = 16
PITCH = TILE + 1
HALF = TILE // 4
ROWS = 80
DAY_ROWS = 32
VMEM_LIMIT = 56 * 1024 * 1024


def round_up(value, unit):
    return -(-value // unit) * unit


def fourier_kernel(coarse_cos_ref, coarse_sin_ref, fine_cos_ref, fine_sin_ref, out_ref):
    lon_count = out_ref.shape[1]
    fine_cos, fine_sin = fine_cos_ref[...], fine_sin_ref[...]
    for index in range(-(-lon_count // LANES)):
        width = min(LANES, lon_count - index * LANES)
        coarse_cos = coarse_cos_ref[:, index : index + 1]
        coarse_sin = coarse_sin_ref[:, index : index + 1]
        values = (coarse_cos * fine_cos - coarse_sin * fine_sin).astype(jnp.bfloat16)
        out_ref[:, index * LANES : index * LANES + width] = values[:, :width]


def fourier_rows(waves, lon_count):
    blocks, slots = waves.shape
    rows = blocks * 2 * slots

    def parts(step):
        lons = jnp.arange(LANES, dtype=jnp.int32) * step
        phase = waves[:, :, None] * lons % lon_count
        angle = phase.astype(jnp.float32) * (2.0 * math.pi / lon_count)
        return jnp.cos(angle), jnp.sin(angle)

    def both(first, second):
        return jnp.stack([first, second], axis=1).reshape(rows, LANES)

    coarse_cos, coarse_sin = parts(LANES)
    fine_cos, fine_sin = parts(1)
    return pl.pallas_call(
        fourier_kernel,
        out_shape=jax.ShapeDtypeStruct((rows, lon_count), jnp.bfloat16),
        compiler_params=pltpu.CompilerParams(vmem_limit_bytes=VMEM_LIMIT),
    )(
        both(coarse_cos, -coarse_sin),
        both(coarse_sin, coarse_cos),
        both(fine_cos, fine_cos),
        both(fine_sin, fine_sin),
    )


def transform_kernel(in_ref, table_ref, *out_refs):
    lats, _, days = in_ref.shape
    for lat in range(0, lats, 2):
        both = jnp.concatenate([in_ref[lat], in_ref[lat + 1]], axis=1)
        sums = jnp.dot(table_ref[...], both, preferred_element_type=jnp.float32).astype(jnp.bfloat16)
        begin = 0
        for out_ref in out_refs:
            piece = sums[begin : begin + out_ref.shape[1]]
            begin += out_ref.shape[1]
            out_ref[lat] = piece[:, :days]
            out_ref[lat + 1] = piece[:, days:]


def longitude_sums(fields, table, block_rows):
    lats, lon_count, days = fields.shape
    group = 8 if lats % 8 == 0 else 2
    rows = table.shape[0]
    blocks = rows // block_rows
    return pl.pallas_call(
        transform_kernel,
        grid=(lats // group,),
        in_specs=[
            pl.BlockSpec((group, lon_count, days), lambda i: (i, 0, 0)),
            pl.BlockSpec((rows, lon_count), lambda i: (0, 0)),
        ],
        out_specs=[pl.BlockSpec((group, block_rows, days), lambda i: (i, 0, 0))] * blocks,
        out_shape=[jax.ShapeDtypeStruct((lats, block_rows, days), jnp.bfloat16)] * blocks,
        compiler_params=pltpu.CompilerParams(vmem_limit_bytes=VMEM_LIMIT),
    )(fields, table)


def table_kernel(steps, lane_tiles, top, low_ref, first_ref, second_ref, cos_ref, weight_ref, out_ref, rows_ref, scale_ref):
    tiles = range(lane_tiles)
    low = low_ref[...]
    high = top - low
    low_next = low + 1.0
    lat_count = out_ref.shape[2]
    pairs = out_ref.shape[0]

    def lanes(ref, tile):
        return ref[:, tile * LANES : (tile + 1) * LANES]

    cosines = [lanes(cos_ref, t) for t in tiles]
    weights = [lanes(weight_ref, t) for t in tiles]
    second = [lanes(second_ref, t) for t in tiles]
    for t in tiles:
        half = jnp.exp(0.5 * second[t])
        scale_ref[2, :, t * LANES : (t + 1) * LANES] = half * weights[t]
        scale_ref[3, :, t * LANES : (t + 1) * LANES] = half

    def block(index, carry):
        current, lagged, scale, last_inverse = carry
        for t in tiles:
            largest = jnp.maximum(jnp.maximum(jnp.abs(current[t]), jnp.abs(lagged[t])), 1.0)
            current[t] = current[t] / largest
            lagged[t] = lagged[t] / largest
            scale[t] = scale[t] + jnp.log(largest)
            half = jnp.exp(0.5 * scale[t])
            scale_ref[0, :, t * LANES : (t + 1) * LANES] = half * weights[t]
            scale_ref[1, :, t * LANES : (t + 1) * LANES] = half
        begin = (index * TILE).astype(jnp.float32)
        for step in range(TILE):
            row = begin + float(step)
            after = low < row
            above = row - jnp.where(after, low_next, 0.0)
            order = jnp.where(after, low, high)
            degree = above + order
            spread = above * (degree + order)
            square = 4.0 * degree * degree - 1.0
            root = lax.rsqrt(jnp.maximum(square * spread, 1.0))
            factor = square * root
            inverse = spread * root
            fresh = above == 0.0
            for t in tiles:
                advanced = factor * (cosines[t] * current[t] - last_inverse * lagged[t])
                lagged[t] = current[t]
                current[t] = jnp.where(fresh, 1.0, advanced)
                rows_ref[t, pl.ds(step, pairs, stride=TILE), :] = current[t]
            last_inverse = inverse
        renewed = (low_next >= begin) & (low_next < begin + float(TILE))
        for t in tiles:
            scale[t] = jnp.where(renewed, second[t], scale[t])
        row_index = lax.broadcasted_iota(jnp.int32, (TILE, LANES), 0).astype(jnp.float32) + begin
        for pair in range(pairs):
            mark = low[pair : pair + 1, :]
            before = (row_index <= mark) | (mark + 1.0 < begin)
            for t in tiles:
                span = slice(t * LANES, min((t + 1) * LANES, lat_count))
                width = span.stop - span.start
                here = slice(t * LANES, (t + 1) * LANES)
                values = rows_ref[t, pair * TILE : (pair + 1) * TILE, :]
                one = jnp.where(before, scale_ref[0, pair : pair + 1, here], scale_ref[2, pair : pair + 1, here])
                two = jnp.where(before, scale_ref[1, pair : pair + 1, here], scale_ref[3, pair : pair + 1, here])
                values = (values * one * two).astype(jnp.bfloat16)
                out_ref[pair, pl.ds(pl.multiple_of(index * TILE, TILE), TILE), span] = values[:, :width]
        return current, lagged, scale, last_inverse

    zeros = jnp.zeros((pairs, LANES), jnp.float32)
    start = (
        [zeros for _ in tiles],
        [zeros for _ in tiles],
        [lanes(first_ref, t) for t in tiles],
        zeros,
    )
    lax.fori_loop(0, steps // TILE, block, start)


def packed_table(low_waves, lats, lat_count, degree_count, steps):
    pair_count = low_waves.shape[0]
    lat_half = lats.shape[0]
    lane_tiles = -(-lat_half // LANES)
    width = lane_tiles * LANES
    top = float(degree_count - 1)
    index = jnp.pad(lats, (0, width - lat_half), mode="edge")
    colatitude = (index.astype(jnp.float32) + 0.5) * (math.pi / lat_count)
    sines = jnp.sin(colatitude)
    log_sines = jnp.log(sines)
    low = low_waves.astype(jnp.float32)

    def log_start(order):
        base = 0.5 * (
            jnp.log(order + 0.5)
            + jax.scipy.special.gammaln(order + 0.5)
            - jax.scipy.special.gammaln(order + 1.0)
            - 0.5 * math.log(math.pi)
        )
        return base[:, None] + order[:, None] * log_sines[None, :]

    def spread(row):
        return jnp.broadcast_to(row[None, :], (pair_count, width))

    return pl.pallas_call(
        functools.partial(table_kernel, steps, lane_tiles, top),
        out_shape=jax.ShapeDtypeStruct((pair_count, steps, lat_half), jnp.bfloat16),
        scratch_shapes=[
            pltpu.VMEM((lane_tiles, pair_count * TILE, LANES), jnp.float32),
            pltpu.VMEM((4, pair_count, width), jnp.float32),
        ],
        compiler_params=pltpu.CompilerParams(vmem_limit_bytes=VMEM_LIMIT),
    )(
        jnp.broadcast_to(low[:, None], (pair_count, LANES)),
        log_start(top - low),
        log_start(low),
        spread(jnp.cos(colatitude)),
        spread(sines * (math.pi / lat_count)),
    )


def gather_slots(in_refs, flat_ref, slot_ref):
    lats, rows, days = in_refs[0].shape
    lat_half = len(in_refs) * lats
    step = 8 if lats % 8 == 0 else lats

    for part in range(2):
        for source, in_ref in enumerate(in_refs):

            def spread(index, carry, source=source, in_ref=in_ref, part=part):
                first = index * step
                values = in_ref[pl.ds(first, step), part * TILE : (part + 1) * TILE, :].astype(jnp.float32)
                begin = source * lats + first
                if step == 8:
                    window = flat_ref.at[pl.ds(pl.multiple_of(begin * PITCH, 8), 8 * PITCH)]
                else:
                    window = flat_ref.at[begin * PITCH : (begin + step) * PITCH]
                for lat in range(step):
                    window[lat * PITCH : lat * PITCH + TILE, :] = values[lat]
                return carry

            if step == 8:
                lax.fori_loop(0, lats // step, spread, 0)
            else:
                spread(0, 0)
        for slot in range(TILE):
            column = flat_ref[pl.ds(slot, lat_half, stride=PITCH), :]
            slot_ref[slot, :, part * days : (part + 1) * days] = column.astype(jnp.bfloat16)


def pair_sum(pair, low, table_ref, slot_ref):
    table = table_ref[pair]
    high_sum = jnp.dot(table, slot_ref[2 * pair], preferred_element_type=jnp.float32)
    low_sum = jnp.dot(table, slot_ref[2 * pair + 1], preferred_element_type=jnp.float32)
    row = lax.broadcasted_iota(jnp.int32, high_sum.shape, 0)
    return jnp.where(row <= low, high_sum, low_sum)


def by_halves(one):
    def two(step, carry):
        one(0, step)
        one(1, step)
        return carry

    lax.fori_loop(0, HALF, two, 0)


def partial_kernel(degrees, low_ref, table_ref, *rest):
    *in_refs, first_ref, second_ref, flat_ref, slot_ref, last_ref = rest
    out_refs = (first_ref, second_ref)
    gather_slots(in_refs, flat_ref, slot_ref)
    last_ref[...] = jnp.zeros_like(last_ref)
    last_row = lax.broadcasted_iota(jnp.int32, last_ref.shape[1:], 0)

    def one(half, step):
        pair = half * HALF + step
        sums = pair_sum(pair, low_ref[pair], table_ref, slot_ref)
        begin = pl.multiple_of(step * degrees, TILE)
        out_refs[half][pl.ds(begin, degrees), :] = sums[:degrees].astype(jnp.bfloat16)
        last_ref[half] = jnp.where(last_row == step, sums[degrees : degrees + 1], last_ref[half])

    by_halves(one)
    for half in range(2):
        out_refs[half][HALF * degrees :, :] = last_ref[half].astype(jnp.bfloat16)


def pack_kernel(low_ref, in_ref, ar_ref, half_ref):
    pairs, _, width = in_ref.shape
    steps = ar_ref.shape[1]
    lane = lax.broadcasted_iota(jnp.int32, (1, width), 1)
    degrees = round_up(steps, LANES) - LANES

    def one(pair, carry):
        low = low_ref[pair]
        rows = in_ref[pair]
        high_rows = pltpu.roll(rows, width - (degrees - 1 - low), 1)
        low_rows = pltpu.roll(rows, 1, 1)
        for index, out_ref in enumerate((ar_ref, half_ref)):
            packed = jnp.where(
                lane <= low, high_rows[2 * index : 2 * index + 1], low_rows[2 * index + 1 : 2 * index + 2]
            )
            out_ref[pair] = jnp.broadcast_to(packed, (LANES, width)).T[:steps]
        return carry

    lax.fori_loop(0, pairs, one, 0)


def packed_columns(low, values, steps):
    pairs = values.shape[0]
    return pl.pallas_call(
        pack_kernel,
        in_specs=[pl.BlockSpec(memory_space=pltpu.SMEM), pl.BlockSpec(memory_space=pltpu.VMEM)],
        out_shape=[jax.ShapeDtypeStruct((pairs, steps, LANES), jnp.float32)] * 2,
        compiler_params=pltpu.CompilerParams(vmem_limit_bytes=VMEM_LIMIT),
    )(low, values)


def finish_kernel(sources, low_ref, swap_ref, table_ref, first_ref, second_ref, ar_ref, half_ref, season_ref, *rest):
    out_ref, misc_ref, flat_ref, slot_ref, turned_ref, innovation_ref, stacked_ref = rest[-7:]
    steps = table_ref.shape[1]
    days = out_ref.shape[0]
    degrees = out_ref.shape[3]
    lane_tiles = degrees // LANES
    width = degrees + LANES
    gather_slots(rest[:sources], flat_ref, slot_ref)
    lane = lax.broadcasted_iota(jnp.int32, (ROWS, LANES), 1)
    degree = lax.broadcasted_iota(jnp.int32, (DAY_ROWS, degrees), 1)
    last_row = lax.broadcasted_iota(jnp.int32, (TILE, 2 * days), 0)
    turn = (
        lax.broadcasted_iota(jnp.int32, (days, days), 0) == lax.broadcasted_iota(jnp.int32, (days, days), 1)
    ).astype(jnp.bfloat16)
    pick_row = lax.broadcasted_iota(jnp.int32, (TILE, LANES), 0)
    pick_lane = lax.broadcasted_iota(jnp.int32, (TILE, LANES), 1)
    pick = (pick_lane == jnp.where(pick_row < 8, pick_row, pick_row + (LANES // 2 - 8))).astype(jnp.bfloat16)
    transposed = (((1,), (1,)), ((), ()))
    other_refs = (first_ref, second_ref)

    for half in range(2):
        stacked_ref[half, :, steps:] = jnp.zeros((2 * days + TILE, width - steps), jnp.float32)

    def one(part_of, step):
        pair = part_of * HALF + step
        low = low_ref[pair]
        other_ref = other_refs[part_of]
        begin = pl.multiple_of(step * degrees, TILE)
        last = jnp.where(last_row == step, other_ref[HALF * degrees :, :].astype(jnp.float32), 0.0)
        last = jnp.where(last_row == 0, jnp.sum(last, axis=0, keepdims=True), 0.0)
        table = table_ref[pair]
        high_sum = jnp.dot(table, slot_ref[2 * pair], preferred_element_type=jnp.float32)
        low_sum = jnp.dot(table, slot_ref[2 * pair + 1], preferred_element_type=jnp.float32)
        for first in range(0, steps, ROWS):
            here = slice(first, first + ROWS)
            row = lax.broadcasted_iota(jnp.int32, (ROWS, 2 * days), 0) + first
            own = jnp.where(row <= low, high_sum[here], low_sum[here])
            count = min(ROWS, degrees - first)
            other = other_ref[pl.ds(begin + first, count), :].astype(jnp.float32)
            if count < ROWS:
                other = jnp.concatenate([other, last], axis=0)
            total = own + other
            ar = ar_ref[pair, here]
            half = half_ref[pair, here]
            shifted_parts = []
            sum_coef = sum_var = 0.0
            for part in range(2):
                spectral = total[:, part * days : (part + 1) * days]
                shifted = pltpu.roll(spectral, 1, 1)
                shifted_parts.append(shifted)
                previous = jnp.where(lane == 0, 0.0, shifted)
                residual = spectral - ar * previous
                innovation_ref[part_of, part, here] = (residual * season_ref[0:1, :] * half).astype(jnp.bfloat16)
                weighted = residual * season_ref[1:2, :]
                sum_coef = sum_coef + weighted * previous
                sum_var = sum_var + weighted * residual
            sum_coef = jnp.sum(sum_coef, axis=1, keepdims=True)
            sum_var = jnp.sum(sum_var, axis=1, keepdims=True)
            misc = jnp.where(
                lane < 2,
                shifted_parts[0],
                jnp.where(lane < 4, pltpu.roll(shifted_parts[1], 2, 1), jnp.where(lane == 4, sum_coef, sum_var)),
            )
            misc_high = misc.astype(jnp.bfloat16).astype(jnp.float32)
            misc_low = pltpu.roll(misc - misc_high, LANES // 2, 1)
            misc = jnp.where(lane < LANES // 2, misc_high, misc_low)
            innovation_ref[part_of, 2, here] = misc.astype(jnp.bfloat16)
        for part in range(3):
            placer = turn if part < 2 else pick
            stacked_ref[part_of, part * days : part * days + placer.shape[0], :steps] = lax.dot_general(
                placer, innovation_ref[part_of, part], transposed, preferred_element_type=jnp.float32
            )
        high = degrees - 1 - low
        swap = swap_ref[pair]
        for shift, start, slot in ((high, high, 2 * pair + swap), (width - 1, low, 2 * pair + 1 - swap)):
            for first in range(0, 2 * days, DAY_ROWS):
                stacked = stacked_ref[part_of, first : first + DAY_ROWS, :]
                placed = jnp.where(degree >= start, pltpu.roll(stacked, shift, 1)[:, :degrees], 0.0)
                part, day = divmod(first, days)
                for t in range(lane_tiles):
                    turned_ref[part, t, pl.ds(day * PITCH + slot, DAY_ROWS, stride=PITCH), :] = placed[
                        :, t * LANES : (t + 1) * LANES
                    ]
            stacked = stacked_ref[part_of, 2 * days :, :]
            placed = jnp.where(degree[:TILE] >= start, pltpu.roll(stacked, shift, 1)[:, :degrees], 0.0)
            misc_ref[slot] = placed[:8] + placed[8:]

    by_halves(one)

    def write(step, carry):
        begin = pl.multiple_of(step * 8 * PITCH, 8)
        for part in range(2):
            for t in range(lane_tiles):
                window = turned_ref.at[part, t, pl.ds(begin, 8 * PITCH)]
                for day in range(8):
                    values = window[day * PITCH : day * PITCH + TILE, :]
                    out_ref[step * 8 + day, part, :, t * LANES : (t + 1) * LANES] = values.astype(jnp.bfloat16)
        return carry

    lax.fori_loop(0, days // 8, write, 0)


def leading(shape, chunk):
    return pl.BlockSpec(shape, lambda i: (chunk,) + (0,) * (len(shape) - 1))


def partial_sums(chunk, place, low, blocks, table, degrees):
    lats, rows, days = blocks[0].shape
    steps, lat_half = table.shape[1:]
    out_rows = HALF * degrees + TILE
    pairs = TILE // 2
    return pl.pallas_call(
        functools.partial(partial_kernel, degrees),
        grid=(1,),
        in_specs=[
            pl.BlockSpec(memory_space=pltpu.SMEM),
            leading((pairs, steps, lat_half), chunk),
        ]
        + [pl.BlockSpec((lats, 2 * TILE, days), lambda i: (0, place, 0)) for _ in blocks],
        out_specs=[leading((out_rows, 2 * days), 0)] * 2,
        out_shape=[jax.ShapeDtypeStruct((out_rows, 2 * days), jnp.bfloat16)] * 2,
        scratch_shapes=[
            pltpu.VMEM((lat_half * PITCH, days), jnp.float32),
            pltpu.VMEM((TILE, lat_half, 2 * days), jnp.bfloat16),
            pltpu.VMEM((2, TILE, 2 * days), jnp.float32),
        ],
        compiler_params=pltpu.CompilerParams(vmem_limit_bytes=VMEM_LIMIT),
    )(low, table, *blocks)


def finish(chunk, low, swap, blocks, table, other, columns, season, held, slot_total, degrees):
    lats, rows, days = blocks[0].shape
    steps, lat_half = table.shape[1:]
    pairs = TILE // 2
    smem = pl.BlockSpec(memory_space=pltpu.SMEM)
    operands = [low, swap, table, *other, *columns, season, *blocks]
    in_specs = [
        smem,
        smem,
        leading((pairs, steps, lat_half), chunk),
        leading(other[0].shape, 0),
        leading(other[1].shape, 0),
        leading((pairs, steps, LANES), chunk),
        leading((pairs, steps, LANES), chunk),
        leading((8, LANES), 0),
    ] + [leading(block.shape, 0) for block in blocks]
    aliases = {}
    if held is not None:
        operands.append(held)
        in_specs.append(pl.BlockSpec(memory_space=pl.ANY))
        aliases = {len(operands) - 1: 0}
    return pl.pallas_call(
        functools.partial(finish_kernel, len(blocks)),
        grid=(1,),
        in_specs=in_specs,
        out_specs=[
            pl.BlockSpec((days, 2, TILE, degrees), lambda i: (0, 0, chunk, 0)),
            leading((TILE, 8, degrees), 0),
        ],
        out_shape=[
            jax.ShapeDtypeStruct((days, 2, slot_total, degrees), jnp.bfloat16),
            jax.ShapeDtypeStruct((TILE, 8, degrees), jnp.float32),
        ],
        input_output_aliases=aliases,
        scratch_shapes=[
            pltpu.VMEM((lat_half * PITCH, days), jnp.float32),
            pltpu.VMEM((TILE, lat_half, 2 * days), jnp.bfloat16),
            pltpu.VMEM((2, degrees // LANES, days * PITCH, LANES), jnp.float32),
            pltpu.VMEM((2, 3, steps, LANES), jnp.bfloat16),
            pltpu.VMEM((2, 2 * days + TILE, degrees + LANES), jnp.float32),
        ],
        compiler_params=pltpu.CompilerParams(vmem_limit_bytes=VMEM_LIMIT),
    )(*operands)


def after(values, waited):
    return lax.optimization_barrier((values, waited))[0]


def per_device(fields, wave_table, day_of_year, ar_coef, log_var):
    band_count = lax.axis_size("band")
    time_count = lax.axis_size("tm")
    band = lax.axis_index("band")
    slot_count, degree_count = ar_coef.shape
    day_count, lat_local, lon_count = fields.shape
    lat_count = lat_local * band_count
    group = band_count // 2
    steps = round_up(degree_count + 1, TILE)
    total_days = day_count * time_count
    slot_pad = round_up(slot_count, TILE)
    chunks = slot_pad // TILE
    pairs = slot_pad // 2
    half_index = band // group
    rank = band % group
    mirror = [(i, (i + group) % band_count) for i in range(band_count)]
    peers = [rank ^ k for k in range(group)]

    fields = fields.transpose(1, 2, 0)

    waves = wave_table.reshape(2, group, slot_count // 2, 2)
    high_low = jnp.stack([waves.max(-1), waves.min(-1)], axis=-1)
    high_low = jnp.pad(high_low, ((0, 0), (0, 0), (0, pairs - slot_count // 2), (0, 0)))
    ordered = high_low.reshape(2, group, slot_pad)
    present = jnp.arange(slot_pad) < slot_count

    def by_peer(side):
        table = lax.dynamic_index_in_dim(ordered, side, 0, keepdims=False)
        return jnp.stack([lax.dynamic_index_in_dim(table, peer, 0, keepdims=False) for peer in peers])

    own_waves, far_waves = by_peer(half_index), by_peer(1 - half_index)
    own_low, far_low = own_waves[0, 1::2], far_waves[0, 1::2]
    lats = jnp.concatenate(
        [(half_index * group + peer) * lat_local + jnp.arange(lat_local, dtype=jnp.int32) for peer in peers]
    )

    def table_of(waves_of, first, count):
        picked = waves_of[:, first * TILE : (first + count) * TILE].reshape(group * count, TILE)
        table = fourier_rows(picked, lon_count)
        if slot_pad != slot_count:
            mask = present[first * TILE : (first + count) * TILE].reshape(count, 1, TILE)
            mask = jnp.broadcast_to(mask, (group, count, 2, TILE)).reshape(-1, 1)
            table = table * mask.astype(jnp.bfloat16)
        return table

    across = list(range(group // 2, group))
    order = across[:0:-1] + list(range(1, group // 2)) + across[:1]

    def exchange(blocks, order):
        moved = [blocks[0]] + [None] * (group - 1)
        for k in order:
            moved[k] = lax.ppermute(blocks[k], "band", [(i, i ^ k) for i in range(band_count)])
        return moved

    blocks = longitude_sums(fields, table_of(far_waves, 0, 1), 2 * TILE)
    far = [exchange(blocks, order)]
    if chunks > 1:
        later = after(fields, blocks[0])
        blocks = longitude_sums(later, table_of(far_waves, 1, chunks - 1), (chunks - 1) * 2 * TILE)
        far.append(exchange(blocks, order))
    far_table = packed_table(after(far_low, blocks[0]), lats, lat_count, degree_count, steps)

    others = []

    def send_sums(chunk, waited):
        low = far_low[chunk * TILE // 2 : (chunk + 1) * TILE // 2]
        sums = partial_sums(chunk, max(chunk - 1, 0), after(low, waited), far[min(chunk, 1)], far_table, degree_count)
        sums = after(sums, others[-1]) if others else sums
        others.append([lax.ppermute(part, "band", mirror) for part in sums])
        return sums

    sums = send_sums(0, blocks[0])

    fields, own_waves, own_low, ar_coef, log_var = after((fields, own_waves, own_low, ar_coef, log_var), sums)
    blocks = longitude_sums(fields, table_of(own_waves, 0, chunks), 2 * TILE)
    own_table = packed_table(after(own_low, blocks[0]), lats, lat_count, degree_count, steps)
    slot_waves = lax.dynamic_slice_in_dim(wave_table, band * slot_count, slot_count)
    pad_slots = (0, slot_pad - slot_count)
    swap = (jnp.pad(slot_waves, pad_slots)[::2] == own_low).astype(jnp.int32)

    def by_pair(values):
        values = jnp.pad(values, (pad_slots, (0, LANES))).reshape(pairs, 2, degree_count + LANES)
        return jnp.where(swap[:, None, None] == 1, values[:, ::-1], values)

    values = jnp.concatenate([by_pair(ar_coef), by_pair(jnp.exp(-0.5 * log_var))], axis=1)
    columns = packed_columns(own_low, jnp.pad(values, ((0, 0), (0, 4), (0, 0))), steps)
    for chunk in range(1, chunks):
        send_sums(chunk, own_table if chunk == 1 else columns[0])

    season = 1.0 + 0.5 * jnp.cos(day_of_year.astype(jnp.float32) * (2.0 * math.pi / 365.0))
    later = (jnp.arange(day_count) > 0).astype(jnp.float32)
    season_rows = jnp.pad(jnp.stack([lax.rsqrt(season), later / season]), ((0, 6), (0, 0)))

    own = [exchange(after(blocks[::chunks], ([far[-1][k] for k in across], own_table)), order)]
    innovation = None
    misc = []
    for chunk in range(chunks):
        if chunk + 1 < chunks:
            crossed = own[-1]
            own.append(exchange(after(blocks[chunk + 1 :: chunks], (crossed, misc[:chunk])), order))
        span = slice(chunk * TILE // 2, (chunk + 1) * TILE // 2)
        innovation, rows = finish(
            chunk, own_low[span], swap[span], own[chunk], own_table, others[chunk], columns, season_rows,
            innovation, slot_pad, degree_count,
        )
        misc.append(rows)
    innovation = innovation[:, :, :slot_count]
    misc = jnp.concatenate(misc, axis=0)[:slot_count, :6]

    degree_list = jnp.arange(degree_count, dtype=jnp.int32)
    valid_mask = (degree_list[None, :] >= slot_waves[:, None]).astype(jnp.float32)
    edges = misc.transpose(1, 0, 2)
    route = [(i, i + 1) for i in range(time_count - 1)]
    carried = lax.ppermute(edges[0:4:2].astype(jnp.bfloat16), "tm", route).astype(jnp.float32)
    scale = jnp.exp(-0.5 * log_var) * lax.rsqrt(season[0]) * valid_mask
    opening = ((edges[1:4:2] - ar_coef[None] * carried) * scale[None]).astype(jnp.bfloat16)
    innovation = lax.dynamic_update_slice_in_dim(innovation, opening[None], 0, 0)

    column_width = degree_count // time_count
    place = lax.axis_index("tm")
    columns = [misc[:, :, i * column_width : (i + 1) * column_width] for i in range(time_count)]
    moved = lax.all_to_all(jnp.stack(columns).astype(jnp.bfloat16), "tm", 0, 0, tiled=True).astype(jnp.float32)

    def own_columns(values):
        return lax.dynamic_slice_in_dim(values, place * column_width, column_width, 1)

    local_ar, local_var = own_columns(ar_coef), jnp.exp(-own_columns(log_var))
    first_days = day_of_year[0] + (jnp.arange(time_count, dtype=jnp.int32) - place) * day_count
    first_days = (first_days % 365).astype(jnp.float32)
    openness = 1.0 / (1.0 + 0.5 * jnp.cos(first_days * (2.0 * math.pi / 365.0)))
    first = moved[:, :, 1:4:2]
    before = jnp.concatenate([jnp.zeros_like(moved[:1, :, 0:4:2]), moved[:-1, :, 0:4:2]], axis=0)
    residual = first - local_ar[None, :, None] * before
    weighted = residual * openness[:, None, None, None]
    sum_coef = jnp.sum(moved[:, :, 4], axis=0) + jnp.sum(weighted * before, axis=(0, 2))
    sum_var = jnp.sum(moved[:, :, 5], axis=0) + jnp.sum(weighted * residual, axis=(0, 2))
    local_mask = own_columns(valid_mask)
    grad_coef = -local_mask * local_var * sum_coef / (2.0 * total_days)
    grad_var = local_mask * (total_days - 0.5 * local_var * sum_var) / (2.0 * total_days)
    return innovation, grad_coef, grad_var


def solution(mesh):
    in_specs = (P("tm", "band", None), P(), P("tm"), P("band", None), P("band", None))
    out_specs = (P("tm", None, "band", None), P("band", "tm"), P("band", "tm"))
    return jax.shard_map(
        per_device, mesh=mesh, in_specs=in_specs, out_specs=out_specs, check_vma=False
    )
```

```python
import functools
import math

import jax
import jax.numpy as jnp
from jax import lax
from jax.experimental import pallas as pl
from jax.experimental.pallas import tpu as pltpu
from jax.sharding import PartitionSpec as P

LANES = 128
TILE = 16
PITCH = TILE + 1
HALF = TILE // 4
ROWS = 80
DAY_ROWS = 32
VMEM_LIMIT = 56 * 1024 * 1024


def round_up(value, unit):
    return -(-value // unit) * unit


def fourier_kernel(coarse_cos_ref, coarse_sin_ref, fine_cos_ref, fine_sin_ref, out_ref):
    lon_count = out_ref.shape[1]
    fine_cos, fine_sin = fine_cos_ref[...], fine_sin_ref[...]
    for index in range(-(-lon_count // LANES)):
        width = min(LANES, lon_count - index * LANES)
        coarse_cos = coarse_cos_ref[:, index : index + 1]
        coarse_sin = coarse_sin_ref[:, index : index + 1]
        values = (coarse_cos * fine_cos - coarse_sin * fine_sin).astype(jnp.bfloat16)
        out_ref[:, index * LANES : index * LANES + width] = values[:, :width]


def fourier_rows(waves, lon_count):
    blocks, slots = waves.shape
    rows = blocks * 2 * slots

    def parts(step):
        lons = jnp.arange(LANES, dtype=jnp.int32) * step
        phase = waves[:, :, None] * lons % lon_count
        angle = phase.astype(jnp.float32) * (2.0 * math.pi / lon_count)
        return jnp.cos(angle), jnp.sin(angle)

    def both(first, second):
        return jnp.stack([first, second], axis=1).reshape(rows, LANES)

    coarse_cos, coarse_sin = parts(LANES)
    fine_cos, fine_sin = parts(1)
    return pl.pallas_call(
        fourier_kernel,
        out_shape=jax.ShapeDtypeStruct((rows, lon_count), jnp.bfloat16),
        compiler_params=pltpu.CompilerParams(vmem_limit_bytes=VMEM_LIMIT),
    )(
        both(coarse_cos, -coarse_sin),
        both(coarse_sin, coarse_cos),
        both(fine_cos, fine_cos),
        both(fine_sin, fine_sin),
    )


def transform_kernel(in_ref, table_ref, *out_refs):
    lats, _, days = in_ref.shape
    for lat in range(0, lats, 2):
        both = jnp.concatenate([in_ref[lat], in_ref[lat + 1]], axis=1)
        sums = jnp.dot(table_ref[...], both, preferred_element_type=jnp.float32).astype(jnp.bfloat16)
        begin = 0
        for out_ref in out_refs:
            piece = sums[begin : begin + out_ref.shape[1]]
            begin += out_ref.shape[1]
            out_ref[lat] = piece[:, :days]
            out_ref[lat + 1] = piece[:, days:]


def longitude_sums(fields, table, block_rows):
    lats, lon_count, days = fields.shape
    group = 8 if lats % 8 == 0 else 2
    rows = table.shape[0]
    blocks = rows // block_rows
    return pl.pallas_call(
        transform_kernel,
        grid=(lats // group,),
        in_specs=[
            pl.BlockSpec((group, lon_count, days), lambda i: (i, 0, 0)),
            pl.BlockSpec((rows, lon_count), lambda i: (0, 0)),
        ],
        out_specs=[pl.BlockSpec((group, block_rows, days), lambda i: (i, 0, 0))] * blocks,
        out_shape=[jax.ShapeDtypeStruct((lats, block_rows, days), jnp.bfloat16)] * blocks,
        compiler_params=pltpu.CompilerParams(vmem_limit_bytes=VMEM_LIMIT),
    )(fields, table)


def table_kernel(steps, lane_tiles, top, low_ref, first_ref, second_ref, cos_ref, weight_ref, out_ref, rows_ref, scale_ref):
    tiles = range(lane_tiles)
    low = low_ref[...]
    high = top - low
    low_next = low + 1.0
    lat_count = out_ref.shape[2]
    pairs = out_ref.shape[0]

    def lanes(ref, tile):
        return ref[:, tile * LANES : (tile + 1) * LANES]

    cosines = [lanes(cos_ref, t) for t in tiles]
    weights = [lanes(weight_ref, t) for t in tiles]
    second = [lanes(second_ref, t) for t in tiles]
    for t in tiles:
        half = jnp.exp(0.5 * second[t])
        scale_ref[2, :, t * LANES : (t + 1) * LANES] = half * weights[t]
        scale_ref[3, :, t * LANES : (t + 1) * LANES] = half

    def block(index, carry):
        current, lagged, scale, last_inverse = carry
        for t in tiles:
            largest = jnp.maximum(jnp.maximum(jnp.abs(current[t]), jnp.abs(lagged[t])), 1.0)
            current[t] = current[t] / largest
            lagged[t] = lagged[t] / largest
            scale[t] = scale[t] + jnp.log(largest)
            half = jnp.exp(0.5 * scale[t])
            scale_ref[0, :, t * LANES : (t + 1) * LANES] = half * weights[t]
            scale_ref[1, :, t * LANES : (t + 1) * LANES] = half
        begin = (index * TILE).astype(jnp.float32)
        for step in range(TILE):
            row = begin + float(step)
            after = low < row
            above = row - jnp.where(after, low_next, 0.0)
            order = jnp.where(after, low, high)
            degree = above + order
            spread = above * (degree + order)
            square = 4.0 * degree * degree - 1.0
            root = lax.rsqrt(jnp.maximum(square * spread, 1.0))
            factor = square * root
            inverse = spread * root
            fresh = above == 0.0
            for t in tiles:
                advanced = factor * (cosines[t] * current[t] - last_inverse * lagged[t])
                lagged[t] = current[t]
                current[t] = jnp.where(fresh, 1.0, advanced)
                rows_ref[t, pl.ds(step, pairs, stride=PITCH), :] = current[t]
            last_inverse = inverse
        renewed = (low_next >= begin) & (low_next < begin + float(TILE))
        for t in tiles:
            scale[t] = jnp.where(renewed, second[t], scale[t])
        row_index = lax.broadcasted_iota(jnp.int32, (TILE, LANES), 0).astype(jnp.float32) + begin
        for pair in range(pairs):
            mark = low[pair : pair + 1, :]
            before = (row_index <= mark) | (mark + 1.0 < begin)
            for t in tiles:
                span = slice(t * LANES, min((t + 1) * LANES, lat_count))
                width = span.stop - span.start
                here = slice(t * LANES, (t + 1) * LANES)
                values = rows_ref[t, pair * PITCH : pair * PITCH + TILE, :]
                one = jnp.where(before, scale_ref[0, pair : pair + 1, here], scale_ref[2, pair : pair + 1, here])
                two = jnp.where(before, scale_ref[1, pair : pair + 1, here], scale_ref[3, pair : pair + 1, here])
                values = (values * one * two).astype(jnp.bfloat16)
                out_ref[pair, pl.ds(pl.multiple_of(index * TILE, TILE), TILE), span] = values[:, :width]
        return current, lagged, scale, last_inverse

    zeros = jnp.zeros((pairs, LANES), jnp.float32)
    start = (
        [zeros for _ in tiles],
        [zeros for _ in tiles],
        [lanes(first_ref, t) for t in tiles],
        zeros,
    )
    lax.fori_loop(0, steps // TILE, block, start)


def packed_table(low_waves, lats, lat_count, degree_count, steps):
    pair_count = low_waves.shape[0]
    lat_half = lats.shape[0]
    lane_tiles = -(-lat_half // LANES)
    width = lane_tiles * LANES
    top = float(degree_count - 1)
    index = jnp.pad(lats, (0, width - lat_half), mode="edge")
    colatitude = (index.astype(jnp.float32) + 0.5) * (math.pi / lat_count)
    sines = jnp.sin(colatitude)
    log_sines = jnp.log(sines)
    low = low_waves.astype(jnp.float32)

    def log_start(order):
        base = 0.5 * (
            jnp.log(order + 0.5)
            + jax.scipy.special.gammaln(order + 0.5)
            - jax.scipy.special.gammaln(order + 1.0)
            - 0.5 * math.log(math.pi)
        )
        return base[:, None] + order[:, None] * log_sines[None, :]

    def spread(row):
        return jnp.broadcast_to(row[None, :], (pair_count, width))

    return pl.pallas_call(
        functools.partial(table_kernel, steps, lane_tiles, top),
        out_shape=jax.ShapeDtypeStruct((pair_count, steps, lat_half), jnp.bfloat16),
        scratch_shapes=[
            pltpu.VMEM((lane_tiles, pair_count * PITCH, LANES), jnp.float32),
            pltpu.VMEM((4, pair_count, width), jnp.float32),
        ],
        compiler_params=pltpu.CompilerParams(vmem_limit_bytes=VMEM_LIMIT),
    )(
        jnp.broadcast_to(low[:, None], (pair_count, LANES)),
        log_start(top - low),
        log_start(low),
        spread(jnp.cos(colatitude)),
        spread(sines * (math.pi / lat_count)),
    )


def gather_slots(in_refs, flat_ref, slot_ref):
    lats, rows, days = in_refs[0].shape
    lat_half = len(in_refs) * lats
    step = 8 if lats % 8 == 0 else lats

    for part in range(2):
        for source, in_ref in enumerate(in_refs):

            def spread(index, carry, source=source, in_ref=in_ref, part=part):
                first = index * step
                values = in_ref[pl.ds(first, step), part * TILE : (part + 1) * TILE, :].astype(jnp.float32)
                begin = source * lats + first
                if step == 8:
                    window = flat_ref.at[pl.ds(pl.multiple_of(begin * PITCH, 8), 8 * PITCH)]
                else:
                    window = flat_ref.at[begin * PITCH : (begin + step) * PITCH]
                for lat in range(step):
                    window[lat * PITCH : lat * PITCH + TILE, :] = values[lat]
                return carry

            if step == 8:
                lax.fori_loop(0, lats // step, spread, 0)
            else:
                spread(0, 0)
        for slot in range(TILE):
            column = flat_ref[pl.ds(slot, lat_half, stride=PITCH), :]
            slot_ref[slot, :, part * days : (part + 1) * days] = column.astype(jnp.bfloat16)


def pair_sum(pair, low, table_ref, slot_ref):
    table = table_ref[pair]
    high_sum = jnp.dot(table, slot_ref[2 * pair], preferred_element_type=jnp.float32)
    low_sum = jnp.dot(table, slot_ref[2 * pair + 1], preferred_element_type=jnp.float32)
    row = lax.broadcasted_iota(jnp.int32, high_sum.shape, 0)
    return jnp.where(row <= low, high_sum, low_sum)


def by_halves(one):
    def two(step, carry):
        one(0, step)
        one(1, step)
        return carry

    lax.fori_loop(0, HALF, two, 0)


def partial_kernel(degrees, low_ref, table_ref, *rest):
    *in_refs, first_ref, second_ref, flat_ref, slot_ref, last_ref = rest
    out_refs = (first_ref, second_ref)
    gather_slots(in_refs, flat_ref, slot_ref)
    last_ref[...] = jnp.zeros_like(last_ref)
    last_row = lax.broadcasted_iota(jnp.int32, last_ref.shape[1:], 0)

    def one(half, step):
        pair = half * HALF + step
        sums = pair_sum(pair, low_ref[pair], table_ref, slot_ref)
        begin = pl.multiple_of(step * degrees, TILE)
        out_refs[half][pl.ds(begin, degrees), :] = sums[:degrees].astype(jnp.bfloat16)
        last_ref[half] = jnp.where(last_row == step, sums[degrees : degrees + 1], last_ref[half])

    by_halves(one)
    for half in range(2):
        out_refs[half][HALF * degrees :, :] = last_ref[half].astype(jnp.bfloat16)


def pack_kernel(low_ref, in_ref, ar_ref, half_ref):
    pairs, _, width = in_ref.shape
    steps = ar_ref.shape[1]
    lane = lax.broadcasted_iota(jnp.int32, (1, width), 1)
    degrees = round_up(steps, LANES) - LANES

    def one(pair, carry):
        low = low_ref[pair]
        rows = in_ref[pair]
        high_rows = pltpu.roll(rows, width - (degrees - 1 - low), 1)
        low_rows = pltpu.roll(rows, 1, 1)
        for index, out_ref in enumerate((ar_ref, half_ref)):
            packed = jnp.where(
                lane <= low, high_rows[2 * index : 2 * index + 1], low_rows[2 * index + 1 : 2 * index + 2]
            )
            out_ref[pair] = jnp.broadcast_to(packed, (LANES, width)).T[:steps]
        return carry

    lax.fori_loop(0, pairs, one, 0)


def packed_columns(low, values, steps):
    pairs = values.shape[0]
    return pl.pallas_call(
        pack_kernel,
        in_specs=[pl.BlockSpec(memory_space=pltpu.SMEM), pl.BlockSpec(memory_space=pltpu.VMEM)],
        out_shape=[jax.ShapeDtypeStruct((pairs, steps, LANES), jnp.float32)] * 2,
        compiler_params=pltpu.CompilerParams(vmem_limit_bytes=VMEM_LIMIT),
    )(low, values)


def finish_kernel(sources, low_ref, swap_ref, table_ref, first_ref, second_ref, ar_ref, half_ref, season_ref, *rest):
    out_ref, misc_ref, flat_ref, slot_ref, turned_ref, innovation_ref, stacked_ref = rest[-7:]
    steps = table_ref.shape[1]
    days = out_ref.shape[0]
    degrees = out_ref.shape[3]
    lane_tiles = degrees // LANES
    width = degrees + LANES
    gather_slots(rest[:sources], flat_ref, slot_ref)
    lane = lax.broadcasted_iota(jnp.int32, (ROWS, LANES), 1)
    degree = lax.broadcasted_iota(jnp.int32, (DAY_ROWS, degrees), 1)
    last_row = lax.broadcasted_iota(jnp.int32, (TILE, 2 * days), 0)
    turn = (
        lax.broadcasted_iota(jnp.int32, (days, days), 0) == lax.broadcasted_iota(jnp.int32, (days, days), 1)
    ).astype(jnp.bfloat16)
    pick_row = lax.broadcasted_iota(jnp.int32, (TILE, LANES), 0)
    pick_lane = lax.broadcasted_iota(jnp.int32, (TILE, LANES), 1)
    pick = (pick_lane == jnp.where(pick_row < 8, pick_row, pick_row + (LANES // 2 - 8))).astype(jnp.bfloat16)
    transposed = (((1,), (1,)), ((), ()))
    other_refs = (first_ref, second_ref)

    for half in range(2):
        stacked_ref[half, :, steps:] = jnp.zeros((2 * days + TILE, width - steps), jnp.float32)

    def one(part_of, step):
        pair = part_of * HALF + step
        low = low_ref[pair]
        other_ref = other_refs[part_of]
        begin = pl.multiple_of(step * degrees, TILE)
        last = jnp.where(last_row == step, other_ref[HALF * degrees :, :].astype(jnp.float32), 0.0)
        last = jnp.where(last_row == 0, jnp.sum(last, axis=0, keepdims=True), 0.0)
        table = table_ref[pair]
        high_sum = jnp.dot(table, slot_ref[2 * pair], preferred_element_type=jnp.float32)
        low_sum = jnp.dot(table, slot_ref[2 * pair + 1], preferred_element_type=jnp.float32)
        for first in range(0, steps, ROWS):
            here = slice(first, first + ROWS)
            row = lax.broadcasted_iota(jnp.int32, (ROWS, 2 * days), 0) + first
            own = jnp.where(row <= low, high_sum[here], low_sum[here])
            count = min(ROWS, degrees - first)
            other = other_ref[pl.ds(begin + first, count), :].astype(jnp.float32)
            if count < ROWS:
                other = jnp.concatenate([other, last], axis=0)
            total = own + other
            ar = ar_ref[pair, here]
            half = half_ref[pair, here]
            shifted_parts = []
            sum_coef = sum_var = 0.0
            for part in range(2):
                spectral = total[:, part * days : (part + 1) * days]
                shifted = pltpu.roll(spectral, 1, 1)
                shifted_parts.append(shifted)
                previous = jnp.where(lane == 0, 0.0, shifted)
                residual = spectral - ar * previous
                innovation_ref[part_of, part, here] = (residual * season_ref[0:1, :] * half).astype(jnp.bfloat16)
                weighted = residual * season_ref[1:2, :]
                sum_coef = sum_coef + weighted * previous
                sum_var = sum_var + weighted * residual
            sum_coef = jnp.sum(sum_coef, axis=1, keepdims=True)
            sum_var = jnp.sum(sum_var, axis=1, keepdims=True)
            misc = jnp.where(
                lane < 2,
                shifted_parts[0],
                jnp.where(lane < 4, pltpu.roll(shifted_parts[1], 2, 1), jnp.where(lane == 4, sum_coef, sum_var)),
            )
            misc_high = misc.astype(jnp.bfloat16).astype(jnp.float32)
            misc_low = pltpu.roll(misc - misc_high, LANES // 2, 1)
            misc = jnp.where(lane < LANES // 2, misc_high, misc_low)
            innovation_ref[part_of, 2, here] = misc.astype(jnp.bfloat16)
        for part in range(3):
            placer = turn if part < 2 else pick
            stacked_ref[part_of, part * days : part * days + placer.shape[0], :steps] = lax.dot_general(
                placer, innovation_ref[part_of, part], transposed, preferred_element_type=jnp.float32
            )
        high = degrees - 1 - low
        swap = swap_ref[pair]
        for shift, start, slot in ((high, high, 2 * pair + swap), (width - 1, low, 2 * pair + 1 - swap)):
            for first in range(0, 2 * days, DAY_ROWS):
                stacked = stacked_ref[part_of, first : first + DAY_ROWS, :]
                placed = jnp.where(degree >= start, pltpu.roll(stacked, shift, 1)[:, :degrees], 0.0)
                part, day = divmod(first, days)
                for t in range(lane_tiles):
                    turned_ref[part, t, pl.ds(day * PITCH + slot, DAY_ROWS, stride=PITCH), :] = placed[
                        :, t * LANES : (t + 1) * LANES
                    ]
            stacked = stacked_ref[part_of, 2 * days :, :]
            placed = jnp.where(degree[:TILE] >= start, pltpu.roll(stacked, shift, 1)[:, :degrees], 0.0)
            misc_ref[slot] = placed[:8] + placed[8:]

    by_halves(one)

    def write(step, carry):
        begin = pl.multiple_of(step * 8 * PITCH, 8)
        for part in range(2):
            for t in range(lane_tiles):
                window = turned_ref.at[part, t, pl.ds(begin, 8 * PITCH)]
                for day in range(8):
                    values = window[day * PITCH : day * PITCH + TILE, :]
                    out_ref[step * 8 + day, part, :, t * LANES : (t + 1) * LANES] = values.astype(jnp.bfloat16)
        return carry

    lax.fori_loop(0, days // 8, write, 0)


def leading(shape, chunk):
    return pl.BlockSpec(shape, lambda i: (chunk,) + (0,) * (len(shape) - 1))


def partial_sums(chunk, place, low, blocks, table, degrees):
    lats, rows, days = blocks[0].shape
    steps, lat_half = table.shape[1:]
    out_rows = HALF * degrees + TILE
    pairs = TILE // 2
    return pl.pallas_call(
        functools.partial(partial_kernel, degrees),
        grid=(1,),
        in_specs=[
            pl.BlockSpec(memory_space=pltpu.SMEM),
            leading((pairs, steps, lat_half), chunk),
        ]
        + [pl.BlockSpec((lats, 2 * TILE, days), lambda i: (0, place, 0)) for _ in blocks],
        out_specs=[leading((out_rows, 2 * days), 0)] * 2,
        out_shape=[jax.ShapeDtypeStruct((out_rows, 2 * days), jnp.bfloat16)] * 2,
        scratch_shapes=[
            pltpu.VMEM((lat_half * PITCH, days), jnp.float32),
            pltpu.VMEM((TILE, lat_half, 2 * days), jnp.bfloat16),
            pltpu.VMEM((2, TILE, 2 * days), jnp.float32),
        ],
        compiler_params=pltpu.CompilerParams(vmem_limit_bytes=VMEM_LIMIT),
    )(low, table, *blocks)


def finish(chunk, low, swap, blocks, table, other, columns, season, held, slot_total, degrees):
    lats, rows, days = blocks[0].shape
    steps, lat_half = table.shape[1:]
    pairs = TILE // 2
    smem = pl.BlockSpec(memory_space=pltpu.SMEM)
    operands = [low, swap, table, *other, *columns, season, *blocks]
    in_specs = [
        smem,
        smem,
        leading((pairs, steps, lat_half), chunk),
        leading(other[0].shape, 0),
        leading(other[1].shape, 0),
        leading((pairs, steps, LANES), chunk),
        leading((pairs, steps, LANES), chunk),
        leading((8, LANES), 0),
    ] + [leading(block.shape, 0) for block in blocks]
    aliases = {}
    if held is not None:
        operands.append(held)
        in_specs.append(pl.BlockSpec(memory_space=pl.ANY))
        aliases = {len(operands) - 1: 0}
    return pl.pallas_call(
        functools.partial(finish_kernel, len(blocks)),
        grid=(1,),
        in_specs=in_specs,
        out_specs=[
            pl.BlockSpec((days, 2, TILE, degrees), lambda i: (0, 0, chunk, 0)),
            leading((TILE, 8, degrees), 0),
        ],
        out_shape=[
            jax.ShapeDtypeStruct((days, 2, slot_total, degrees), jnp.bfloat16),
            jax.ShapeDtypeStruct((TILE, 8, degrees), jnp.float32),
        ],
        input_output_aliases=aliases,
        scratch_shapes=[
            pltpu.VMEM((lat_half * PITCH, days), jnp.float32),
            pltpu.VMEM((TILE, lat_half, 2 * days), jnp.bfloat16),
            pltpu.VMEM((2, degrees // LANES, days * PITCH, LANES), jnp.float32),
            pltpu.VMEM((2, 3, steps, LANES), jnp.bfloat16),
            pltpu.VMEM((2, 2 * days + TILE, degrees + LANES), jnp.float32),
        ],
        compiler_params=pltpu.CompilerParams(vmem_limit_bytes=VMEM_LIMIT),
    )(*operands)


def after(values, waited):
    return lax.optimization_barrier((values, waited))[0]


def per_device(fields, wave_table, day_of_year, ar_coef, log_var):
    band_count = lax.axis_size("band")
    time_count = lax.axis_size("tm")
    band = lax.axis_index("band")
    slot_count, degree_count = ar_coef.shape
    day_count, lat_local, lon_count = fields.shape
    lat_count = lat_local * band_count
    group = band_count // 2
    steps = round_up(degree_count + 1, TILE)
    total_days = day_count * time_count
    slot_pad = round_up(slot_count, TILE)
    chunks = slot_pad // TILE
    pairs = slot_pad // 2
    half_index = band // group
    rank = band % group
    mirror = [(i, (i + group) % band_count) for i in range(band_count)]
    peers = [rank ^ k for k in range(group)]

    fields = fields.transpose(1, 2, 0)

    waves = wave_table.reshape(2, group, slot_count // 2, 2)
    high_low = jnp.stack([waves.max(-1), waves.min(-1)], axis=-1)
    high_low = jnp.pad(high_low, ((0, 0), (0, 0), (0, pairs - slot_count // 2), (0, 0)))
    ordered = high_low.reshape(2, group, slot_pad)
    present = jnp.arange(slot_pad) < slot_count

    def by_peer(side):
        table = lax.dynamic_index_in_dim(ordered, side, 0, keepdims=False)
        return jnp.stack([lax.dynamic_index_in_dim(table, peer, 0, keepdims=False) for peer in peers])

    own_waves, far_waves = by_peer(half_index), by_peer(1 - half_index)
    own_low, far_low = own_waves[0, 1::2], far_waves[0, 1::2]
    lats = jnp.concatenate(
        [(half_index * group + peer) * lat_local + jnp.arange(lat_local, dtype=jnp.int32) for peer in peers]
    )

    def table_of(waves_of, first, count):
        picked = waves_of[:, first * TILE : (first + count) * TILE].reshape(group * count, TILE)
        table = fourier_rows(picked, lon_count)
        if slot_pad != slot_count:
            mask = present[first * TILE : (first + count) * TILE].reshape(count, 1, TILE)
            mask = jnp.broadcast_to(mask, (group, count, 2, TILE)).reshape(-1, 1)
            table = table * mask.astype(jnp.bfloat16)
        return table

    across = list(range(group // 2, group))
    order = across[:0:-1] + list(range(1, group // 2)) + across[:1]

    def exchange(blocks, order):
        moved = [blocks[0]] + [None] * (group - 1)
        for k in order:
            moved[k] = lax.ppermute(blocks[k], "band", [(i, i ^ k) for i in range(band_count)])
        return moved

    blocks = longitude_sums(fields, table_of(far_waves, 0, 1), 2 * TILE)
    far = [exchange(blocks, order)]
    if chunks > 1:
        later = after(fields, blocks[0])
        blocks = longitude_sums(later, table_of(far_waves, 1, chunks - 1), (chunks - 1) * 2 * TILE)
        far.append(exchange(blocks, order))
    far_table = packed_table(after(far_low, blocks[0]), lats, lat_count, degree_count, steps)

    others = []

    def send_sums(chunk, waited):
        low = far_low[chunk * TILE // 2 : (chunk + 1) * TILE // 2]
        sums = partial_sums(chunk, max(chunk - 1, 0), after(low, waited), far[min(chunk, 1)], far_table, degree_count)
        sums = after(sums, others[-1]) if others else sums
        others.append([lax.ppermute(part, "band", mirror) for part in sums])
        return sums

    sums = send_sums(0, blocks[0])

    fields, own_waves, own_low, ar_coef, log_var = after((fields, own_waves, own_low, ar_coef, log_var), sums)
    blocks = longitude_sums(fields, table_of(own_waves, 0, chunks), 2 * TILE)
    own_table = packed_table(after(own_low, blocks[0]), lats, lat_count, degree_count, steps)
    slot_waves = lax.dynamic_slice_in_dim(wave_table, band * slot_count, slot_count)
    pad_slots = (0, slot_pad - slot_count)
    swap = (jnp.pad(slot_waves, pad_slots)[::2] == own_low).astype(jnp.int32)

    def by_pair(values):
        values = jnp.pad(values, (pad_slots, (0, LANES))).reshape(pairs, 2, degree_count + LANES)
        return jnp.where(swap[:, None, None] == 1, values[:, ::-1], values)

    values = jnp.concatenate([by_pair(ar_coef), by_pair(jnp.exp(-0.5 * log_var))], axis=1)
    columns = packed_columns(own_low, jnp.pad(values, ((0, 0), (0, 4), (0, 0))), steps)
    for chunk in range(1, chunks):
        send_sums(chunk, own_table if chunk == 1 else columns[0])

    season = 1.0 + 0.5 * jnp.cos(day_of_year.astype(jnp.float32) * (2.0 * math.pi / 365.0))
    later = (jnp.arange(day_count) > 0).astype(jnp.float32)
    season_rows = jnp.pad(jnp.stack([lax.rsqrt(season), later / season]), ((0, 6), (0, 0)))

    own = [exchange(after(blocks[::chunks], ([far[-1][k] for k in across], own_table)), order)]
    innovation = None
    misc = []
    for chunk in range(chunks):
        if chunk + 1 < chunks:
            crossed = own[-1]
            own.append(exchange(after(blocks[chunk + 1 :: chunks], (crossed, misc[:chunk])), order))
        span = slice(chunk * TILE // 2, (chunk + 1) * TILE // 2)
        innovation, rows = finish(
            chunk, own_low[span], swap[span], own[chunk], own_table, others[chunk], columns, season_rows,
            innovation, slot_pad, degree_count,
        )
        misc.append(rows)
    innovation = innovation[:, :, :slot_count]
    misc = jnp.concatenate(misc, axis=0)[:slot_count, :6]

    degree_list = jnp.arange(degree_count, dtype=jnp.int32)
    valid_mask = (degree_list[None, :] >= slot_waves[:, None]).astype(jnp.float32)
    edges = misc.transpose(1, 0, 2)
    route = [(i, i + 1) for i in range(time_count - 1)]
    carried = lax.ppermute(edges[0:4:2].astype(jnp.bfloat16), "tm", route).astype(jnp.float32)
    scale = jnp.exp(-0.5 * log_var) * lax.rsqrt(season[0]) * valid_mask
    opening = ((edges[1:4:2] - ar_coef[None] * carried) * scale[None]).astype(jnp.bfloat16)
    innovation = lax.dynamic_update_slice_in_dim(innovation, opening[None], 0, 0)

    column_width = degree_count // time_count
    place = lax.axis_index("tm")
    columns = [misc[:, :, i * column_width : (i + 1) * column_width] for i in range(time_count)]
    moved = lax.all_to_all(jnp.stack(columns).astype(jnp.bfloat16), "tm", 0, 0, tiled=True).astype(jnp.float32)

    def own_columns(values):
        return lax.dynamic_slice_in_dim(values, place * column_width, column_width, 1)

    local_ar, local_var = own_columns(ar_coef), jnp.exp(-own_columns(log_var))
    first_days = day_of_year[0] + (jnp.arange(time_count, dtype=jnp.int32) - place) * day_count
    first_days = (first_days % 365).astype(jnp.float32)
    openness = 1.0 / (1.0 + 0.5 * jnp.cos(first_days * (2.0 * math.pi / 365.0)))
    first = moved[:, :, 1:4:2]
    before = jnp.concatenate([jnp.zeros_like(moved[:1, :, 0:4:2]), moved[:-1, :, 0:4:2]], axis=0)
    residual = first - local_ar[None, :, None] * before
    weighted = residual * openness[:, None, None, None]
    sum_coef = jnp.sum(moved[:, :, 4], axis=0) + jnp.sum(weighted * before, axis=(0, 2))
    sum_var = jnp.sum(moved[:, :, 5], axis=0) + jnp.sum(weighted * residual, axis=(0, 2))
    local_mask = own_columns(valid_mask)
    grad_coef = -local_mask * local_var * sum_coef / (2.0 * total_days)
    grad_var = local_mask * (total_days - 0.5 * local_var * sum_var) / (2.0 * total_days)
    return innovation, grad_coef, grad_var


def solution(mesh):
    in_specs = (P("tm", "band", None), P(), P("tm"), P("band", None), P("band", None))
    out_specs = (P("tm", None, "band", None), P("band", "tm"), P("band", "tm"))
    return jax.shard_map(
        per_device, mesh=mesh, in_specs=in_specs, out_specs=out_specs, check_vma=False
    )
```

```python
import functools
import math

import jax
import jax.numpy as jnp
from jax import lax
from jax.experimental import pallas as pl
from jax.experimental.pallas import tpu as pltpu
from jax.sharding import PartitionSpec as P

LANES = 128
TILE = 16
PITCH = TILE + 1
HALF = TILE // 4
ROWS = 80
DAY_ROWS = 32
VMEM_LIMIT = 56 * 1024 * 1024


def round_up(value, unit):
    return -(-value // unit) * unit


def fourier_kernel(coarse_cos_ref, coarse_sin_ref, fine_cos_ref, fine_sin_ref, out_ref):
    lon_count = out_ref.shape[1]
    fine_cos, fine_sin = fine_cos_ref[...], fine_sin_ref[...]
    for index in range(-(-lon_count // LANES)):
        width = min(LANES, lon_count - index * LANES)
        coarse_cos = coarse_cos_ref[:, index : index + 1]
        coarse_sin = coarse_sin_ref[:, index : index + 1]
        values = (coarse_cos * fine_cos - coarse_sin * fine_sin).astype(jnp.bfloat16)
        out_ref[:, index * LANES : index * LANES + width] = values[:, :width]


def fourier_rows(waves, lon_count):
    blocks, slots = waves.shape
    rows = blocks * 2 * slots

    def parts(step):
        lons = jnp.arange(LANES, dtype=jnp.int32) * step
        phase = waves[:, :, None] * lons % lon_count
        angle = phase.astype(jnp.float32) * (2.0 * math.pi / lon_count)
        return jnp.cos(angle), jnp.sin(angle)

    def both(first, second):
        return jnp.stack([first, second], axis=1).reshape(rows, LANES)

    coarse_cos, coarse_sin = parts(LANES)
    fine_cos, fine_sin = parts(1)
    return pl.pallas_call(
        fourier_kernel,
        out_shape=jax.ShapeDtypeStruct((rows, lon_count), jnp.bfloat16),
        compiler_params=pltpu.CompilerParams(vmem_limit_bytes=VMEM_LIMIT),
    )(
        both(coarse_cos, -coarse_sin),
        both(coarse_sin, coarse_cos),
        both(fine_cos, fine_cos),
        both(fine_sin, fine_sin),
    )


def transform_kernel(in_ref, table_ref, *out_refs):
    lats, _, days = in_ref.shape
    for lat in range(0, lats, 2):
        both = jnp.concatenate([in_ref[lat], in_ref[lat + 1]], axis=1)
        sums = jnp.dot(table_ref[...], both, preferred_element_type=jnp.float32).astype(jnp.bfloat16)
        begin = 0
        for out_ref in out_refs:
            piece = sums[begin : begin + out_ref.shape[1]]
            begin += out_ref.shape[1]
            out_ref[lat] = piece[:, :days]
            out_ref[lat + 1] = piece[:, days:]


def longitude_sums(fields, table, block_rows):
    lats, lon_count, days = fields.shape
    group = 8 if lats % 8 == 0 else 2
    rows = table.shape[0]
    blocks = rows // block_rows
    return pl.pallas_call(
        transform_kernel,
        grid=(lats // group,),
        in_specs=[
            pl.BlockSpec((group, lon_count, days), lambda i: (i, 0, 0)),
            pl.BlockSpec((rows, lon_count), lambda i: (0, 0)),
        ],
        out_specs=[pl.BlockSpec((group, block_rows, days), lambda i: (i, 0, 0))] * blocks,
        out_shape=[jax.ShapeDtypeStruct((lats, block_rows, days), jnp.bfloat16)] * blocks,
        compiler_params=pltpu.CompilerParams(vmem_limit_bytes=VMEM_LIMIT),
    )(fields, table)


def table_kernel(steps, lane_tiles, top, low_ref, first_ref, second_ref, cos_ref, weight_ref, out_ref, rows_ref, scale_ref):
    tiles = range(lane_tiles)
    low = low_ref[...]
    high = top - low
    low_next = low + 1.0
    lat_count = out_ref.shape[2]
    pairs = out_ref.shape[0]

    def lanes(ref, tile):
        return ref[:, tile * LANES : (tile + 1) * LANES]

    cosines = [lanes(cos_ref, t) for t in tiles]
    weights = [lanes(weight_ref, t) for t in tiles]
    second = [lanes(second_ref, t) for t in tiles]
    for t in tiles:
        half = jnp.exp(0.5 * second[t])
        scale_ref[2, :, t * LANES : (t + 1) * LANES] = half * weights[t]
        scale_ref[3, :, t * LANES : (t + 1) * LANES] = half

    def block(index, carry):
        current, lagged, scale, last_inverse = carry
        for t in tiles:
            largest = jnp.maximum(jnp.maximum(jnp.abs(current[t]), jnp.abs(lagged[t])), 1.0)
            current[t] = current[t] / largest
            lagged[t] = lagged[t] / largest
            scale[t] = scale[t] + jnp.log(largest)
            half = jnp.exp(0.5 * scale[t])
            scale_ref[0, :, t * LANES : (t + 1) * LANES] = half * weights[t]
            scale_ref[1, :, t * LANES : (t + 1) * LANES] = half
        begin = (index * TILE).astype(jnp.float32)
        for step in range(TILE):
            row = begin + float(step)
            after = low < row
            above = row - jnp.where(after, low_next, 0.0)
            order = jnp.where(after, low, high)
            degree = above + order
            spread = above * (degree + order)
            square = 4.0 * degree * degree - 1.0
            root = lax.rsqrt(jnp.maximum(square * spread, 1.0))
            factor = square * root
            inverse = spread * root
            fresh = above == 0.0
            for t in tiles:
                advanced = factor * (cosines[t] * current[t] - last_inverse * lagged[t])
                lagged[t] = current[t]
                current[t] = jnp.where(fresh, 1.0, advanced)
                rows_ref[t, pl.ds(step, pairs, stride=PITCH), :] = current[t]
            last_inverse = inverse
        renewed = (low_next >= begin) & (low_next < begin + float(TILE))
        for t in tiles:
            scale[t] = jnp.where(renewed, second[t], scale[t])
        row_index = lax.broadcasted_iota(jnp.int32, (TILE, LANES), 0).astype(jnp.float32) + begin
        for pair in range(pairs):
            mark = low[pair : pair + 1, :]
            before = (row_index <= mark) | (mark + 1.0 < begin)
            for t in tiles:
                span = slice(t * LANES, min((t + 1) * LANES, lat_count))
                width = span.stop - span.start
                here = slice(t * LANES, (t + 1) * LANES)
                values = rows_ref[t, pair * PITCH : pair * PITCH + TILE, :]
                one = jnp.where(before, scale_ref[0, pair : pair + 1, here], scale_ref[2, pair : pair + 1, here])
                two = jnp.where(before, scale_ref[1, pair : pair + 1, here], scale_ref[3, pair : pair + 1, here])
                values = (values * one * two).astype(jnp.bfloat16)
                out_ref[pair, pl.ds(pl.multiple_of(index * TILE, TILE), TILE), span] = values[:, :width]
        return current, lagged, scale, last_inverse

    zeros = jnp.zeros((pairs, LANES), jnp.float32)
    start = (
        [zeros for _ in tiles],
        [zeros for _ in tiles],
        [lanes(first_ref, t) for t in tiles],
        zeros,
    )
    lax.fori_loop(0, steps // TILE, block, start)


def packed_table(low_waves, lats, lat_count, degree_count, steps):
    pair_count = low_waves.shape[0]
    lat_half = lats.shape[0]
    lane_tiles = -(-lat_half // LANES)
    width = lane_tiles * LANES
    top = float(degree_count - 1)
    index = jnp.pad(lats, (0, width - lat_half), mode="edge")
    colatitude = (index.astype(jnp.float32) + 0.5) * (math.pi / lat_count)
    sines = jnp.sin(colatitude)
    log_sines = jnp.log(sines)
    low = low_waves.astype(jnp.float32)

    def log_start(order):
        base = 0.5 * (
            jnp.log(order + 0.5)
            + jax.scipy.special.gammaln(order + 0.5)
            - jax.scipy.special.gammaln(order + 1.0)
            - 0.5 * math.log(math.pi)
        )
        return base[:, None] + order[:, None] * log_sines[None, :]

    def spread(row):
        return jnp.broadcast_to(row[None, :], (pair_count, width))

    return pl.pallas_call(
        functools.partial(table_kernel, steps, lane_tiles, top),
        out_shape=jax.ShapeDtypeStruct((pair_count, steps, lat_half), jnp.bfloat16),
        scratch_shapes=[
            pltpu.VMEM((lane_tiles, pair_count * PITCH, LANES), jnp.float32),
            pltpu.VMEM((4, pair_count, width), jnp.float32),
        ],
        compiler_params=pltpu.CompilerParams(vmem_limit_bytes=VMEM_LIMIT),
    )(
        jnp.broadcast_to(low[:, None], (pair_count, LANES)),
        log_start(top - low),
        log_start(low),
        spread(jnp.cos(colatitude)),
        spread(sines * (math.pi / lat_count)),
    )


def gather_slots(in_refs, flat_ref, slot_ref):
    lats, rows, days = in_refs[0].shape
    lat_half = len(in_refs) * lats
    step = 8 if lats % 8 == 0 else lats

    for part in range(2):
        for source, in_ref in enumerate(in_refs):

            def spread(index, carry, source=source, in_ref=in_ref, part=part):
                first = index * step
                values = in_ref[pl.ds(first, step), part * TILE : (part + 1) * TILE, :].astype(jnp.float32)
                begin = source * lats + first
                if step == 8:
                    window = flat_ref.at[pl.ds(pl.multiple_of(begin * PITCH, 8), 8 * PITCH)]
                else:
                    window = flat_ref.at[begin * PITCH : (begin + step) * PITCH]
                for lat in range(step):
                    window[lat * PITCH : lat * PITCH + TILE, :] = values[lat]
                return carry

            if step == 8:
                lax.fori_loop(0, lats // step, spread, 0)
            else:
                spread(0, 0)
        for slot in range(TILE):
            column = flat_ref[pl.ds(slot, lat_half, stride=PITCH), :]
            slot_ref[slot, :, part * days : (part + 1) * days] = column.astype(jnp.bfloat16)


def pair_sum(pair, low, table_ref, slot_ref):
    table = table_ref[pair]
    high_sum = jnp.dot(table, slot_ref[2 * pair], preferred_element_type=jnp.float32)
    low_sum = jnp.dot(table, slot_ref[2 * pair + 1], preferred_element_type=jnp.float32)
    row = lax.broadcasted_iota(jnp.int32, high_sum.shape, 0)
    return jnp.where(row <= low, high_sum, low_sum)


def by_halves(one):
    def two(step, carry):
        one(0, step)
        one(1, step)
        return carry

    lax.fori_loop(0, HALF, two, 0)


def partial_kernel(degrees, low_ref, table_ref, *rest):
    *in_refs, first_ref, second_ref, flat_ref, slot_ref, last_ref = rest
    out_refs = (first_ref, second_ref)
    gather_slots(in_refs, flat_ref, slot_ref)
    last_ref[...] = jnp.zeros_like(last_ref)
    last_row = lax.broadcasted_iota(jnp.int32, last_ref.shape[1:], 0)

    def one(half, step):
        pair = half * HALF + step
        sums = pair_sum(pair, low_ref[pair], table_ref, slot_ref)
        begin = pl.multiple_of(step * degrees, TILE)
        out_refs[half][pl.ds(begin, degrees), :] = sums[:degrees].astype(jnp.bfloat16)
        last_ref[half] = jnp.where(last_row == step, sums[degrees : degrees + 1], last_ref[half])

    by_halves(one)
    for half in range(2):
        out_refs[half][HALF * degrees :, :] = last_ref[half].astype(jnp.bfloat16)


def pack_kernel(low_ref, in_ref, ar_ref, half_ref):
    pairs, _, width = in_ref.shape
    steps = ar_ref.shape[1]
    lane = lax.broadcasted_iota(jnp.int32, (1, width), 1)
    degrees = round_up(steps, LANES) - LANES

    def one(pair, carry):
        low = low_ref[pair]
        rows = in_ref[pair]
        high_rows = pltpu.roll(rows, width - (degrees - 1 - low), 1)
        low_rows = pltpu.roll(rows, 1, 1)
        for index, out_ref in enumerate((ar_ref, half_ref)):
            packed = jnp.where(
                lane <= low, high_rows[2 * index : 2 * index + 1], low_rows[2 * index + 1 : 2 * index + 2]
            )
            out_ref[pair] = jnp.broadcast_to(packed, (LANES, width)).T[:steps]
        return carry

    lax.fori_loop(0, pairs, one, 0)


def packed_columns(low, values, steps):
    pairs = values.shape[0]
    return pl.pallas_call(
        pack_kernel,
        in_specs=[pl.BlockSpec(memory_space=pltpu.SMEM), pl.BlockSpec(memory_space=pltpu.VMEM)],
        out_shape=[jax.ShapeDtypeStruct((pairs, steps, LANES), jnp.float32)] * 2,
        compiler_params=pltpu.CompilerParams(vmem_limit_bytes=VMEM_LIMIT),
    )(low, values)


def finish_kernel(sources, low_ref, swap_ref, table_ref, first_ref, second_ref, ar_ref, half_ref, season_ref, *rest):
    out_ref, misc_ref, edge_ref, send_ref, flat_ref, slot_ref, turned_ref, innovation_ref, stacked_ref = rest[-9:]
    steps = table_ref.shape[1]
    days = out_ref.shape[0]
    degrees = out_ref.shape[3]
    lane_tiles = degrees // LANES
    width = degrees + LANES
    gather_slots(rest[:sources], flat_ref, slot_ref)
    lane = lax.broadcasted_iota(jnp.int32, (ROWS, LANES), 1)
    degree = lax.broadcasted_iota(jnp.int32, (DAY_ROWS, degrees), 1)
    last_row = lax.broadcasted_iota(jnp.int32, (TILE, 2 * days), 0)
    turn = (
        lax.broadcasted_iota(jnp.int32, (days, days), 0) == lax.broadcasted_iota(jnp.int32, (days, days), 1)
    ).astype(jnp.bfloat16)
    pick_row = lax.broadcasted_iota(jnp.int32, (TILE, LANES), 0)
    pick_lane = lax.broadcasted_iota(jnp.int32, (TILE, LANES), 1)
    pick = (pick_lane == jnp.where(pick_row < 8, pick_row, pick_row + (LANES // 2 - 8))).astype(jnp.bfloat16)
    transposed = (((1,), (1,)), ((), ()))
    other_refs = (first_ref, second_ref)

    for half in range(2):
        stacked_ref[half, :, steps:] = jnp.zeros((2 * days + TILE, width - steps), jnp.float32)

    def one(part_of, step):
        pair = part_of * HALF + step
        low = low_ref[pair]
        other_ref = other_refs[part_of]
        begin = pl.multiple_of(step * degrees, TILE)
        last = jnp.where(last_row == step, other_ref[HALF * degrees :, :].astype(jnp.float32), 0.0)
        last = jnp.where(last_row == 0, jnp.sum(last, axis=0, keepdims=True), 0.0)
        table = table_ref[pair]
        high_sum = jnp.dot(table, slot_ref[2 * pair], preferred_element_type=jnp.float32)
        low_sum = jnp.dot(table, slot_ref[2 * pair + 1], preferred_element_type=jnp.float32)
        for first in range(0, steps, ROWS):
            here = slice(first, first + ROWS)
            row = lax.broadcasted_iota(jnp.int32, (ROWS, 2 * days), 0) + first
            own = jnp.where(row <= low, high_sum[here], low_sum[here])
            count = min(ROWS, degrees - first)
            other = other_ref[pl.ds(begin + first, count), :].astype(jnp.float32)
            if count < ROWS:
                other = jnp.concatenate([other, last], axis=0)
            total = own + other
            ar = ar_ref[pair, here]
            half = half_ref[pair, here]
            shifted_parts = []
            sum_coef = sum_var = 0.0
            for part in range(2):
                spectral = total[:, part * days : (part + 1) * days]
                shifted = pltpu.roll(spectral, 1, 1)
                shifted_parts.append(shifted)
                previous = jnp.where(lane == 0, 0.0, shifted)
                residual = spectral - ar * previous
                innovation_ref[part_of, part, here] = (residual * season_ref[0:1, :] * half).astype(jnp.bfloat16)
                weighted = residual * season_ref[1:2, :]
                sum_coef = sum_coef + weighted * previous
                sum_var = sum_var + weighted * residual
            sum_coef = jnp.sum(sum_coef, axis=1, keepdims=True)
            sum_var = jnp.sum(sum_var, axis=1, keepdims=True)
            misc = jnp.where(
                lane < 2,
                shifted_parts[0],
                jnp.where(lane < 4, pltpu.roll(shifted_parts[1], 2, 1), jnp.where(lane == 4, sum_coef, sum_var)),
            )
            misc_high = misc.astype(jnp.bfloat16).astype(jnp.float32)
            misc_low = pltpu.roll(misc - misc_high, LANES // 2, 1)
            misc = jnp.where(lane < LANES // 2, misc_high, misc_low)
            innovation_ref[part_of, 2, here] = misc.astype(jnp.bfloat16)
        for part in range(3):
            placer = turn if part < 2 else pick
            stacked_ref[part_of, part * days : part * days + placer.shape[0], :steps] = lax.dot_general(
                placer, innovation_ref[part_of, part], transposed, preferred_element_type=jnp.float32
            )
        high = degrees - 1 - low
        swap = swap_ref[pair]
        for shift, start, slot in ((high, high, 2 * pair + swap), (width - 1, low, 2 * pair + 1 - swap)):
            for first in range(0, 2 * days, DAY_ROWS):
                stacked = stacked_ref[part_of, first : first + DAY_ROWS, :]
                placed = jnp.where(degree >= start, pltpu.roll(stacked, shift, 1)[:, :degrees], 0.0)
                part, day = divmod(first, days)
                for t in range(lane_tiles):
                    turned_ref[part, t, pl.ds(day * PITCH + slot, DAY_ROWS, stride=PITCH), :] = placed[
                        :, t * LANES : (t + 1) * LANES
                    ]
            stacked = stacked_ref[part_of, 2 * days :, :]
            placed = jnp.where(degree[:TILE] >= start, pltpu.roll(stacked, shift, 1)[:, :degrees], 0.0)
            placed = placed[:8] + placed[8:]
            misc_ref[slot] = placed
            edge_ref[slot] = placed.astype(jnp.bfloat16)
            columns = send_ref.shape[3]
            for peer in range(send_ref.shape[0]):
                send_ref[peer, slot] = placed[:, peer * columns : (peer + 1) * columns].astype(jnp.bfloat16)

    by_halves(one)

    def write(step, carry):
        begin = pl.multiple_of(step * 8 * PITCH, 8)
        for part in range(2):
            for t in range(lane_tiles):
                window = turned_ref.at[part, t, pl.ds(begin, 8 * PITCH)]
                for day in range(8):
                    values = window[day * PITCH : day * PITCH + TILE, :]
                    out_ref[step * 8 + day, part, :, t * LANES : (t + 1) * LANES] = values.astype(jnp.bfloat16)
        return carry

    lax.fori_loop(0, days // 8, write, 0)


def leading(shape, chunk):
    return pl.BlockSpec(shape, lambda i: (chunk,) + (0,) * (len(shape) - 1))


def partial_sums(chunk, place, low, blocks, table, degrees):
    lats, rows, days = blocks[0].shape
    steps, lat_half = table.shape[1:]
    out_rows = HALF * degrees + TILE
    pairs = TILE // 2
    return pl.pallas_call(
        functools.partial(partial_kernel, degrees),
        grid=(1,),
        in_specs=[
            pl.BlockSpec(memory_space=pltpu.SMEM),
            leading((pairs, steps, lat_half), chunk),
        ]
        + [pl.BlockSpec((lats, 2 * TILE, days), lambda i: (0, place, 0)) for _ in blocks],
        out_specs=[leading((out_rows, 2 * days), 0)] * 2,
        out_shape=[jax.ShapeDtypeStruct((out_rows, 2 * days), jnp.bfloat16)] * 2,
        scratch_shapes=[
            pltpu.VMEM((lat_half * PITCH, days), jnp.float32),
            pltpu.VMEM((TILE, lat_half, 2 * days), jnp.bfloat16),
            pltpu.VMEM((2, TILE, 2 * days), jnp.float32),
        ],
        compiler_params=pltpu.CompilerParams(vmem_limit_bytes=VMEM_LIMIT),
    )(low, table, *blocks)


def finish(chunk, low, swap, blocks, table, other, columns, season, held, slot_total, degrees, time_count):
    lats, rows, days = blocks[0].shape
    steps, lat_half = table.shape[1:]
    pairs = TILE // 2
    smem = pl.BlockSpec(memory_space=pltpu.SMEM)
    operands = [low, swap, table, *other, *columns, season, *blocks]
    in_specs = [
        smem,
        smem,
        leading((pairs, steps, lat_half), chunk),
        leading(other[0].shape, 0),
        leading(other[1].shape, 0),
        leading((pairs, steps, LANES), chunk),
        leading((pairs, steps, LANES), chunk),
        leading((8, LANES), 0),
    ] + [leading(block.shape, 0) for block in blocks]
    aliases = {}
    if held is not None:
        operands.append(held)
        in_specs.append(pl.BlockSpec(memory_space=pl.ANY))
        aliases = {len(operands) - 1: 0}
    return pl.pallas_call(
        functools.partial(finish_kernel, len(blocks)),
        grid=(1,),
        in_specs=in_specs,
        out_specs=[
            pl.BlockSpec((days, 2, TILE, degrees), lambda i: (0, 0, chunk, 0)),
            leading((TILE, 8, degrees), 0),
            leading((TILE, 8, degrees), 0),
            leading((time_count, TILE, 8, degrees // time_count), 0),
        ],
        out_shape=[
            jax.ShapeDtypeStruct((days, 2, slot_total, degrees), jnp.bfloat16),
            jax.ShapeDtypeStruct((TILE, 8, degrees), jnp.float32),
            jax.ShapeDtypeStruct((TILE, 8, degrees), jnp.bfloat16),
            jax.ShapeDtypeStruct((time_count, TILE, 8, degrees // time_count), jnp.bfloat16),
        ],
        input_output_aliases=aliases,
        scratch_shapes=[
            pltpu.VMEM((lat_half * PITCH, days), jnp.float32),
            pltpu.VMEM((TILE, lat_half, 2 * days), jnp.bfloat16),
            pltpu.VMEM((2, degrees // LANES, days * PITCH, LANES), jnp.float32),
            pltpu.VMEM((2, 3, steps, LANES), jnp.bfloat16),
            pltpu.VMEM((2, 2 * days + TILE, degrees + LANES), jnp.float32),
        ],
        compiler_params=pltpu.CompilerParams(vmem_limit_bytes=VMEM_LIMIT),
    )(*operands)


def after(values, waited):
    return lax.optimization_barrier((values, waited))[0]


def per_device(fields, wave_table, day_of_year, ar_coef, log_var):
    band_count = lax.axis_size("band")
    time_count = lax.axis_size("tm")
    band = lax.axis_index("band")
    slot_count, degree_count = ar_coef.shape
    day_count, lat_local, lon_count = fields.shape
    lat_count = lat_local * band_count
    group = band_count // 2
    steps = round_up(degree_count + 1, TILE)
    total_days = day_count * time_count
    slot_pad = round_up(slot_count, TILE)
    chunks = slot_pad // TILE
    pairs = slot_pad // 2
    half_index = band // group
    rank = band % group
    mirror = [(i, (i + group) % band_count) for i in range(band_count)]
    peers = [rank ^ k for k in range(group)]

    fields = fields.transpose(1, 2, 0)

    waves = wave_table.reshape(2, group, slot_count // 2, 2)
    high_low = jnp.stack([waves.max(-1), waves.min(-1)], axis=-1)
    high_low = jnp.pad(high_low, ((0, 0), (0, 0), (0, pairs - slot_count // 2), (0, 0)))
    ordered = high_low.reshape(2, group, slot_pad)
    present = jnp.arange(slot_pad) < slot_count

    def by_peer(side):
        table = lax.dynamic_index_in_dim(ordered, side, 0, keepdims=False)
        return jnp.stack([lax.dynamic_index_in_dim(table, peer, 0, keepdims=False) for peer in peers])

    own_waves, far_waves = by_peer(half_index), by_peer(1 - half_index)
    own_low, far_low = own_waves[0, 1::2], far_waves[0, 1::2]
    lats = jnp.concatenate(
        [(half_index * group + peer) * lat_local + jnp.arange(lat_local, dtype=jnp.int32) for peer in peers]
    )

    def table_of(waves_of, first, count):
        picked = waves_of[:, first * TILE : (first + count) * TILE].reshape(group * count, TILE)
        table = fourier_rows(picked, lon_count)
        if slot_pad != slot_count:
            mask = present[first * TILE : (first + count) * TILE].reshape(count, 1, TILE)
            mask = jnp.broadcast_to(mask, (group, count, 2, TILE)).reshape(-1, 1)
            table = table * mask.astype(jnp.bfloat16)
        return table

    across = list(range(group // 2, group))
    order = across[:0:-1] + list(range(1, group // 2)) + across[:1]

    def exchange(blocks, order):
        moved = [blocks[0]] + [None] * (group - 1)
        for k in order:
            moved[k] = lax.ppermute(blocks[k], "band", [(i, i ^ k) for i in range(band_count)])
        return moved

    blocks = longitude_sums(fields, table_of(far_waves, 0, 1), 2 * TILE)
    far = [exchange(blocks, order)]
    if chunks > 1:
        later = after(fields, blocks[0])
        blocks = longitude_sums(later, table_of(far_waves, 1, chunks - 1), (chunks - 1) * 2 * TILE)
        far.append(exchange(blocks, order))
    far_table = packed_table(after(far_low, blocks[0]), lats, lat_count, degree_count, steps)

    others = []

    def send_sums(chunk, waited):
        low = far_low[chunk * TILE // 2 : (chunk + 1) * TILE // 2]
        sums = partial_sums(chunk, max(chunk - 1, 0), after(low, waited), far[min(chunk, 1)], far_table, degree_count)
        sums = after(sums, others[-1]) if others else sums
        others.append([lax.ppermute(part, "band", mirror) for part in sums])
        return sums

    sums = send_sums(0, blocks[0])

    fields, own_waves, own_low, ar_coef, log_var = after((fields, own_waves, own_low, ar_coef, log_var), sums)
    blocks = longitude_sums(fields, table_of(own_waves, 0, chunks), 2 * TILE)
    own_table = packed_table(after(own_low, blocks[0]), lats, lat_count, degree_count, steps)
    slot_waves = lax.dynamic_slice_in_dim(wave_table, band * slot_count, slot_count)
    pad_slots = (0, slot_pad - slot_count)
    swap = (jnp.pad(slot_waves, pad_slots)[::2] == own_low).astype(jnp.int32)

    def by_pair(values):
        values = jnp.pad(values, (pad_slots, (0, LANES))).reshape(pairs, 2, degree_count + LANES)
        return jnp.where(swap[:, None, None] == 1, values[:, ::-1], values)

    values = jnp.concatenate([by_pair(ar_coef), by_pair(jnp.exp(-0.5 * log_var))], axis=1)
    columns = packed_columns(own_low, jnp.pad(values, ((0, 0), (0, 4), (0, 0))), steps)
    for chunk in range(1, chunks):
        send_sums(chunk, own_table if chunk == 1 else columns[0])

    season = 1.0 + 0.5 * jnp.cos(day_of_year.astype(jnp.float32) * (2.0 * math.pi / 365.0))
    later = (jnp.arange(day_count) > 0).astype(jnp.float32)
    season_rows = jnp.pad(jnp.stack([lax.rsqrt(season), later / season]), ((0, 6), (0, 0)))

    own = [exchange(after(blocks[::chunks], ([far[-1][k] for k in across], own_table)), order)]
    innovation = None
    misc, carried, moved = [], [], []
    route = [(i, i + 1) for i in range(time_count - 1)]
    for chunk in range(chunks):
        if chunk + 1 < chunks:
            crossed = own[-1]
            own.append(exchange(after(blocks[chunk + 1 :: chunks], (crossed, misc[:chunk])), order))
        span = slice(chunk * TILE // 2, (chunk + 1) * TILE // 2)
        innovation, rows, edges, sent = finish(
            chunk, after(own_low[span], others[1:2]), swap[span], own[chunk], own_table, others[chunk], columns, season_rows,
            innovation, slot_pad, degree_count, time_count,
        )
        misc.append(rows)
        carried.append(edges)
        moved.append(sent)
    innovation = innovation[:, :, :slot_count]
    carried = lax.ppermute(jnp.concatenate(carried, axis=0), "tm", route)
    moved = lax.all_to_all(jnp.concatenate(moved, axis=1), "tm", 0, 0, tiled=True)

    degree_list = jnp.arange(degree_count, dtype=jnp.int32)
    valid_mask = (degree_list[None, :] >= slot_waves[:, None]).astype(jnp.float32)
    first_day = jnp.stack([jnp.concatenate([rows[:, i] for rows in misc])[:slot_count] for i in (1, 3)])
    last_day = jnp.stack([carried[:slot_count, i] for i in (0, 2)]).astype(jnp.float32)
    scale = jnp.exp(-0.5 * log_var) * lax.rsqrt(season[0]) * valid_mask
    opening = ((first_day - ar_coef[None] * last_day) * scale[None]).astype(jnp.bfloat16)
    innovation = lax.dynamic_update_slice_in_dim(innovation, opening[None], 0, 0)

    column_width = degree_count // time_count
    place = lax.axis_index("tm")
    def own_columns(values):
        return lax.dynamic_slice_in_dim(values, place * column_width, column_width, 1)

    local_ar, local_var = own_columns(ar_coef), jnp.exp(-own_columns(log_var))
    first_days = day_of_year[0] + (jnp.arange(time_count, dtype=jnp.int32) - place) * day_count
    first_days = (first_days % 365).astype(jnp.float32)
    openness = 1.0 / (1.0 + 0.5 * jnp.cos(first_days * (2.0 * math.pi / 365.0)))
    moved = moved[:, :slot_count].astype(jnp.float32)
    first = moved[:, :, 1:4:2]
    before = jnp.concatenate([jnp.zeros_like(moved[:1, :, 0:4:2]), moved[:-1, :, 0:4:2]], axis=0)
    residual = first - local_ar[None, :, None] * before
    weighted = residual * openness[:, None, None, None]
    sum_coef = jnp.sum(moved[:, :, 4], axis=0) + jnp.sum(weighted * before, axis=(0, 2))
    sum_var = jnp.sum(moved[:, :, 5], axis=0) + jnp.sum(weighted * residual, axis=(0, 2))
    local_mask = own_columns(valid_mask)
    grad_coef = -local_mask * local_var * sum_coef / (2.0 * total_days)
    grad_var = local_mask * (total_days - 0.5 * local_var * sum_var) / (2.0 * total_days)
    return innovation, grad_coef, grad_var


def solution(mesh):
    in_specs = (P("tm", "band", None), P(), P("tm"), P("band", None), P("band", None))
    out_specs = (P("tm", None, "band", None), P("band", "tm"), P("band", "tm"))
    return jax.shard_map(
        per_device, mesh=mesh, in_specs=in_specs, out_specs=out_specs, check_vma=False
    )
```

```python
import functools
import math

import jax
import jax.numpy as jnp
from jax import lax
from jax.experimental import pallas as pl
from jax.experimental.pallas import tpu as pltpu
from jax.sharding import PartitionSpec as P

LANES = 128
TILE = 16
PITCH = TILE + 1
HALF = TILE // 4
ROWS = 80
DAY_ROWS = 32
VMEM_LIMIT = 56 * 1024 * 1024


def round_up(value, unit):
    return -(-value // unit) * unit


def fourier_kernel(coarse_cos_ref, coarse_sin_ref, fine_cos_ref, fine_sin_ref, out_ref):
    lon_count = out_ref.shape[1]
    fine_cos, fine_sin = fine_cos_ref[...], fine_sin_ref[...]
    for index in range(-(-lon_count // LANES)):
        width = min(LANES, lon_count - index * LANES)
        coarse_cos = coarse_cos_ref[:, index : index + 1]
        coarse_sin = coarse_sin_ref[:, index : index + 1]
        values = (coarse_cos * fine_cos - coarse_sin * fine_sin).astype(jnp.bfloat16)
        out_ref[:, index * LANES : index * LANES + width] = values[:, :width]


def fourier_rows(waves, lon_count):
    blocks, slots = waves.shape
    rows = blocks * 2 * slots

    def parts(step):
        lons = jnp.arange(LANES, dtype=jnp.int32) * step
        phase = waves[:, :, None] * lons % lon_count
        angle = phase.astype(jnp.float32) * (2.0 * math.pi / lon_count)
        return jnp.cos(angle), jnp.sin(angle)

    def both(first, second):
        return jnp.stack([first, second], axis=1).reshape(rows, LANES)

    coarse_cos, coarse_sin = parts(LANES)
    fine_cos, fine_sin = parts(1)
    return pl.pallas_call(
        fourier_kernel,
        out_shape=jax.ShapeDtypeStruct((rows, lon_count), jnp.bfloat16),
        compiler_params=pltpu.CompilerParams(vmem_limit_bytes=VMEM_LIMIT),
    )(
        both(coarse_cos, -coarse_sin),
        both(coarse_sin, coarse_cos),
        both(fine_cos, fine_cos),
        both(fine_sin, fine_sin),
    )


def transform_kernel(in_ref, table_ref, *out_refs):
    lats, _, days = in_ref.shape
    for lat in range(0, lats, 2):
        both = jnp.concatenate([in_ref[lat], in_ref[lat + 1]], axis=1)
        sums = jnp.dot(table_ref[...], both, preferred_element_type=jnp.float32).astype(jnp.bfloat16)
        begin = 0
        for out_ref in out_refs:
            piece = sums[begin : begin + out_ref.shape[1]]
            begin += out_ref.shape[1]
            out_ref[lat] = piece[:, :days]
            out_ref[lat + 1] = piece[:, days:]


def longitude_sums(fields, table, block_rows):
    lats, lon_count, days = fields.shape
    group = 22 if lats % 22 == 0 else 2
    rows = table.shape[0]
    blocks = rows // block_rows
    return pl.pallas_call(
        transform_kernel,
        grid=(lats // group,),
        in_specs=[
            pl.BlockSpec((group, lon_count, days), lambda i: (i, 0, 0)),
            pl.BlockSpec((rows, lon_count), lambda i: (0, 0)),
        ],
        out_specs=[pl.BlockSpec((group, block_rows, days), lambda i: (i, 0, 0))] * blocks,
        out_shape=[jax.ShapeDtypeStruct((lats, block_rows, days), jnp.bfloat16)] * blocks,
        compiler_params=pltpu.CompilerParams(vmem_limit_bytes=VMEM_LIMIT),
    )(fields, table)


def table_kernel(steps, lane_tiles, top, low_ref, first_ref, second_ref, cos_ref, weight_ref, out_ref, rows_ref, scale_ref):
    tiles = range(lane_tiles)
    low = low_ref[...]
    high = top - low
    low_next = low + 1.0
    lat_count = out_ref.shape[2]
    pairs = out_ref.shape[0]

    def lanes(ref, tile):
        return ref[:, tile * LANES : (tile + 1) * LANES]

    cosines = [lanes(cos_ref, t) for t in tiles]
    weights = [lanes(weight_ref, t) for t in tiles]
    second = [lanes(second_ref, t) for t in tiles]
    for t in tiles:
        half = jnp.exp(0.5 * second[t])
        scale_ref[2, :, t * LANES : (t + 1) * LANES] = half * weights[t]
        scale_ref[3, :, t * LANES : (t + 1) * LANES] = half

    def block(index, carry):
        current, lagged, scale, last_inverse = carry
        for t in tiles:
            largest = jnp.maximum(jnp.maximum(jnp.abs(current[t]), jnp.abs(lagged[t])), 1.0)
            current[t] = current[t] / largest
            lagged[t] = lagged[t] / largest
            scale[t] = scale[t] + jnp.log(largest)
            half = jnp.exp(0.5 * scale[t])
            scale_ref[0, :, t * LANES : (t + 1) * LANES] = half * weights[t]
            scale_ref[1, :, t * LANES : (t + 1) * LANES] = half
        begin = (index * TILE).astype(jnp.float32)
        for step in range(TILE):
            row = begin + float(step)
            after = low < row
            above = row - jnp.where(after, low_next, 0.0)
            order = jnp.where(after, low, high)
            degree = above + order
            spread = above * (degree + order)
            square = 4.0 * degree * degree - 1.0
            root = lax.rsqrt(jnp.maximum(square * spread, 1.0))
            factor = square * root
            inverse = spread * root
            fresh = above == 0.0
            for t in tiles:
                advanced = factor * (cosines[t] * current[t] - last_inverse * lagged[t])
                lagged[t] = current[t]
                current[t] = jnp.where(fresh, 1.0, advanced)
                rows_ref[t, pl.ds(step, pairs, stride=PITCH), :] = current[t]
            last_inverse = inverse
        renewed = (low_next >= begin) & (low_next < begin + float(TILE))
        for t in tiles:
            scale[t] = jnp.where(renewed, second[t], scale[t])
        row_index = lax.broadcasted_iota(jnp.int32, (TILE, LANES), 0).astype(jnp.float32) + begin
        for pair in range(pairs):
            mark = low[pair : pair + 1, :]
            before = (row_index <= mark) | (mark + 1.0 < begin)
            for t in tiles:
                span = slice(t * LANES, min((t + 1) * LANES, lat_count))
                width = span.stop - span.start
                here = slice(t * LANES, (t + 1) * LANES)
                values = rows_ref[t, pair * PITCH : pair * PITCH + TILE, :]
                one = jnp.where(before, scale_ref[0, pair : pair + 1, here], scale_ref[2, pair : pair + 1, here])
                two = jnp.where(before, scale_ref[1, pair : pair + 1, here], scale_ref[3, pair : pair + 1, here])
                values = (values * one * two).astype(jnp.bfloat16)
                out_ref[pair, pl.ds(pl.multiple_of(index * TILE, TILE), TILE), span] = values[:, :width]
        return current, lagged, scale, last_inverse

    zeros = jnp.zeros((pairs, LANES), jnp.float32)
    start = (
        [zeros for _ in tiles],
        [zeros for _ in tiles],
        [lanes(first_ref, t) for t in tiles],
        zeros,
    )
    lax.fori_loop(0, steps // TILE, block, start)


def packed_table(low_waves, lats, lat_count, degree_count, steps):
    pair_count = low_waves.shape[0]
    lat_half = lats.shape[0]
    lane_tiles = -(-lat_half // LANES)
    width = lane_tiles * LANES
    top = float(degree_count - 1)
    index = jnp.pad(lats, (0, width - lat_half), mode="edge")
    colatitude = (index.astype(jnp.float32) + 0.5) * (math.pi / lat_count)
    sines = jnp.sin(colatitude)
    log_sines = jnp.log(sines)
    low = low_waves.astype(jnp.float32)

    def log_start(order):
        base = 0.5 * (
            jnp.log(order + 0.5)
            + jax.scipy.special.gammaln(order + 0.5)
            - jax.scipy.special.gammaln(order + 1.0)
            - 0.5 * math.log(math.pi)
        )
        return base[:, None] + order[:, None] * log_sines[None, :]

    def spread(row):
        return jnp.broadcast_to(row[None, :], (pair_count, width))

    return pl.pallas_call(
        functools.partial(table_kernel, steps, lane_tiles, top),
        out_shape=jax.ShapeDtypeStruct((pair_count, steps, lat_half), jnp.bfloat16),
        scratch_shapes=[
            pltpu.VMEM((lane_tiles, pair_count * PITCH, LANES), jnp.float32),
            pltpu.VMEM((4, pair_count, width), jnp.float32),
        ],
        compiler_params=pltpu.CompilerParams(vmem_limit_bytes=VMEM_LIMIT),
    )(
        jnp.broadcast_to(low[:, None], (pair_count, LANES)),
        log_start(top - low),
        log_start(low),
        spread(jnp.cos(colatitude)),
        spread(sines * (math.pi / lat_count)),
    )


def gather_slots(in_refs, flat_ref, slot_ref):
    lats, rows, days = in_refs[0].shape
    lat_half = len(in_refs) * lats
    step = 8 if lats % 8 == 0 else lats

    for part in range(2):
        for source, in_ref in enumerate(in_refs):

            def spread(index, carry, source=source, in_ref=in_ref, part=part):
                first = index * step
                values = in_ref[pl.ds(first, step), part * TILE : (part + 1) * TILE, :].astype(jnp.float32)
                begin = source * lats + first
                if step == 8:
                    window = flat_ref.at[pl.ds(pl.multiple_of(begin * PITCH, 8), 8 * PITCH)]
                else:
                    window = flat_ref.at[begin * PITCH : (begin + step) * PITCH]
                for lat in range(step):
                    window[lat * PITCH : lat * PITCH + TILE, :] = values[lat]
                return carry

            if step == 8:
                lax.fori_loop(0, lats // step, spread, 0)
            else:
                spread(0, 0)
        for slot in range(TILE):
            column = flat_ref[pl.ds(slot, lat_half, stride=PITCH), :]
            slot_ref[slot, :, part * days : (part + 1) * days] = column.astype(jnp.bfloat16)


def pair_sum(pair, low, table_ref, slot_ref):
    table = table_ref[pair]
    high_sum = jnp.dot(table, slot_ref[2 * pair], preferred_element_type=jnp.float32)
    low_sum = jnp.dot(table, slot_ref[2 * pair + 1], preferred_element_type=jnp.float32)
    row = lax.broadcasted_iota(jnp.int32, high_sum.shape, 0)
    return jnp.where(row <= low, high_sum, low_sum)


def by_halves(one):
    def two(step, carry):
        one(0, step)
        one(1, step)
        return carry

    lax.fori_loop(0, HALF, two, 0)


def partial_kernel(degrees, low_ref, table_ref, *rest):
    *in_refs, first_ref, second_ref, flat_ref, slot_ref, last_ref = rest
    out_refs = (first_ref, second_ref)
    gather_slots(in_refs, flat_ref, slot_ref)
    last_ref[...] = jnp.zeros_like(last_ref)
    last_row = lax.broadcasted_iota(jnp.int32, last_ref.shape[1:], 0)

    def one(half, step):
        pair = half * HALF + step
        sums = pair_sum(pair, low_ref[pair], table_ref, slot_ref)
        begin = pl.multiple_of(step * degrees, TILE)
        out_refs[half][pl.ds(begin, degrees), :] = sums[:degrees].astype(jnp.bfloat16)
        last_ref[half] = jnp.where(last_row == step, sums[degrees : degrees + 1], last_ref[half])

    by_halves(one)
    for half in range(2):
        out_refs[half][HALF * degrees :, :] = last_ref[half].astype(jnp.bfloat16)


def pack_kernel(low_ref, in_ref, ar_ref, half_ref):
    pairs, _, width = in_ref.shape
    steps = ar_ref.shape[1]
    lane = lax.broadcasted_iota(jnp.int32, (1, width), 1)
    degrees = round_up(steps, LANES) - LANES

    def one(pair, carry):
        low = low_ref[pair]
        rows = in_ref[pair]
        high_rows = pltpu.roll(rows, width - (degrees - 1 - low), 1)
        low_rows = pltpu.roll(rows, 1, 1)
        for index, out_ref in enumerate((ar_ref, half_ref)):
            packed = jnp.where(
                lane <= low, high_rows[2 * index : 2 * index + 1], low_rows[2 * index + 1 : 2 * index + 2]
            )
            out_ref[pair] = jnp.broadcast_to(packed, (LANES, width)).T[:steps]
        return carry

    lax.fori_loop(0, pairs, one, 0)


def packed_columns(low, values, steps):
    pairs = values.shape[0]
    return pl.pallas_call(
        pack_kernel,
        in_specs=[pl.BlockSpec(memory_space=pltpu.SMEM), pl.BlockSpec(memory_space=pltpu.VMEM)],
        out_shape=[jax.ShapeDtypeStruct((pairs, steps, LANES), jnp.float32)] * 2,
        compiler_params=pltpu.CompilerParams(vmem_limit_bytes=VMEM_LIMIT),
    )(low, values)


def finish_kernel(sources, low_ref, swap_ref, table_ref, first_ref, second_ref, ar_ref, half_ref, season_ref, *rest):
    out_ref, misc_ref, flat_ref, slot_ref, turned_ref, innovation_ref, stacked_ref = rest[-7:]
    steps = table_ref.shape[1]
    days = out_ref.shape[0]
    degrees = out_ref.shape[3]
    lane_tiles = degrees // LANES
    width = degrees + LANES
    gather_slots(rest[:sources], flat_ref, slot_ref)
    lane = lax.broadcasted_iota(jnp.int32, (ROWS, LANES), 1)
    degree = lax.broadcasted_iota(jnp.int32, (DAY_ROWS, degrees), 1)
    last_row = lax.broadcasted_iota(jnp.int32, (TILE, 2 * days), 0)
    turn = (
        lax.broadcasted_iota(jnp.int32, (days, days), 0) == lax.broadcasted_iota(jnp.int32, (days, days), 1)
    ).astype(jnp.bfloat16)
    pick_row = lax.broadcasted_iota(jnp.int32, (TILE, LANES), 0)
    pick_lane = lax.broadcasted_iota(jnp.int32, (TILE, LANES), 1)
    pick = (pick_lane == jnp.where(pick_row < 8, pick_row, pick_row + (LANES // 2 - 8))).astype(jnp.bfloat16)
    transposed = (((1,), (1,)), ((), ()))
    other_refs = (first_ref, second_ref)

    for half in range(2):
        stacked_ref[half, :, steps:] = jnp.zeros((2 * days + TILE, width - steps), jnp.float32)

    def one(part_of, step):
        pair = part_of * HALF + step
        low = low_ref[pair]
        other_ref = other_refs[part_of]
        begin = pl.multiple_of(step * degrees, TILE)
        last = jnp.where(last_row == step, other_ref[HALF * degrees :, :].astype(jnp.float32), 0.0)
        last = jnp.where(last_row == 0, jnp.sum(last, axis=0, keepdims=True), 0.0)
        table = table_ref[pair]
        high_sum = jnp.dot(table, slot_ref[2 * pair], preferred_element_type=jnp.float32)
        low_sum = jnp.dot(table, slot_ref[2 * pair + 1], preferred_element_type=jnp.float32)
        for first in range(0, steps, ROWS):
            here = slice(first, first + ROWS)
            row = lax.broadcasted_iota(jnp.int32, (ROWS, 2 * days), 0) + first
            own = jnp.where(row <= low, high_sum[here], low_sum[here])
            count = min(ROWS, degrees - first)
            other = other_ref[pl.ds(begin + first, count), :].astype(jnp.float32)
            if count < ROWS:
                other = jnp.concatenate([other, last], axis=0)
            total = own + other
            ar = ar_ref[pair, here]
            half = half_ref[pair, here]
            shifted_parts = []
            sum_coef = sum_var = 0.0
            for part in range(2):
                spectral = total[:, part * days : (part + 1) * days]
                shifted = pltpu.roll(spectral, 1, 1)
                shifted_parts.append(shifted)
                previous = jnp.where(lane == 0, 0.0, shifted)
                residual = spectral - ar * previous
                innovation_ref[part_of, part, here] = (residual * season_ref[0:1, :] * half).astype(jnp.bfloat16)
                weighted = residual * season_ref[1:2, :]
                sum_coef = sum_coef + weighted * previous
                sum_var = sum_var + weighted * residual
            sum_coef = jnp.sum(sum_coef, axis=1, keepdims=True)
            sum_var = jnp.sum(sum_var, axis=1, keepdims=True)
            misc = jnp.where(
                lane < 2,
                shifted_parts[0],
                jnp.where(lane < 4, pltpu.roll(shifted_parts[1], 2, 1), jnp.where(lane == 4, sum_coef, sum_var)),
            )
            misc_high = misc.astype(jnp.bfloat16).astype(jnp.float32)
            misc_low = pltpu.roll(misc - misc_high, LANES // 2, 1)
            misc = jnp.where(lane < LANES // 2, misc_high, misc_low)
            innovation_ref[part_of, 2, here] = misc.astype(jnp.bfloat16)
        for part in range(3):
            placer = turn if part < 2 else pick
            stacked_ref[part_of, part * days : part * days + placer.shape[0], :steps] = lax.dot_general(
                placer, innovation_ref[part_of, part], transposed, preferred_element_type=jnp.float32
            )
        high = degrees - 1 - low
        swap = swap_ref[pair]
        for shift, start, slot in ((high, high, 2 * pair + swap), (width - 1, low, 2 * pair + 1 - swap)):
            for first in range(0, 2 * days, DAY_ROWS):
                stacked = stacked_ref[part_of, first : first + DAY_ROWS, :]
                placed = jnp.where(degree >= start, pltpu.roll(stacked, shift, 1)[:, :degrees], 0.0)
                part, day = divmod(first, days)
                for t in range(lane_tiles):
                    turned_ref[part, t, pl.ds(day * PITCH + slot, DAY_ROWS, stride=PITCH), :] = placed[
                        :, t * LANES : (t + 1) * LANES
                    ]
            stacked = stacked_ref[part_of, 2 * days :, :]
            placed = jnp.where(degree[:TILE] >= start, pltpu.roll(stacked, shift, 1)[:, :degrees], 0.0)
            misc_ref[slot] = placed[:8] + placed[8:]

    by_halves(one)

    def write(step, carry):
        begin = pl.multiple_of(step * 8 * PITCH, 8)
        for part in range(2):
            for t in range(lane_tiles):
                window = turned_ref.at[part, t, pl.ds(begin, 8 * PITCH)]
                for day in range(8):
                    values = window[day * PITCH : day * PITCH + TILE, :]
                    out_ref[step * 8 + day, part, :, t * LANES : (t + 1) * LANES] = values.astype(jnp.bfloat16)
        return carry

    lax.fori_loop(0, days // 8, write, 0)


def leading(shape, chunk):
    return pl.BlockSpec(shape, lambda i: (chunk,) + (0,) * (len(shape) - 1))


def partial_sums(chunk, place, low, blocks, table, degrees):
    lats, rows, days = blocks[0].shape
    steps, lat_half = table.shape[1:]
    out_rows = HALF * degrees + TILE
    pairs = TILE // 2
    return pl.pallas_call(
        functools.partial(partial_kernel, degrees),
        grid=(1,),
        in_specs=[
            pl.BlockSpec(memory_space=pltpu.SMEM),
            leading((pairs, steps, lat_half), chunk),
        ]
        + [pl.BlockSpec((lats, 2 * TILE, days), lambda i: (0, place, 0)) for _ in blocks],
        out_specs=[leading((out_rows, 2 * days), 0)] * 2,
        out_shape=[jax.ShapeDtypeStruct((out_rows, 2 * days), jnp.bfloat16)] * 2,
        scratch_shapes=[
            pltpu.VMEM((lat_half * PITCH, days), jnp.float32),
            pltpu.VMEM((TILE, lat_half, 2 * days), jnp.bfloat16),
            pltpu.VMEM((2, TILE, 2 * days), jnp.float32),
        ],
        compiler_params=pltpu.CompilerParams(vmem_limit_bytes=VMEM_LIMIT),
    )(low, table, *blocks)


def finish(chunk, low, swap, blocks, table, other, columns, season, held, slot_total, degrees):
    lats, rows, days = blocks[0].shape
    steps, lat_half = table.shape[1:]
    pairs = TILE // 2
    smem = pl.BlockSpec(memory_space=pltpu.SMEM)
    operands = [low, swap, table, *other, *columns, season, *blocks]
    in_specs = [
        smem,
        smem,
        leading((pairs, steps, lat_half), chunk),
        leading(other[0].shape, 0),
        leading(other[1].shape, 0),
        leading((pairs, steps, LANES), chunk),
        leading((pairs, steps, LANES), chunk),
        leading((8, LANES), 0),
    ] + [leading(block.shape, 0) for block in blocks]
    aliases = {}
    if held is not None:
        operands.append(held)
        in_specs.append(pl.BlockSpec(memory_space=pl.ANY))
        aliases = {len(operands) - 1: 0}
    return pl.pallas_call(
        functools.partial(finish_kernel, len(blocks)),
        grid=(1,),
        in_specs=in_specs,
        out_specs=[
            pl.BlockSpec((days, 2, TILE, degrees), lambda i: (0, 0, chunk, 0)),
            leading((TILE, 8, degrees), 0),
        ],
        out_shape=[
            jax.ShapeDtypeStruct((days, 2, slot_total, degrees), jnp.bfloat16),
            jax.ShapeDtypeStruct((TILE, 8, degrees), jnp.float32),
        ],
        input_output_aliases=aliases,
        scratch_shapes=[
            pltpu.VMEM((lat_half * PITCH, days), jnp.float32),
            pltpu.VMEM((TILE, lat_half, 2 * days), jnp.bfloat16),
            pltpu.VMEM((2, degrees // LANES, days * PITCH, LANES), jnp.float32),
            pltpu.VMEM((2, 3, steps, LANES), jnp.bfloat16),
            pltpu.VMEM((2, 2 * days + TILE, degrees + LANES), jnp.float32),
        ],
        compiler_params=pltpu.CompilerParams(vmem_limit_bytes=VMEM_LIMIT),
    )(*operands)


def after(values, waited):
    return lax.optimization_barrier((values, waited))[0]


def per_device(fields, wave_table, day_of_year, ar_coef, log_var):
    band_count = lax.axis_size("band")
    time_count = lax.axis_size("tm")
    band = lax.axis_index("band")
    slot_count, degree_count = ar_coef.shape
    day_count, lat_local, lon_count = fields.shape
    lat_count = lat_local * band_count
    group = band_count // 2
    steps = round_up(degree_count + 1, TILE)
    total_days = day_count * time_count
    slot_pad = round_up(slot_count, TILE)
    chunks = slot_pad // TILE
    pairs = slot_pad // 2
    half_index = band // group
    rank = band % group
    mirror = [(i, (i + group) % band_count) for i in range(band_count)]
    peers = [rank ^ k for k in range(group)]

    fields = fields.transpose(1, 2, 0)

    waves = wave_table.reshape(2, group, slot_count // 2, 2)
    high_low = jnp.stack([waves.max(-1), waves.min(-1)], axis=-1)
    high_low = jnp.pad(high_low, ((0, 0), (0, 0), (0, pairs - slot_count // 2), (0, 0)))
    ordered = high_low.reshape(2, group, slot_pad)
    present = jnp.arange(slot_pad) < slot_count

    def by_peer(side):
        table = lax.dynamic_index_in_dim(ordered, side, 0, keepdims=False)
        return jnp.stack([lax.dynamic_index_in_dim(table, peer, 0, keepdims=False) for peer in peers])

    own_waves, far_waves = by_peer(half_index), by_peer(1 - half_index)
    own_low, far_low = own_waves[0, 1::2], far_waves[0, 1::2]
    lats = jnp.concatenate(
        [(half_index * group + peer) * lat_local + jnp.arange(lat_local, dtype=jnp.int32) for peer in peers]
    )

    def table_of(waves_of, first, count):
        picked = waves_of[:, first * TILE : (first + count) * TILE].reshape(group * count, TILE)
        table = fourier_rows(picked, lon_count)
        if slot_pad != slot_count:
            mask = present[first * TILE : (first + count) * TILE].reshape(count, 1, TILE)
            mask = jnp.broadcast_to(mask, (group, count, 2, TILE)).reshape(-1, 1)
            table = table * mask.astype(jnp.bfloat16)
        return table

    across = list(range(group // 2, group))
    order = across[:0:-1] + list(range(1, group // 2)) + across[:1]

    def exchange(blocks, order):
        moved = [blocks[0]] + [None] * (group - 1)
        for k in order:
            moved[k] = lax.ppermute(blocks[k], "band", [(i, i ^ k) for i in range(band_count)])
        return moved

    blocks = longitude_sums(fields, table_of(far_waves, 0, 1), 2 * TILE)
    far = [exchange(blocks, order)]
    if chunks > 1:
        later = after(fields, blocks[0])
        blocks = longitude_sums(later, table_of(far_waves, 1, chunks - 1), (chunks - 1) * 2 * TILE)
        far.append(exchange(blocks, order))
    far_table = packed_table(after(far_low, blocks[0]), lats, lat_count, degree_count, steps)

    others = []

    def send_sums(chunk, waited):
        low = far_low[chunk * TILE // 2 : (chunk + 1) * TILE // 2]
        sums = partial_sums(chunk, max(chunk - 1, 0), after(low, waited), far[min(chunk, 1)], far_table, degree_count)
        sums = after(sums, others[-1]) if others else sums
        others.append([lax.ppermute(part, "band", mirror) for part in sums])
        return sums

    sums = send_sums(0, blocks[0])

    fields, own_waves, own_low, ar_coef, log_var = after((fields, own_waves, own_low, ar_coef, log_var), sums)
    blocks = longitude_sums(fields, table_of(own_waves, 0, chunks), 2 * TILE)
    own_table = packed_table(after(own_low, blocks[0]), lats, lat_count, degree_count, steps)
    slot_waves = lax.dynamic_slice_in_dim(wave_table, band * slot_count, slot_count)
    pad_slots = (0, slot_pad - slot_count)
    swap = (jnp.pad(slot_waves, pad_slots)[::2] == own_low).astype(jnp.int32)

    def by_pair(values):
        values = jnp.pad(values, (pad_slots, (0, LANES))).reshape(pairs, 2, degree_count + LANES)
        return jnp.where(swap[:, None, None] == 1, values[:, ::-1], values)

    values = jnp.concatenate([by_pair(ar_coef), by_pair(jnp.exp(-0.5 * log_var))], axis=1)
    columns = packed_columns(own_low, jnp.pad(values, ((0, 0), (0, 4), (0, 0))), steps)
    for chunk in range(1, chunks):
        send_sums(chunk, own_table if chunk == 1 else columns[0])

    season = 1.0 + 0.5 * jnp.cos(day_of_year.astype(jnp.float32) * (2.0 * math.pi / 365.0))
    later = (jnp.arange(day_count) > 0).astype(jnp.float32)
    season_rows = jnp.pad(jnp.stack([lax.rsqrt(season), later / season]), ((0, 6), (0, 0)))

    own = [exchange(after(blocks[::chunks], ([far[-1][k] for k in across], own_table)), order)]
    innovation = None
    misc = []
    for chunk in range(chunks):
        if chunk + 1 < chunks:
            crossed = own[-1]
            own.append(exchange(after(blocks[chunk + 1 :: chunks], (crossed, misc[:chunk])), order))
        span = slice(chunk * TILE // 2, (chunk + 1) * TILE // 2)
        innovation, rows = finish(
            chunk, own_low[span], swap[span], own[chunk], own_table, others[chunk], columns, season_rows,
            innovation, slot_pad, degree_count,
        )
        misc.append(rows)
    innovation = innovation[:, :, :slot_count]
    misc = jnp.concatenate(misc, axis=0)[:slot_count, :6]

    degree_list = jnp.arange(degree_count, dtype=jnp.int32)
    valid_mask = (degree_list[None, :] >= slot_waves[:, None]).astype(jnp.float32)
    edges = misc.transpose(1, 0, 2)
    route = [(i, i + 1) for i in range(time_count - 1)]
    carried = lax.ppermute(edges[0:4:2].astype(jnp.bfloat16), "tm", route).astype(jnp.float32)
    scale = jnp.exp(-0.5 * log_var) * lax.rsqrt(season[0]) * valid_mask
    opening = ((edges[1:4:2] - ar_coef[None] * carried) * scale[None]).astype(jnp.bfloat16)
    innovation = lax.dynamic_update_slice_in_dim(innovation, opening[None], 0, 0)

    column_width = degree_count // time_count
    place = lax.axis_index("tm")
    columns = [misc[:, :, i * column_width : (i + 1) * column_width] for i in range(time_count)]
    moved = lax.all_to_all(jnp.stack(columns).astype(jnp.bfloat16), "tm", 0, 0, tiled=True).astype(jnp.float32)

    def own_columns(values):
        return lax.dynamic_slice_in_dim(values, place * column_width, column_width, 1)

    local_ar, local_var = own_columns(ar_coef), jnp.exp(-own_columns(log_var))
    first_days = day_of_year[0] + (jnp.arange(time_count, dtype=jnp.int32) - place) * day_count
    first_days = (first_days % 365).astype(jnp.float32)
    openness = 1.0 / (1.0 + 0.5 * jnp.cos(first_days * (2.0 * math.pi / 365.0)))
    first = moved[:, :, 1:4:2]
    before = jnp.concatenate([jnp.zeros_like(moved[:1, :, 0:4:2]), moved[:-1, :, 0:4:2]], axis=0)
    residual = first - local_ar[None, :, None] * before
    weighted = residual * openness[:, None, None, None]
    sum_coef = jnp.sum(moved[:, :, 4], axis=0) + jnp.sum(weighted * before, axis=(0, 2))
    sum_var = jnp.sum(moved[:, :, 5], axis=0) + jnp.sum(weighted * residual, axis=(0, 2))
    local_mask = own_columns(valid_mask)
    grad_coef = -local_mask * local_var * sum_coef / (2.0 * total_days)
    grad_var = local_mask * (total_days - 0.5 * local_var * sum_var) / (2.0 * total_days)
    return innovation, grad_coef, grad_var


def solution(mesh):
    in_specs = (P("tm", "band", None), P(), P("tm"), P("band", None), P("band", None))
    out_specs = (P("tm", None, "band", None), P("band", "tm"), P("band", "tm"))
    return jax.shard_map(
        per_device, mesh=mesh, in_specs=in_specs, out_specs=out_specs, check_vma=False
    )
```
